128 devices in a mesh: row: 4 (over x), col: 16 (over z, y), layer: 2 (over core).
Axes of the slice: x: 4, y: 4, z: 4, core: 2. Of those that a mesh axis runs over, the one named last changes fastest.
Arguments:
- markov: bfloat16 [12288, 12288], P('row', 'col'), may hold values from 0.049804688 to 1
- pattern: int32 [96, 96], replicated, may hold values from 0 to 1, as said below
- keep: int32 [96, 96], replicated, may hold values from 0 to 1, as said below
Outputs:
- cluster: float32 [12288, 12288], P('row', ('col', 'layer'))
The draws below stay inside these ranges and needn't reach their ends.
Inputs may be any that keep to these rules, and one draw needn't show every extreme that they name: Every diagonal tile is present: pattern[i, i] = 1. No row of pattern has more than 72 present tiles, and in every draw some row has exactly that many. Every diagonal tile survives: keep[i, i] = 1.
All inputs are finite; a program needn't handle non-finite values.
Results may differ from the reference program's by a relative error of at most 0.0003.
Values may be sent and summed in bfloat16 or wider, within the bound.
No kernel may reach another device: no remote copies, remote signals or barrier semaphores. Data moves between devices by JAX's collectives and lax.ppermute only.
A program may use at most 192 MiB of HBM per device.

```python
import jax
import jax.numpy as jnp

TILE = 128
TILES = 96
ORDER = 12288


def draw_pattern(key, part):
    key = jax.random.fold_in(key, 11)
    key_level, key_heavy, key_forced, key_order = jax.random.split(key, 4)
    places = jnp.arange(TILES)
    level = jax.random.randint(key_level, (TILES,), 1, TILES // 4 + 1)
    heavy = jax.random.randint(key_heavy, (TILES,), 0, 8) == 0
    forced = jax.random.randint(key_forced, (), 0, TILES)
    heavy = heavy | (places == forced)
    level = jnp.where(heavy, 3 * TILES // 4, level)
    row_keys = jax.random.split(key_order, TILES)
    scores = jax.vmap(lambda one_key: jax.random.permutation(one_key, TILES))(row_keys)
    diagonal = places[:, None] == places[None, :]
    scores = jnp.where(diagonal, -1, scores)
    ranking = jnp.argsort(jnp.argsort(scores, axis=1, stable=True), axis=1, stable=True)
    return jnp.where(ranking < level[:, None], 1, 0).astype(jnp.int32)


def draw_keep(key, part):
    key = jax.random.fold_in(key, 23)
    roll = jax.random.randint(key, (TILES, TILES), 0, 2)
    places = jnp.arange(TILES)
    diagonal = places[:, None] == places[None, :]
    return jnp.where((roll == 1) | diagonal, 1, 0).astype(jnp.int32)


def block_levels(key, shape, pieces, smallest, largest):
    loudness, own = 1.0, jax.random.fold_in(key, 6)
    for position, parts in pieces:
        steps = jnp.exp(jax.random.uniform(jax.random.fold_in(own, position), (parts,), jnp.float32, smallest / len(pieces), largest / len(pieces)))
        loudness = loudness * jnp.repeat(steps, shape[position] // parts).reshape([-1 if axis == position else 1 for axis in range(len(shape))])
    return loudness


def setup_inputs(seed: int = 0) -> dict:
    splits = jax.random.split(jax.random.key(seed), 4)
    markov = jnp.clip(0.049804688 + 0.9501953 * jax.random.uniform(splits[0], (ORDER, ORDER), jnp.float32) ** block_levels(splits[0], (ORDER, ORDER), ((0, 4), (1, 16)), -0.2, 0.2), 0.049804688, 1.0).astype(jnp.bfloat16)
    pattern = draw_pattern(jax.random.fold_in(splits[3], 71), 0)
    keep = draw_keep(jax.random.fold_in(splits[3], 71), 0)
    return {"markov": markov, "pattern": pattern, "keep": keep}


def reference(markov, pattern, keep):
    order = TILES * TILE
    live = (markov.reshape(TILES, TILE, TILES, TILE) * pattern.astype(jnp.bfloat16)[:, None, :, None]).reshape(order, order)
    square = jnp.dot(live, live, preferred_element_type=jnp.float32)
    inflated = square * square
    kept = (inflated.reshape(TILES, TILE, TILES, TILE) * keep.astype(jnp.float32)[:, None, :, None]).reshape(order, order)
    totals = jnp.sum(kept, axis=0)
    return order * kept / totals[None, :]
```

```python
import functools

import jax
import jax.numpy as jnp
from jax import lax
from jax.experimental import pallas as pl
from jax.experimental.pallas import tpu as pltpu
from jax.sharding import PartitionSpec as P

TILE = 128
SIDE = 4
GROUP = 4
CAP1 = 20
CAP2 = 42
RIGHT_BITS = 4096
PLACE = 16
MIB = 1024 * 1024

SMEM = pl.BlockSpec(memory_space=pltpu.SMEM)
VMEM = pl.BlockSpec(memory_space=pltpu.VMEM)
HBM = pl.BlockSpec(memory_space=pltpu.HBM)


def position():
    return lax.axis_index("row"), lax.axis_index("col"), lax.axis_index("layer")


def dot(a, b):
    return jnp.dot(a.astype(jnp.bfloat16), b.astype(jnp.bfloat16), preferred_element_type=jnp.float32)


def where_in(shape):
    return lax.broadcasted_iota(jnp.int32, shape, 0), lax.broadcasted_iota(jnp.int32, shape, 1)


def ranks(block_rows, present):
    tiles = present.shape[0]
    ones = jnp.ones((8, tiles), jnp.bfloat16)
    level_row = lax.dot_general(ones, present.astype(jnp.bfloat16), (((1,), (1,)), ((), ())), preferred_element_type=jnp.float32)[:1]
    level_col = jnp.sum(present, axis=1, keepdims=True)
    a, b = where_in((tiles, tiles))
    same = jnp.where(a // block_rows == b // block_rows, 1.0, 0.0)
    above = jnp.where(level_col > level_row, 1.0, 0.0) + jnp.where(level_col == level_row, jnp.where(a < b, 1.0, 0.0), 0.0)
    below = jnp.where(level_col < level_row, 1.0, 0.0) + jnp.where(level_col == level_row, jnp.where(a > b, 1.0, 0.0), 0.0)
    return (
        jnp.sum(above * same, axis=0, keepdims=True).astype(jnp.int32),
        jnp.sum(below * same, axis=1, keepdims=True).astype(jnp.int32),
    )


def core_slot(rank):
    return ((rank + 1) // 2) % 2, rank // 2


def plan_kernel(z, pattern_ref, plan_ref):
    present = pattern_ref[...].astype(jnp.float32)
    i, k = where_in((z.tiles, TILE))
    weights = jnp.where(i // z.block_cols == k, jnp.left_shift(1, i % z.block_cols), 0)
    bits = dot(present, weights).astype(jnp.int32)
    rank_row, rank_col = ranks(z.block_rows, present)
    core, slot = core_slot(rank_row)
    plan_ref[...] = jnp.zeros_like(plan_ref)
    plan_ref[z.tiles:z.tiles + 1, 0:z.tiles] = core * z.half + slot
    core, slot = core_slot(rank_col)
    plan_ref[0:z.tiles, :] = jnp.where(k == PLACE, core * z.half + slot, bits)


class Sizes:
    def __init__(self, rows_dev, cols_dev, tiles):
        self.block_rows = rows_dev // TILE
        self.block_cols = cols_dev // TILE
        self.half = self.block_rows // 2
        self.tiles = tiles
        self.blocks = tiles // self.block_rows


def check_kernel(z, pattern_ref, keep_ref, _, flag_ref):
    groups = 2 * z.blocks
    present = pattern_ref[...].astype(jnp.float32)
    keep = keep_ref[...].astype(jnp.float32)
    rank, _ = ranks(z.block_rows, present)
    core, slot = core_slot(rank)
    owner, row = where_in((2 * groups, z.tiles))
    member = jnp.where(owner % groups == (row // z.block_rows) * 2 + core, 1.0, 0.0)
    member = member * jnp.where(owner // groups == slot % 2, 1.0, 0.0)
    i, k = where_in((2 * groups, z.tiles))
    odd = (i // groups + k) % 2
    i, k = where_in((z.tiles, TILE))
    per_block = jnp.where(i // z.block_cols == k, 1.0, 0.0)
    per_outer = [
        jnp.where(i // (z.block_cols * SIDE) == k, 1.0, 0.0),
        jnp.where((i // z.block_cols) % SIDE == k, 1.0, 0.0),
    ]
    by_k = dot(member, present)
    over = jnp.zeros((1, 1), jnp.int32)
    for h in range(2):
        counts = dot(jnp.where(odd == h, by_k, 0.0), per_block)
        most = jnp.max(counts[:groups] + counts[groups:], keepdims=True)
        over = over + jnp.where(most > CAP1, 1, 0)
    present_t = present.T
    column = where_in((z.tiles, z.tiles))[1]
    lane = where_in((groups, TILE))[1]
    for c in range(SIDE * SIDE):
        used = dot(jnp.where(column // z.block_cols == c, keep, 0.0), present_t)
        by_k = dot(member, jnp.where(used > 0, present, 0.0))
        for h in range(2):
            counts = dot(jnp.where(odd == h, by_k, 0.0), per_outer[h])
            me = c // SIDE if h == 0 else c % SIDE
            counts = jnp.where(lane == me, 0.0, counts[:groups] + counts[groups:])
            over = over + jnp.where(jnp.max(counts, keepdims=True) > CAP2, 1, 0)
    flag_ref[...] = jnp.broadcast_to(jnp.minimum(over, 1), flag_ref.shape)


def pack_kernel(z, plan, markov, first, second, both, held, inverse, entries, sem):
    r, c, l = position()
    load = pltpu.make_async_copy(markov, held, sem)
    load.start()

    @pl.loop(0, z.block_rows)
    def _(i):
        inverse[plan[z.tiles, r * z.block_rows + i]] = i

    def pair(t, counts):
        counts = list(counts)
        for odd in range(2):
            i = inverse[l * z.half + 2 * t + odd]
            mask = plan[r * z.block_rows + i, c]
            for j in range(z.block_cols):
                h = (odd + j) % 2
                entries[h, counts[h]] = i * 8 + j
                counts[h] = counts[h] + ((mask >> j) & 1)
        return tuple(counts)

    counts = lax.fori_loop(0, z.half // 2, pair, (jnp.int32(0), jnp.int32(0)))
    load.wait()
    for h, out in enumerate((first, second)):
        @pl.loop(0, jnp.minimum(counts[h], CAP1))
        def _(n, h=h, out=out):
            entry = entries[h, n]
            i = pl.multiple_of((entry // 8) * TILE, TILE)
            j = pl.multiple_of((entry % 8) * TILE, TILE)
            tile = held[pl.ds(i, TILE), pl.ds(j, TILE)]
            out[n] = tile
            both[h * CAP1 + n] = tile


def turned(distance, sign):
    d = lax.rem(distance * sign + 2 * SIDE, SIDE)
    return jnp.where(d == 0, 0, jnp.where(d == 3, 1, jnp.where(d == 1, 2, 3)))


def tables_kernel(z, plan, pattern_ref, keep_ref, _, sends, lists):
    r, c, l = position()
    cz, cy = c // SIDE, c % SIDE
    sign = 1 - 2 * l
    present = pattern_ref[...].astype(jnp.float32)
    keep = keep_ref[...].astype(jnp.float32)
    one = lambda x: jnp.where(x, 1.0, 0.0)

    place = plan[0:z.tiles, PLACE:PLACE + 1]
    place_row = plan[z.tiles:z.tiles + 1, 0:z.tiles]
    k, s = where_in((z.tiles, TILE))
    mine = one((place == l * z.half + s) & (s < z.half) & (k // z.block_rows == r))
    has = dot(present.T, mine)
    kept = dot(keep.T, mine)

    a, b = where_in((z.tiles, z.tiles))
    block_a, block_b = a // z.block_cols, b // z.block_cols
    below = one(b < a)
    u, v = where_in((TILE, TILE))
    earlier = one(u < v)

    def placed(mask, group):
        return dot(group * below, mask) + dot(dot(group, mask), earlier)

    def needed(there):
        return one(dot(jnp.where(block_b == there, present, 0.0), kept) > 0) * has

    halves = [one((k + s) % 2 == h) for h in range(2)]
    block = k // z.block_cols
    outers = [block // SIDE, block % SIDE]
    groups = [one(block_a // SIDE == block_b // SIDE), one(block_a % SIDE == block_b % SIDE)]
    me = [cz, cy]
    same_block = one(block_a == block_b)
    within = sum(halves[h] * placed(has * halves[h], same_block) for h in range(2))
    need_me = needed(c)
    lane = where_in((1, TILE))[1]
    place_left = jnp.zeros((z.tiles, TILE), jnp.float32)
    stride = SIDE * CAP1 + 3 * CAP2

    def compact(mask, position, value, columns, empty):
        where = jnp.where(mask > 0, position, -1.0).astype(jnp.int32)
        value = value.astype(jnp.int32) - empty
        row = jnp.zeros((1, TILE), jnp.int32)
        for n in columns:
            hit = where[:, n:n + 1] == where_in((z.tiles, TILE))[1]
            row = row + jnp.sum(jnp.where(hit, value[:, n:n + 1], 0), axis=0, keepdims=True)
        return row + empty

    for h in range(2):
        outer, inner = outers[h], outers[1 - h]
        held = turned(inner - me[1 - h], sign).astype(jnp.float32) * CAP1 + within
        ring = one(outer == me[h])
        for n, distance in enumerate((sign, -sign, 2)):
            there = lax.rem(me[h] + distance + SIDE, SIDE)
            target = there * SIDE + cy if h == 0 else cz * SIDE + there
            mask = needed(target) * halves[h] * ring
            row = compact(mask, placed(mask, groups[h]), held, range(z.half), 0)
            count = jnp.sum(jnp.sum(mask, axis=0, keepdims=True), axis=1, keepdims=True).astype(jnp.int32)
            sends[h * 3 + n:h * 3 + n + 1, :] = jnp.where(lane == TILE - 1, jnp.minimum(count, CAP2), row)
        mask = need_me * halves[h]
        arrived = SIDE * CAP1 + (turned(outer - me[h], sign).astype(jnp.float32) - 1) * CAP2 + placed(mask, groups[h])
        place_left = place_left + halves[h] * (h * stride + jnp.where(outer == me[h], held, arrived))

    core = place // z.half
    slot = place % z.half
    core_row = place_row // z.half
    slot_row = place_row % z.half
    ahead = one((a // z.block_rows == b // z.block_rows) & (core == core_row) & (slot_row < slot))
    column = dot(present, one((k == c * z.block_cols + s) & (s < z.block_cols)))
    place_right = jnp.zeros((z.tiles, TILE), jnp.float32)
    everyone = jnp.ones((TILE, TILE), jnp.float32)
    for h in range(2):
        half = one((slot + s) % 2 == h)
        mask = column * half
        place_right = place_right + half * (h * CAP1 + dot(mask, earlier) + dot(dot(ahead, mask), everyone))
    place_right = place_right + (((k // z.block_rows) * 2 + core) * (2 * CAP1)).astype(jnp.float32)

    pairs = z.half * z.block_cols
    to_slot = one((u == v // z.block_cols) & (v < pairs))
    to_column = one((u == v % z.block_cols) & (v < pairs))
    kept_here = dot(kept, to_slot) * one((k == c * z.block_cols + s % z.block_cols) & (s < pairs))
    mask = dot(has, to_slot) * dot(column, to_column) * jnp.sum(kept_here, axis=0, keepdims=True)
    where = dot(below, mask)

    def spread(x, to):
        x = x.astype(jnp.int32)
        return dot(x // 64, to) * 64 + dot(x % 64, to)

    value = spread(place_left, to_slot) * RIGHT_BITS + spread(place_right, to_column)
    empty = 2 * stride * RIGHT_BITS + 2 * z.blocks * 2 * CAP1
    count = jnp.sum(mask, axis=0, keepdims=True).astype(jnp.int32)
    for n in range(pairs):
        row = compact(mask, where, value, (n,), empty)
        lists[n:n + 1, :] = jnp.where(lane == TILE - 1, count[:, n:n + 1], row)


def load_all(parts, held, sem):
    copies, at = [], 0
    for n, part in enumerate(parts):
        size = part.shape[0]
        copies.append(pltpu.make_async_copy(part, held.at[pl.ds(at, size)], sem.at[n]))
        copies[-1].start()
        at += size
    return copies


def second_kernel(sends, *refs):
    sources, outs, (held, sem) = refs[:8], refs[8:14], refs[14:]
    for copy in load_all(sources, held, sem):
        copy.wait()
    for n, out in enumerate(outs):
        base = (n // 3) * SIDE * CAP1

        @pl.loop(0, sends[n, TILE - 1])
        def _(t, n=n, out=out, base=base):
            out[t] = held[base + sends[n, t]]


def product_kernel(z, n_left, n_right, lists, *refs):
    parts, (mine, other, totals) = refs[:n_left + n_right], refs[n_left + n_right:n_left + n_right + 3]
    left, right, stage, sums, sem, out_sem = refs[n_left + n_right + 3:]
    r, c, l = position()
    width = z.block_cols * TILE // 2
    copies = load_all(parts[:n_left], left, sem.at[0]) + load_all(parts[n_left:], right, sem.at[1])
    left[left.shape[0] - 1] = jnp.zeros((TILE, TILE), left.dtype)
    right[right.shape[0] - 1] = jnp.zeros((TILE, TILE), right.dtype)
    sums[...] = jnp.zeros_like(sums)
    for copy in copies:
        copy.wait()

    def outward(s):
        here = pl.ds(pl.multiple_of(s * TILE, TILE), TILE)
        slot = s % 2
        return [
            pltpu.make_async_copy(stage.at[slot, :, pl.ds(pl.multiple_of(l * width, TILE), width)], mine.at[here], out_sem.at[slot, 0]),
            pltpu.make_async_copy(stage.at[slot, :, pl.ds(pl.multiple_of((1 - l) * width, TILE), width)], other.at[here], out_sem.at[slot, 1]),
        ]

    @pl.loop(0, z.half)
    def _(s):
        @pl.when(s >= 2)
        def _():
            for copy in outward(s - 2):
                copy.wait()

        for j in range(z.block_cols):
            n = s * z.block_cols + j
            count = lists[n, TILE - 1]

            def group(g, acc, n=n):
                entries = [lists[n, g * GROUP + u] for u in range(GROUP)]
                lhs = jnp.concatenate([left[e // RIGHT_BITS] for e in entries], axis=1)
                rhs = jnp.concatenate([right[e % RIGHT_BITS] for e in entries], axis=0)
                return acc + jnp.dot(lhs, rhs, preferred_element_type=jnp.float32)

            acc = lax.fori_loop(0, (count + GROUP - 1) // GROUP, group, jnp.zeros((TILE, TILE), jnp.float32))
            kept = acc * acc
            here = slice(j * TILE, (j + 1) * TILE)
            stage[s % 2, :, here] = kept
            sums[:, here] += jnp.sum(kept.reshape(TILE // 8, 8, TILE), axis=0)
        for copy in outward(s):
            copy.start()

    whole = jnp.sum(sums[...], axis=0, keepdims=True)
    near, far = whole[:, :width], whole[:, width:]
    totals[0:1, :] = jnp.where(l == 0, near, far)
    totals[1:2, :] = jnp.where(l == 0, far, near)
    for s in (z.half - 2, z.half - 1):
        for copy in outward(s):
            copy.wait()


def scale_kernel(z, order, plan, mine, other, totals, received, out):
    r, c, l = position()
    factor = order / (totals[0:1, :] + received[...])

    @pl.loop(0, z.block_rows)
    def _(i):
        place = plan[z.tiles, r * z.block_rows + i]
        core = place // z.half
        source = pl.ds(pl.multiple_of((place % z.half) * TILE, TILE), TILE)
        target = pl.ds(pl.multiple_of(i * TILE, TILE), TILE)

        @pl.when(core == l)
        def _():
            out[target, :] = mine[source, :] * factor

        @pl.when(core != l)
        def _():
            out[target, :] = other[source, :] * factor


def turn(axis, distance, flip=True):
    pairs = []
    for place in range(SIDE * SIDE):
        for core in range(2):
            at = [place // SIDE, place % SIDE]
            at[axis] = (at[axis] + distance * (1 - 2 * core)) % SIDE
            pairs.append((place * 2 + core, (at[0] * SIDE + at[1]) * 2 + core))
    return pairs


def sparse(z, markov, pattern, keep):
    tile = lambda n: jax.ShapeDtypeStruct((n, TILE, TILE), markov.dtype)
    move = lambda x, axis, distance: lax.ppermute(x, ("col", "layer"), turn(axis, distance))
    width = z.block_cols * TILE // 2
    plan = pl.pallas_call(
        functools.partial(plan_kernel, z),
        out_shape=jax.ShapeDtypeStruct((z.tiles + 8, TILE), jnp.int32),
        in_specs=[VMEM],
        out_specs=VMEM,
        name="plan",
    )(pattern)
    first, second, both = pl.pallas_call(
        functools.partial(pack_kernel, z),
        out_shape=[tile(CAP1), tile(CAP1), tile(2 * CAP1)],
        in_specs=[SMEM, HBM],
        out_specs=[VMEM] * 3,
        scratch_shapes=[
            pltpu.VMEM(markov.shape, markov.dtype),
            pltpu.SMEM((z.block_rows,), jnp.int32),
            pltpu.SMEM((2, z.block_rows * z.block_cols), jnp.int32),
            pltpu.SemaphoreType.DMA,
        ],
        compiler_params=pltpu.CompilerParams(vmem_limit_bytes=24 * MIB),
        name="pack",
    )(plan, markov)

    sources = []
    for h, own in enumerate((first, second)):
        behind = move(own, 1 - h, 1)
        ahead = move(own, 1 - h, -1)
        sources.append([own, behind, ahead, move(behind, 1 - h, 1)])
    right = lax.all_gather(both, ("row", "layer"), axis=0, tiled=True)

    sends, lists = pl.pallas_call(
        functools.partial(tables_kernel, z),
        out_shape=[jax.ShapeDtypeStruct((8, TILE), jnp.int32), jax.ShapeDtypeStruct((z.half * z.block_cols, TILE), jnp.int32)],
        in_specs=[VMEM, VMEM, VMEM, HBM],
        out_specs=[VMEM, VMEM],
        name="tables",
    )(plan, pattern, keep, first)
    outs = pl.pallas_call(
        second_kernel,
        out_shape=[tile(CAP2)] * 6,
        in_specs=[SMEM] + [HBM] * 8,
        out_specs=[VMEM] * 6,
        scratch_shapes=[pltpu.VMEM((2 * SIDE * CAP1, TILE, TILE), markov.dtype), pltpu.SemaphoreType.DMA((8,))],
        compiler_params=pltpu.CompilerParams(vmem_limit_bytes=40 * MIB),
        name="second",
    )(sends, *sources[0], *sources[1])
    far = [move(outs[3 * h + 2], h, 1) for h in range(2)]
    near = [(move(outs[3 * h], h, 1), move(outs[3 * h + 1], h, -1)) for h in range(2)]
    far = [move(far[h], h, 1) for h in range(2)]
    left = []
    for h in range(2):
        left += sources[h] + [*near[h], far[h]]

    flag = pl.pallas_call(
        functools.partial(check_kernel, z),
        out_shape=jax.ShapeDtypeStruct((8, TILE), jnp.int32),
        in_specs=[VMEM, VMEM, HBM],
        out_specs=VMEM,
        name="check",
    )(pattern, keep, outs[0])

    n_left = sum(x.shape[0] for x in left)
    n_right = right.shape[0]
    rows = z.half * TILE
    mine, other, totals = pl.pallas_call(
        functools.partial(product_kernel, z, len(left), 1),
        out_shape=[
            jax.ShapeDtypeStruct((rows, width), jnp.float32),
            jax.ShapeDtypeStruct((rows, width), jnp.float32),
            jax.ShapeDtypeStruct((2, width), jnp.float32),
        ],
        in_specs=[SMEM] + [HBM] * (len(left) + 1),
        out_specs=[HBM, HBM, VMEM],
        scratch_shapes=[
            pltpu.VMEM((n_left + 1, TILE, TILE), markov.dtype),
            pltpu.VMEM((n_right + 1, TILE, TILE), markov.dtype),
            pltpu.VMEM((2, TILE, 2 * width), jnp.float32),
            pltpu.VMEM((8, 2 * width), jnp.float32),
            pltpu.SemaphoreType.DMA((2, len(left))),
            pltpu.SemaphoreType.DMA((2, 2)),
        ],
        compiler_params=pltpu.CompilerParams(vmem_limit_bytes=48 * MIB),
        name="product",
    )(lists, *left, right)
    swap = [(0, 1), (1, 0)]
    received = lax.ppermute(other, "layer", swap)
    summed = totals
    for d in range(1, z.blocks):
        summed = summed + lax.ppermute(totals, "row", [(n, (n + d) % z.blocks) for n in range(z.blocks)])
    out = pl.pallas_call(
        functools.partial(scale_kernel, z, float(z.tiles * TILE)),
        out_shape=jax.ShapeDtypeStruct((markov.shape[0], width), jnp.float32),
        in_specs=[SMEM] + [VMEM] * 4,
        out_specs=VMEM,
        compiler_params=pltpu.CompilerParams(vmem_limit_bytes=24 * MIB),
        name="scale",
    )(plan, mine, received, summed, lax.ppermute(summed[1:2], "layer", swap))
    return out, flag[0, 0]


def tile_scale(z, block, tiles, rows, cols):
    shaped = block.reshape(rows, TILE, cols, TILE)
    return (shaped * tiles.astype(block.dtype)[:, None, :, None]).reshape(block.shape)


def dense(z, markov, pattern, keep):
    r, c, l = position()
    cut = lambda x: lax.dynamic_slice(x, (r * z.block_rows, c * z.block_cols), (z.block_rows, z.block_cols))
    live = tile_scale(z, markov, cut(pattern), z.block_rows, z.block_cols)
    left = lax.dynamic_index_in_dim(live.reshape(live.shape[0], 2, live.shape[1] // 2), l, 1, keepdims=False)
    left = lax.all_gather(left, "col", axis=1, tiled=True)
    right = lax.all_gather(live, "row", axis=0, tiled=True)
    right = right.reshape(-1, 2, live.shape[1] // 2, live.shape[1])
    right = lax.dynamic_index_in_dim(right, l, 1, keepdims=False).reshape(-1, live.shape[1])
    square = lax.psum(jnp.dot(left, right, preferred_element_type=jnp.float32), "layer")
    kept = tile_scale(z, square * square, cut(keep), z.block_rows, z.block_cols)
    totals = lax.psum(jnp.sum(kept, axis=0), "row")
    scaled = (z.tiles * TILE) * kept / totals[None, :]
    return lax.dynamic_slice_in_dim(scaled, l * (live.shape[1] // 2), live.shape[1] // 2, 1)


def shards(markov, pattern, keep):
    z = Sizes(*markov.shape, pattern.shape[0])
    out, over = sparse(z, markov, pattern, keep)
    _, out = lax.while_loop(
        lambda state: state[0] > 0,
        lambda state: (jnp.zeros_like(state[0]), dense(z, markov, pattern, keep)),
        (over, out),
    )
    return out


def solution(mesh):
    in_specs = (P("row", "col"), P(), P())
    out_specs = P("row", ("col", "layer"))
    return jax.shard_map(shards, mesh=mesh, in_specs=in_specs, out_specs=out_specs, check_vma=False)
```

```python
import functools

import jax
import jax.numpy as jnp
from jax import lax
from jax.experimental import pallas as pl
from jax.experimental.layout import Layout, with_layout_constraint
from jax.experimental.pallas import tpu as pltpu
from jax.sharding import PartitionSpec as P

TILE = 128
SIDE = 4
GROUP = 4
TOGETHER = 4
CAP1 = 20
CAP2 = 40
CAPM = 48
CHUNK = 4
RIGHT_BITS = 4096
PLACE = 16
MIB = 1024 * 1024

SMEM = pl.BlockSpec(memory_space=pltpu.SMEM)
VMEM = pl.BlockSpec(memory_space=pltpu.VMEM)
HBM = pl.BlockSpec(memory_space=pltpu.HBM)


def position():
    return lax.axis_index("row"), lax.axis_index("col"), lax.axis_index("layer")


def dot(a, b):
    return jnp.dot(a.astype(jnp.bfloat16), b.astype(jnp.bfloat16), preferred_element_type=jnp.float32)


def where_in(shape):
    return lax.broadcasted_iota(jnp.int32, shape, 0), lax.broadcasted_iota(jnp.int32, shape, 1)


def ranks(block_rows, present):
    tiles = present.shape[0]
    ones = jnp.ones((8, tiles), jnp.bfloat16)
    level_row = lax.dot_general(ones, present.astype(jnp.bfloat16), (((1,), (1,)), ((), ())), preferred_element_type=jnp.float32)[:1]
    level_col = jnp.sum(present, axis=1, keepdims=True)
    a, b = where_in((tiles, tiles))
    same = jnp.where(a // block_rows == b // block_rows, 1.0, 0.0)
    above = jnp.where(level_col > level_row, 1.0, 0.0) + jnp.where(level_col == level_row, jnp.where(a < b, 1.0, 0.0), 0.0)
    below = jnp.where(level_col < level_row, 1.0, 0.0) + jnp.where(level_col == level_row, jnp.where(a > b, 1.0, 0.0), 0.0)
    return (
        jnp.sum(above * same, axis=0, keepdims=True).astype(jnp.int32),
        jnp.sum(below * same, axis=1, keepdims=True).astype(jnp.int32),
    )


def core_slot(rank):
    return ((rank + 1) // 2) % 2, rank // 2


class Sizes:
    def __init__(self, rows_dev, cols_dev, tiles):
        self.block_rows = rows_dev // TILE
        self.block_cols = cols_dev // TILE
        self.half = self.block_rows // 2
        self.tiles = tiles
        self.blocks = tiles // self.block_rows


def check_kernel(z, pattern_ref, keep_ref, _, flag_ref):
    groups = 2 * z.blocks
    present = pattern_ref[...].astype(jnp.float32)
    keep = keep_ref[...].astype(jnp.float32)
    rank, _ = ranks(z.block_rows, present)
    core, slot = core_slot(rank)
    owner, row = where_in((2 * groups, z.tiles))
    member = jnp.where(owner % groups == (row // z.block_rows) * 2 + core, 1.0, 0.0)
    member = member * jnp.where(owner // groups == slot % 2, 1.0, 0.0)
    i, k = where_in((2 * groups, z.tiles))
    odd = (i // groups + k) % 2
    i, k = where_in((z.tiles, TILE))
    per_block = jnp.where(i // z.block_cols == k, 1.0, 0.0)
    per_outer = [
        jnp.where(i // (z.block_cols * SIDE) == k, 1.0, 0.0),
        jnp.where((i // z.block_cols) % SIDE == k, 1.0, 0.0),
    ]
    by_k = dot(member, present)
    over = jnp.zeros((1, 1), jnp.int32)
    for h in range(2):
        counts = dot(jnp.where(odd == h, by_k, 0.0), per_block)
        most = jnp.max(counts[:groups] + counts[groups:], keepdims=True)
        over = over + jnp.where(most > CAP1, 1, 0)
    present_t = present.T
    column = where_in((z.tiles, z.tiles))[1]
    lane = where_in((groups, TILE))[1]
    needs = []
    for c in range(SIDE * SIDE):
        used = dot(jnp.where(column // z.block_cols == c, keep, 0.0), present_t)
        needs.append(jnp.where(used > 0, present, 0.0))
    cores = where_in((groups, TILE))[0] % 2
    for c in range(SIDE * SIDE):
        for h in range(2):
            outer, inner = axes_of(h, c)
            up, far, down = [needs[block_at(h, (outer + d) % SIDE, inner)] for d in (1, 2, 3)]
            far_up, far_down = jnp.maximum(far, up), jnp.maximum(far, down)
            for mask, most, core in ((far, CAP2, None), (up, CAP2, 1), (down, CAP2, 0), (far_up, CAPM, 0), (far_down, CAPM, 1)):
                counts = dot(jnp.where(odd == h, dot(member, mask), 0.0), per_outer[h])
                counts = counts[:groups] + counts[groups:]
                counted = jnp.where(lane == outer, counts, 0.0)
                if core is not None:
                    counted = jnp.where(cores == core, counted, 0.0)
                over = over + jnp.where(jnp.max(counted, keepdims=True) > most, 1, 0)
    flag_ref[...] = jnp.broadcast_to(jnp.minimum(over, 1), flag_ref.shape)


def axes_of(h, c):
    return (c // SIDE, c % SIDE) if h == 0 else (c % SIDE, c // SIDE)


def block_at(h, outer, inner):
    return outer * SIDE + inner if h == 0 else inner * SIDE + outer


def pack_kernel(z, pattern_ref, markov, plan_ref, first, second, both, held, plan, inverse, entries, sem):
    r, c, l = position()
    load = pltpu.make_async_copy(markov, held, sem.at[0])
    load.start()
    present = pattern_ref[...].astype(jnp.float32)
    i, k = where_in((z.tiles, TILE))
    weights = jnp.where(i // z.block_cols == k, jnp.left_shift(1, i % z.block_cols), 0)
    bits = dot(present, weights).astype(jnp.int32)
    rank_row, rank_col = ranks(z.block_rows, present)
    core, slot = core_slot(rank_row)
    plan_ref[...] = jnp.zeros_like(plan_ref)
    plan_ref[z.tiles:z.tiles + 1, 0:z.tiles] = core * z.half + slot
    core, slot = core_slot(rank_col)
    plan_ref[0:z.tiles, :] = jnp.where(k == PLACE, core * z.half + slot, bits)
    known = pltpu.make_async_copy(plan_ref, plan, sem.at[1])
    known.start()
    known.wait()

    @pl.loop(0, z.block_rows)
    def _(i):
        inverse[plan[z.tiles, r * z.block_rows + i]] = i

    def pair(t, counts):
        counts = list(counts)
        for odd in range(2):
            i = inverse[l * z.half + 2 * t + odd]
            mask = plan[r * z.block_rows + i, c]
            for j in range(z.block_cols):
                h = (odd + j) % 2
                entries[h, counts[h]] = i * 8 + j
                counts[h] = counts[h] + ((mask >> j) & 1)
        return tuple(counts)

    counts = lax.fori_loop(0, z.half // 2, pair, (jnp.int32(0), jnp.int32(0)))
    load.wait()
    for h, out in enumerate((first, second)):
        @pl.loop(0, jnp.minimum(counts[h], CAP1))
        def _(n, h=h, out=out):
            entry = entries[h, n]
            i = pl.multiple_of((entry // 8) * TILE, TILE)
            j = pl.multiple_of((entry % 8) * TILE, TILE)
            tile = held[pl.ds(i, TILE), pl.ds(j, TILE)]
            out[n] = tile
            both[h * CAP1 + n] = tile


def turned(distance, sign):
    d = lax.rem(distance * sign + 2 * SIDE, SIDE)
    return jnp.where(d == 0, 0, jnp.where(d == 3, 1, jnp.where(d == 1, 2, 3)))


def tables_kernel(z, plan, pattern_ref, keep_ref, _, sends, lists):
    r, c, l = position()
    cz, cy = c // SIDE, c % SIDE
    sign = 1 - 2 * l
    present = pattern_ref[...].astype(jnp.float32)
    keep = keep_ref[...].astype(jnp.float32)
    one = lambda x: jnp.where(x, 1.0, 0.0)

    place = plan[0:z.tiles, PLACE:PLACE + 1]
    place_row = plan[z.tiles:z.tiles + 1, 0:z.tiles]
    k, s = where_in((z.tiles, TILE))
    mine = one((place == l * z.half + s) & (s < z.half) & (k // z.block_rows == r))
    has = dot(present.T, mine)
    kept = dot(keep.T, mine)

    a, b = where_in((z.tiles, z.tiles))
    block_a, block_b = a // z.block_cols, b // z.block_cols
    below = one(b < a)
    u, v = where_in((TILE, TILE))
    earlier = one(u < v)

    def placed(mask, group):
        return dot(group * below, mask) + dot(dot(group, mask), earlier)

    def needed(there):
        return one(dot(jnp.where(block_b == there, present, 0.0), kept) > 0) * has

    halves = [one((k + s) % 2 == h) for h in range(2)]
    block = k // z.block_cols
    outers = [block // SIDE, block % SIDE]
    groups = [one(block_a // SIDE == block_b // SIDE), one(block_a % SIDE == block_b % SIDE)]
    me = [cz, cy]
    same_block = one(block_a == block_b)
    within = sum(halves[h] * placed(has * halves[h], same_block) for h in range(2))
    lane = where_in((1, TILE))[1]
    place_left = jnp.zeros((z.tiles, TILE), jnp.float32)
    stride = SIDE * CAP1 + CAPM + 2 * CAP2
    sizes = jnp.zeros((1, TILE), jnp.float32)
    everyone = jnp.ones((TILE, TILE), jnp.float32)

    def compact(mask, position, value, columns, empty):
        where = jnp.where(mask > 0, position, -1.0).astype(jnp.int32)
        value = value.astype(jnp.int32) - empty
        row = jnp.zeros((1, TILE), jnp.int32)
        for n in columns:
            hit = where[:, n:n + 1] == where_in((z.tiles, TILE))[1]
            row = row + jnp.sum(jnp.where(hit, value[:, n:n + 1], 0), axis=0, keepdims=True)
        return row + empty

    def total(mask):
        return jnp.sum(jnp.sum(mask, axis=0, keepdims=True), axis=1, keepdims=True).astype(jnp.int32)

    def tally(mask, part):
        return jnp.sum(jnp.where(s == part, dot(mask, everyone), 0.0), axis=0, keepdims=True)

    for h in range(2):
        outer, inner = outers[h], outers[1 - h]
        away = lax.rem((outer - me[h]) * sign + 2 * SIDE, SIDE)
        held = turned(inner - me[1 - h], sign).astype(jnp.float32) * CAP1 + within
        wants = []
        for distance in range(SIDE):
            there = lax.rem(me[h] + distance * sign + SIDE, SIDE)
            wants.append(needed(there * SIDE + cy if h == 0 else cz * SIDE + there) * halves[h])
        next_one = sum(jnp.where(away == d, wants[(d + 1) % SIDE], 0.0) for d in range(SIDE))
        opposite = sum(jnp.where(away == d, wants[(d + 2) % SIDE], 0.0) for d in range(SIDE))
        only_far, shared, only_next = opposite * (1 - next_one), opposite * next_one, next_one * (1 - opposite)
        count = lambda mask: dot(dot(groups[h], mask), everyone)
        start_shared = count(only_far)
        start_next = start_shared + count(shared)
        reached = only_far * placed(only_far, groups[h]) + shared * (start_shared + placed(shared, groups[h]))
        reached = reached + only_next * (start_next + placed(only_next, groups[h]))
        ring = one(away == 0)
        for n, (mask, where) in enumerate((
            ((only_far + shared + only_next) * ring, reached),
            (wants[3] * ring, placed(wants[3], groups[h])),
        )):
            row = compact(mask, where, held, range(z.half), 0)
            most = (CAPM, CAP2)[n]
            sends[h * 2 + n:h * 2 + n + 1, :] = jnp.where(lane == TILE - 1, jnp.minimum(total(mask), most), row)
        arrived = jnp.where(away == 3, reached, jnp.where(away == 1, CAPM + placed(wants[0], groups[h]), CAPM + CAP2 + reached))
        place_left = place_left + halves[h] * (h * stride + jnp.where(away == 0, held, SIDE * CAP1 + arrived))
        sizes = sizes + tally(has * halves[h] * ring, h * 7 + turned(inner - me[1 - h], sign))
        sizes = sizes + tally((shared + only_far + only_next) * one(away == 3), h * 7 + 4)
        sizes = sizes + tally(wants[0] * one(away == 1), h * 7 + 5)
        sizes = sizes + tally(opposite * one(away == 2), h * 7 + 6)

    core = place // z.half
    slot = place % z.half
    core_row = place_row // z.half
    slot_row = place_row % z.half
    ahead = one((a // z.block_rows == b // z.block_rows) & (core == core_row) & (slot_row < slot))
    column = dot(present, one((k == c * z.block_cols + s) & (s < z.block_cols)))
    place_right = jnp.zeros((z.tiles, TILE), jnp.float32)
    for h in range(2):
        half = one((slot + s) % 2 == h)
        mask = column * half
        sizes = sizes + tally(mask, 14 + (k // z.block_rows) * 4 + core * 2 + h)
        place_right = place_right + half * (h * CAP1 + dot(mask, earlier) + dot(dot(ahead, mask), everyone))
    place_right = place_right + (((k // z.block_rows) * 2 + core) * (2 * CAP1)).astype(jnp.float32)

    pairs = z.half * z.block_cols
    to_slot = one((u == v // z.block_cols) & (v < pairs))
    to_column = one((u == v % z.block_cols) & (v < pairs))
    kept_here = dot(kept, to_slot) * one((k == c * z.block_cols + s % z.block_cols) & (s < pairs))
    mask = dot(has, to_slot) * dot(column, to_column) * jnp.sum(kept_here, axis=0, keepdims=True)
    where = dot(below, mask)

    def spread(x, to):
        x = x.astype(jnp.int32)
        return dot(x // 64, to) * 64 + dot(x % 64, to)

    value = spread(place_left, to_slot) * RIGHT_BITS + spread(place_right, to_column)
    empty = 2 * stride * RIGHT_BITS + 2 * z.blocks * 2 * CAP1
    count = jnp.sum(mask, axis=0, keepdims=True).astype(jnp.int32)
    for n in range(pairs):
        row = compact(mask, where, value, (n,), empty)
        lists[n:n + 1, :] = jnp.where(lane == TILE - 1, count[:, n:n + 1], row)
    lists[pairs:pairs + 1, :] = jnp.full((1, TILE), empty, jnp.int32)
    lists[pairs + 1:pairs + 2, :] = sizes.astype(jnp.int32)


def load_all(parts, held, sem):
    copies, at = [], 0
    for n, part in enumerate(parts):
        part, start, size = part if isinstance(part, tuple) else (part, 0, part.shape[0])
        copies.append(pltpu.make_async_copy(part.at[pl.ds(start, size)], held.at[pl.ds(at, size)], sem.at[n]))
        copies[-1].start()
        at += size
    return copies


def second_kernel(sends_ref, *refs):
    sources, outs, (held, sends, sem, known) = refs[:8], refs[8:12], refs[12:]
    told = pltpu.make_async_copy(sends_ref, sends, known)
    told.start()
    copies = load_all(sources, held, sem)
    told.wait()
    for copy in copies:
        copy.wait()
    for h in range(2):
        ahead, behind = outs[2 * h:2 * h + 2]
        for n, out in enumerate((ahead, behind)):
            @pl.loop(0, sends[2 * h + n, TILE - 1])
            def _(t, n=2 * h + n, out=out, base=h * SIDE * CAP1):
                out[t] = held[base + sends[n, t]]


def product_kernel(z, n_left, n_right, lists, _, *refs):
    parts, (mine, other, totals) = refs[:n_left + n_right], refs[n_left + n_right:n_left + n_right + 3]
    left, right, total, sums, work, sem, out_sem = refs[n_left + n_right + 3:]
    r, c, l = position()
    width = z.block_cols * TILE // 2
    pairs = z.half * z.block_cols

    def pieces():
        at = 0
        for n in range(n_left):
            yield n, parts[n], 0, left, at, parts[n].shape[0]
            at += parts[n].shape[0]
        for n in range(2 * 2 * z.blocks):
            yield n_left + n, parts[n_left], n * CAP1, right, n * CAP1, CAP1

    def each_copy(act):
        for n, source, start, target, at, room in pieces():
            size = lists[pairs + 1, n]

            @pl.loop(0, jnp.minimum((size + CHUNK - 1) // CHUNK, room // CHUNK))
            def _(t, n=n, source=source, start=start, target=target, at=at):
                act(pltpu.make_async_copy(source.at[pl.ds(start + t * CHUNK, CHUNK)], target.at[pl.ds(at + t * CHUNK, CHUNK)], sem.at[n]))

    each_copy(lambda copy: copy.start())
    left[left.shape[0] - 1] = jnp.zeros((TILE, TILE), left.dtype)
    right[right.shape[0] - 1] = jnp.zeros((TILE, TILE), right.dtype)
    sums[...] = jnp.zeros_like(sums)

    @pl.loop(0, pairs + 1)
    def _(n):
        total[n] = jnp.zeros((TILE, TILE), jnp.float32)

    def flatten(n, at):
        groups = (lists[n, TILE - 1] + GROUP - 1) // GROUP

        def one_group(g, at):
            work[at] = n * 32 + g
            return at + 1

        return lax.fori_loop(0, groups, one_group, at)

    found = lax.fori_loop(0, pairs, flatten, jnp.int32(0))
    for extra in range(TOGETHER):
        work[found + extra] = pairs * 32
    each_copy(lambda copy: copy.wait())

    @pl.loop(0, (found + TOGETHER - 1) // TOGETHER)
    def _(t):
        for m in range(TOGETHER):
            item = work[t * TOGETHER + m]
            n = item // 32
            entries = [lists[n, (item % 32) * GROUP + u] for u in range(GROUP)]
            lhs = jnp.concatenate([left[e // RIGHT_BITS] for e in entries], axis=1)
            rhs = jnp.concatenate([right[e % RIGHT_BITS] for e in entries], axis=0)
            total[n] += jnp.dot(lhs, rhs, preferred_element_type=jnp.float32)

    per_core = z.block_cols // 2

    @pl.loop(0, z.half)
    def _(s):
        for j in range(z.block_cols):
            n = s * z.block_cols + j
            value = total[n]
            kept = value * value
            total[n] = kept
            sums[:, j * TILE:(j + 1) * TILE] += jnp.sum(kept.reshape(TILE // 8, 8, TILE), axis=0)
        n = s * z.block_cols
        near = pl.ds(n + l * per_core, per_core)
        far = pl.ds(n + (1 - l) * per_core, per_core)
        rows = pl.ds(s * per_core, per_core)
        pltpu.make_async_copy(total.at[near], mine.at[rows], out_sem.at[0]).start()
        pltpu.make_async_copy(total.at[far], other.at[rows], out_sem.at[1]).start()

    whole = jnp.sum(sums[...], axis=0, keepdims=True)
    near, far = whole[:, :width], whole[:, width:]
    totals[0:1, :] = jnp.where(l == 0, near, far)
    totals[1:2, :] = jnp.where(l == 0, far, near)
    pltpu.make_async_copy(mine, mine, out_sem.at[0]).wait()
    pltpu.make_async_copy(other, other, out_sem.at[1]).wait()


def scale_kernel(z, order, plan, mine, other, totals, received, out):
    r, c, l = position()
    factor = order / (totals[0:1, :] + received[...])
    per_core = z.block_cols // 2

    @pl.loop(0, z.block_rows)
    def _(i):
        place = plan[z.tiles, r * z.block_rows + i]
        core = place // z.half
        first = (place % z.half) * per_core
        target = pl.ds(pl.multiple_of(i * TILE, TILE), TILE)

        def scaled(source):
            for j in range(per_core):
                columns = slice(j * TILE, (j + 1) * TILE)
                out[target, columns] = source[first + j] * factor[:, columns]

        pl.when(core == l)(lambda: scaled(mine))
        pl.when(core != l)(lambda: scaled(other))


def turn(axis, distance, flip=True):
    pairs = []
    for place in range(SIDE * SIDE):
        for core in range(2):
            at = [place // SIDE, place % SIDE]
            at[axis] = (at[axis] + distance * (1 - 2 * core)) % SIDE
            pairs.append((place * 2 + core, (at[0] * SIDE + at[1]) * 2 + core))
    return pairs


def sparse(z, markov, pattern, keep):
    tile = lambda n: jax.ShapeDtypeStruct((n, TILE, TILE), markov.dtype)
    move = lambda x, axis, distance: lax.ppermute(x, ("col", "layer"), turn(axis, distance))
    width = z.block_cols * TILE // 2
    plan, first, second, both = pl.pallas_call(
        functools.partial(pack_kernel, z),
        out_shape=[jax.ShapeDtypeStruct((z.tiles + 8, TILE), jnp.int32), tile(CAP1), tile(CAP1), tile(2 * CAP1)],
        in_specs=[VMEM, HBM],
        out_specs=[VMEM] * 4,
        scratch_shapes=[
            pltpu.VMEM(markov.shape, markov.dtype),
            pltpu.SMEM((z.tiles + 8, TILE), jnp.int32),
            pltpu.SMEM((z.block_rows,), jnp.int32),
            pltpu.SMEM((2, z.block_rows * z.block_cols), jnp.int32),
            pltpu.SemaphoreType.DMA((2,)),
        ],
        compiler_params=pltpu.CompilerParams(vmem_limit_bytes=16 * MIB),
        name="pack",
    )(pattern, markov)

    sources = []
    for h, own in enumerate((first, second)):
        behind = move(own, 1 - h, 1)
        ahead = move(own, 1 - h, -1)
        sources.append([own, behind, ahead, move(behind, 1 - h, 1)])
    right = lax.all_gather(both, ("row", "layer"), axis=0, tiled=True)

    sends, lists = pl.pallas_call(
        functools.partial(tables_kernel, z),
        out_shape=[jax.ShapeDtypeStruct((8, TILE), jnp.int32), jax.ShapeDtypeStruct((z.half * z.block_cols + 8, TILE), jnp.int32)],
        in_specs=[VMEM, VMEM, VMEM, HBM],
        out_specs=[VMEM, VMEM],
        compiler_params=pltpu.CompilerParams(vmem_limit_bytes=8 * MIB),
        name="tables",
    )(plan, pattern, keep, first)
    outs = pl.pallas_call(
        second_kernel,
        out_shape=[tile(CAPM), tile(CAP2)] * 2,
        in_specs=[HBM] * 9,
        out_specs=[VMEM] * 4,
        scratch_shapes=[
            pltpu.VMEM((2 * SIDE * CAP1, TILE, TILE), markov.dtype),
            pltpu.SMEM((8, TILE), jnp.int32),
            pltpu.SemaphoreType.DMA((8,)),
            pltpu.SemaphoreType.DMA,
        ],
        compiler_params=pltpu.CompilerParams(vmem_limit_bytes=20 * MIB),
        name="second",
    )(sends, *sources[0], *sources[1])
    ahead = [move(outs[2 * h], h, 1) for h in range(2)]
    behind = [move(outs[2 * h + 1], h, -1) for h in range(2)]
    far = [move(ahead[h][:CAP2], h, 1) for h in range(2)]
    left = []
    for h in range(2):
        left += sources[h] + [ahead[h], behind[h], far[h]]

    flag = pl.pallas_call(
        functools.partial(check_kernel, z),
        out_shape=jax.ShapeDtypeStruct((8, TILE), jnp.int32),
        in_specs=[VMEM, VMEM, HBM],
        out_specs=VMEM,
        compiler_params=pltpu.CompilerParams(vmem_limit_bytes=8 * MIB),
        name="check",
    )(pattern, keep, outs[0])

    n_left = 2 * (SIDE * CAP1 + CAPM + 2 * CAP2)
    n_right = right.shape[0]
    pairs = z.half * z.block_cols
    mine, other, totals = pl.pallas_call(
        functools.partial(product_kernel, z, len(left), 1),
        out_shape=[
            jax.ShapeDtypeStruct((pairs // 2, TILE, TILE), jnp.float32),
            jax.ShapeDtypeStruct((pairs // 2, TILE, TILE), jnp.float32),
            jax.ShapeDtypeStruct((2, width), jnp.float32),
        ],
        in_specs=[SMEM] + [HBM] * (len(left) + 2),
        out_specs=[HBM, HBM, VMEM],
        scratch_shapes=[
            pltpu.VMEM((n_left + 1, TILE, TILE), markov.dtype),
            pltpu.VMEM((n_right + 1, TILE, TILE), markov.dtype),
            pltpu.VMEM((z.half * z.block_cols + 1, TILE, TILE), jnp.float32),
            pltpu.VMEM((8, 2 * width), jnp.float32),
            pltpu.SMEM((z.half * z.block_cols * 32 + TOGETHER,), jnp.int32),
            pltpu.SemaphoreType.DMA((len(left) + 4 * z.blocks,)),
            pltpu.SemaphoreType.DMA((2,)),
        ],
        compiler_params=pltpu.CompilerParams(vmem_limit_bytes=60 * MIB),
        name="product",
    )(lists, flag, *left, right)
    swap = [(0, 1), (1, 0)]
    received = lax.ppermute(other, "layer", swap)
    summed = totals
    for d in range(1, z.blocks):
        summed = summed + lax.ppermute(totals, "row", [(n, (n + d) % z.blocks) for n in range(z.blocks)])
    out = pl.pallas_call(
        functools.partial(scale_kernel, z, float(z.tiles * TILE)),
        out_shape=jax.ShapeDtypeStruct((markov.shape[0], width), jnp.float32),
        in_specs=[SMEM] + [VMEM] * 4,
        out_specs=VMEM,
        compiler_params=pltpu.CompilerParams(vmem_limit_bytes=16 * MIB),
        name="scale",
    )(plan, mine, received, summed, lax.ppermute(summed[1:2], "layer", swap))
    return out, flag[0, 0]


def tile_scale(z, block, tiles, rows, cols):
    shaped = block.reshape(rows, TILE, cols, TILE)
    return (shaped * tiles.astype(block.dtype)[:, None, :, None]).reshape(block.shape)


def dense(z, markov, pattern, keep):
    straight = Layout(major_to_minor=(0, 1))
    markov, pattern, keep = [with_layout_constraint(x, straight) for x in (markov, pattern, keep)]
    r, c, l = position()
    cut = lambda x: lax.dynamic_slice(x, (r * z.block_rows, c * z.block_cols), (z.block_rows, z.block_cols))
    live = tile_scale(z, markov, cut(pattern), z.block_rows, z.block_cols)
    left = lax.dynamic_index_in_dim(live.reshape(live.shape[0], 2, live.shape[1] // 2), l, 1, keepdims=False)
    left = lax.all_gather(left, "col", axis=1, tiled=True)
    right = lax.all_gather(live, "row", axis=0, tiled=True)
    right = right.reshape(-1, 2, live.shape[1] // 2, live.shape[1])
    right = lax.dynamic_index_in_dim(right, l, 1, keepdims=False).reshape(-1, live.shape[1])
    square = lax.psum(jnp.dot(left, right, preferred_element_type=jnp.float32), "layer")
    kept = tile_scale(z, square * square, cut(keep), z.block_rows, z.block_cols)
    totals = lax.psum(jnp.sum(kept, axis=0), "row")
    scaled = (z.tiles * TILE) * kept / totals[None, :]
    return lax.dynamic_slice_in_dim(scaled, l * (live.shape[1] // 2), live.shape[1] // 2, 1)


def shards(markov, pattern, keep):
    z = Sizes(*markov.shape, pattern.shape[0])
    out, over = sparse(z, markov, pattern, keep)
    _, out = lax.while_loop(
        lambda state: state[0] > 0,
        lambda state: (jnp.zeros_like(state[0]), dense(z, markov, pattern, keep)),
        (over, out),
    )
    return out


def solution(mesh):
    in_specs = (P("row", "col"), P(), P())
    out_specs = P("row", ("col", "layer"))
    return jax.shard_map(shards, mesh=mesh, in_specs=in_specs, out_specs=out_specs, check_vma=False)
```

```python
import functools

import jax
import jax.numpy as jnp
from jax import lax
from jax.experimental import pallas as pl
from jax.experimental.layout import Layout, with_layout_constraint
from jax.experimental.pallas import tpu as pltpu
from jax.sharding import PartitionSpec as P

TILE = 128
SIDE = 4
GROUP = 4
TOGETHER = 4
CAP1 = 20
CAPF = 24
CAPM = 44
CHUNK = 4
EARLY_LIMIT = 60
LATE_LIMIT = 60
RIGHT_BITS = 4096
PLACE = 16
MIB = 1024 * 1024

SMEM = pl.BlockSpec(memory_space=pltpu.SMEM)
VMEM = pl.BlockSpec(memory_space=pltpu.VMEM)
HBM = pl.BlockSpec(memory_space=pltpu.HBM)


def position():
    return lax.axis_index("row"), lax.axis_index("col"), lax.axis_index("layer")


def dot(a, b):
    return jnp.dot(a.astype(jnp.bfloat16), b.astype(jnp.bfloat16), preferred_element_type=jnp.float32)


def where_in(shape):
    return lax.broadcasted_iota(jnp.int32, shape, 0), lax.broadcasted_iota(jnp.int32, shape, 1)


def ranks(block_rows, present):
    tiles = present.shape[0]
    ones = jnp.ones((8, tiles), jnp.bfloat16)
    level_row = lax.dot_general(ones, present.astype(jnp.bfloat16), (((1,), (1,)), ((), ())), preferred_element_type=jnp.float32)[:1]
    level_col = jnp.sum(present, axis=1, keepdims=True)
    a, b = where_in((tiles, tiles))
    same = jnp.where(a // block_rows == b // block_rows, 1.0, 0.0)
    above = jnp.where(level_col > level_row, 1.0, 0.0) + jnp.where(level_col == level_row, jnp.where(a < b, 1.0, 0.0), 0.0)
    below = jnp.where(level_col < level_row, 1.0, 0.0) + jnp.where(level_col == level_row, jnp.where(a > b, 1.0, 0.0), 0.0)
    return (
        jnp.sum(above * same, axis=0, keepdims=True).astype(jnp.int32),
        jnp.sum(below * same, axis=1, keepdims=True).astype(jnp.int32),
    )


def core_slot(rank):
    return ((rank + 1) // 2) % 2, rank // 2


class Sizes:
    def __init__(self, rows_dev, cols_dev, tiles):
        self.block_rows = rows_dev // TILE
        self.block_cols = cols_dev // TILE
        self.half = self.block_rows // 2
        self.tiles = tiles
        self.blocks = tiles // self.block_rows


def check_kernel(z, pattern_ref, keep_ref, _, flag_ref):
    groups = 2 * z.blocks
    present = pattern_ref[...].astype(jnp.float32)
    keep = keep_ref[...].astype(jnp.float32)
    rank, rank_col = ranks(z.block_rows, present)
    core, slot = core_slot(rank)
    a, b = where_in((z.tiles, z.tiles))
    first_way = jnp.where(((core_slot(rank_col)[1] + b) // 2) % 2 == 0, 1.0, 0.0)
    owner, row = where_in((2 * groups, z.tiles))
    member = jnp.where(owner % groups == (row // z.block_rows) * 2 + core, 1.0, 0.0)
    member = member * jnp.where(owner // groups == slot % 2, 1.0, 0.0)
    i, k = where_in((2 * groups, z.tiles))
    odd = (i // groups + k) % 2
    i, k = where_in((z.tiles, TILE))
    per_block = jnp.where(i // z.block_cols == k, 1.0, 0.0)
    per_outer = [
        jnp.where(i // (z.block_cols * SIDE) == k, 1.0, 0.0),
        jnp.where((i // z.block_cols) % SIDE == k, 1.0, 0.0),
    ]
    by_k = dot(member, present)
    over = jnp.zeros((1, 1), jnp.int32)
    for h in range(2):
        counts = dot(jnp.where(odd == h, by_k, 0.0), per_block)
        most = jnp.max(counts[:groups] + counts[groups:], keepdims=True)
        over = over + jnp.where(most > CAP1, 1, 0)
    present_t = present.T
    column = where_in((z.tiles, z.tiles))[1]
    lane = where_in((groups, TILE))[1]
    needs = []
    for c in range(SIDE * SIDE):
        used = dot(jnp.where(column // z.block_cols == c, keep, 0.0), present_t)
        needs.append(jnp.where(used > 0, present, 0.0))
    cores = where_in((groups, TILE))[0] % 2
    for c in range(SIDE * SIDE):
        for h in range(2):
            outer, inner = axes_of(h, c)
            up, far, down = [needs[block_at(h, (outer + d) % SIDE, inner)] for d in (1, 2, 3)]
            one_far, two_far = far * first_way, far * (1 - first_way)
            for mask, most, core in (
                (one_far, CAPF, None),
                (two_far, CAPF, None),
                (jnp.maximum(one_far, up), CAPM, 0),
                (jnp.maximum(two_far, down), CAPM, 0),
                (jnp.maximum(one_far, down), CAPM, 1),
                (jnp.maximum(two_far, up), CAPM, 1),
            ):
                counts = dot(jnp.where(odd == h, dot(member, mask), 0.0), per_outer[h])
                counts = counts[:groups] + counts[groups:]
                counted = jnp.where(lane == outer, counts, 0.0)
                if core is not None:
                    counted = jnp.where(cores == core, counted, 0.0)
                over = over + jnp.where(jnp.max(counted, keepdims=True) > most, 1, 0)
    flag_ref[...] = jnp.minimum(over, 1)


def axes_of(h, c):
    return (c // SIDE, c % SIDE) if h == 0 else (c % SIDE, c // SIDE)


def block_at(h, outer, inner):
    return outer * SIDE + inner if h == 0 else inner * SIDE + outer


def pack_kernel(z, pattern_ref, markov, plan_ref, places, first, second, both, held, plan, inverse, entries, sem):
    r, c, l = position()
    load = pltpu.make_async_copy(markov, held, sem.at[0])
    load.start()
    present = pattern_ref[...].astype(jnp.float32)
    i, k = where_in((z.tiles, TILE))
    weights = jnp.where(i // z.block_cols == k, jnp.left_shift(1, i % z.block_cols), 0)
    bits = dot(present, weights).astype(jnp.int32)
    rank_row, rank_col = ranks(z.block_rows, present)
    core, slot = core_slot(rank_row)
    plan_ref[...] = jnp.zeros_like(plan_ref)
    plan_ref[z.tiles:z.tiles + 1, 0:z.tiles] = core * z.half + slot
    core, slot = core_slot(rank_col)
    plan_ref[0:z.tiles, :] = jnp.where(k == PLACE, core * z.half + slot, bits)
    places[...] = plan_ref[z.tiles:z.tiles + 8, :]
    known = pltpu.make_async_copy(plan_ref, plan, sem.at[1])
    known.start()
    known.wait()

    @pl.loop(0, z.block_rows)
    def _(i):
        inverse[plan[z.tiles, r * z.block_rows + i]] = i

    def pair(t, counts):
        counts = list(counts)
        for odd in range(2):
            i = inverse[l * z.half + 2 * t + odd]
            mask = plan[r * z.block_rows + i, c]
            for j in range(z.block_cols):
                h = (odd + j) % 2
                entries[h, counts[h]] = i * 8 + j
                counts[h] = counts[h] + ((mask >> j) & 1)
        return tuple(counts)

    counts = lax.fori_loop(0, z.half // 2, pair, (jnp.int32(0), jnp.int32(0)))
    load.wait()
    for h, out in enumerate((first, second)):
        @pl.loop(0, jnp.minimum(counts[h], CAP1))
        def _(n, h=h, out=out):
            entry = entries[h, n]
            i = pl.multiple_of((entry // 8) * TILE, TILE)
            j = pl.multiple_of((entry % 8) * TILE, TILE)
            tile = held[pl.ds(i, TILE), pl.ds(j, TILE)]
            out[n] = tile
            both[h * CAP1 + n] = tile


def turned(distance, sign):
    d = lax.rem(distance * sign + 2 * SIDE, SIDE)
    return jnp.where(d == 0, 0, jnp.where(d == 3, 1, jnp.where(d == 1, 2, 3)))


def tables_kernel(z, plan, pattern_ref, keep_ref, _, sends, early, late):
    r, c, l = position()
    cz, cy = c // SIDE, c % SIDE
    sign = 1 - 2 * l
    present = pattern_ref[...].astype(jnp.float32)
    keep = keep_ref[...].astype(jnp.float32)
    one = lambda x: jnp.where(x, 1.0, 0.0)

    spot = plan[0:z.tiles, PLACE:PLACE + 1]
    place_row = plan[z.tiles:z.tiles + 1, 0:z.tiles]
    k, s = where_in((z.tiles, TILE))
    mine = one((spot == l * z.half + s) & (s < z.half) & (k // z.block_rows == r))
    has = dot(present.T, mine)
    kept = dot(keep.T, mine)

    a, b = where_in((z.tiles, z.tiles))
    block_a, block_b = a // z.block_cols, b // z.block_cols
    below = one(b < a)
    u, v = where_in((TILE, TILE))
    earlier = one(u < v)

    def placed(mask, group):
        return dot(group * below, mask) + dot(dot(group, mask), earlier)

    def needed(there):
        return one(dot(jnp.where(block_b == there, present, 0.0), kept) > 0) * has

    halves = [one((k + s) % 2 == h) for h in range(2)]
    block = k // z.block_cols
    outers = [block // SIDE, block % SIDE]
    groups = [one(block_a // SIDE == block_b // SIDE), one(block_a % SIDE == block_b % SIDE)]
    me = [cz, cy]
    same_block = one(block_a == block_b)
    within = sum(halves[h] * placed(has * halves[h], same_block) for h in range(2))
    lane = where_in((1, TILE))[1]
    place_left = jnp.zeros((z.tiles, TILE), jnp.float32)
    stride = SIDE * CAP1 + 2 * CAPM
    onward = [one(((k + s) // 2) % 2 == way) for way in range(2)]
    sizes = jnp.zeros((1, TILE), jnp.float32)
    late_sizes = jnp.zeros((1, TILE), jnp.float32)
    is_late = jnp.zeros((z.tiles, TILE), jnp.float32)
    everyone = jnp.ones((TILE, TILE), jnp.float32)

    def compact(mask, position, value, columns, empty):
        where = jnp.where(mask > 0, position, -1.0).astype(jnp.int32)
        value = value.astype(jnp.int32) - empty
        row = jnp.zeros((1, TILE), jnp.int32)
        for n in columns:
            hit = where[:, n:n + 1] == where_in((z.tiles, TILE))[1]
            row = row + jnp.sum(jnp.where(hit, value[:, n:n + 1], 0), axis=0, keepdims=True)
        return row + empty

    def total(mask):
        return jnp.sum(jnp.sum(mask, axis=0, keepdims=True), axis=1, keepdims=True).astype(jnp.int32)

    def tally(mask, part):
        return jnp.sum(jnp.where(s == part, dot(mask, everyone), 0.0), axis=0, keepdims=True)

    for h in range(2):
        outer, inner = outers[h], outers[1 - h]
        away = lax.rem((outer - me[h]) * sign + 2 * SIDE, SIDE)
        held = turned(inner - me[1 - h], sign).astype(jnp.float32) * CAP1 + within
        wants = []
        for distance in range(SIDE):
            there = lax.rem(me[h] + distance * sign + SIDE, SIDE)
            wants.append(needed(there * SIDE + cy if h == 0 else cz * SIDE + there) * halves[h])
        opposite = sum(jnp.where(away == d, wants[(d + 2) % SIDE], 0.0) for d in range(SIDE))
        count = lambda mask: dot(dot(groups[h], mask), everyone)
        ring = one(away == 0)
        unions, reached = [], []
        for way in range(2):
            beside = sum(jnp.where(away == d, wants[(d + (1, 3)[way]) % SIDE], 0.0) for d in range(SIDE))
            far = opposite * onward[way]
            only_far, shared, only_beside = far * (1 - beside), far * beside, beside * (1 - far)
            start_shared = count(only_far)
            start_beside = start_shared + count(shared)
            place = only_far * placed(only_far, groups[h]) + shared * (start_shared + placed(shared, groups[h]))
            reached.append(place + only_beside * (start_beside + placed(only_beside, groups[h])))
            unions.append(only_far + shared + only_beside)
            row = compact(unions[way] * ring, reached[way], held, range(z.half), 0)
            n = h * 2 + way
            sends[n:n + 1, :] = jnp.where(lane == TILE - 1, jnp.minimum(total(unions[way] * ring), CAPM), row)
        arrived = jnp.where(away == 3, reached[0], CAPM + reached[1])
        arrived_far = onward[0] * reached[0] + onward[1] * (CAPF + reached[1])
        early_place = h * stride + jnp.where(away == 0, held, SIDE * CAP1 + arrived)
        place_left = place_left + halves[h] * jnp.where(away == 2, h * 2 * CAPF + arrived_far, early_place)
        is_late = is_late + halves[h] * one(away == 2)
        sizes = sizes + tally(has * halves[h] * ring, h * 6 + turned(inner - me[1 - h], sign))
        for way in range(2):
            sizes = sizes + tally(unions[way] * one(away == (3, 1)[way]), h * 6 + 4 + way)
            late_sizes = late_sizes + tally(opposite * onward[way] * one(away == 2), h * 2 + way)

    core = spot // z.half
    slot = spot % z.half
    core_row = place_row // z.half
    slot_row = place_row % z.half
    ahead = one((a // z.block_rows == b // z.block_rows) & (core == core_row) & (slot_row < slot))
    column = dot(present, one((k == c * z.block_cols + s) & (s < z.block_cols)))
    place_right = jnp.zeros((z.tiles, TILE), jnp.float32)
    for h in range(2):
        half = one((slot + s) % 2 == h)
        mask = column * half
        right_part = ((k // z.block_rows) * 2 + core) * 2 + h
        sizes = sizes + tally(mask, 12 + right_part)
        late_sizes = late_sizes + tally(mask, 4 + right_part)
        place_right = place_right + half * (h * CAP1 + dot(mask, earlier) + dot(dot(ahead, mask), everyone))
    place_right = place_right + ((right_part // 2) * (2 * CAP1)).astype(jnp.float32)

    pairs = z.half * z.block_cols
    to_slot = one((u == v // z.block_cols) & (v < pairs))
    to_column = one((u == v % z.block_cols) & (v < pairs))
    kept_here = dot(kept, to_slot) * one((k == c * z.block_cols + s % z.block_cols) & (s < pairs))
    mask = dot(has, to_slot) * dot(column, to_column) * jnp.sum(kept_here, axis=0, keepdims=True)
    is_late = dot(is_late, to_slot)

    def spread(x, to):
        x = x.astype(jnp.int32)
        return dot(x // 64, to) * 64 + dot(x % 64, to)

    value = spread(place_left, to_slot) * RIGHT_BITS + spread(place_right, to_column)
    for lists, mask, parts, n_left in ((early, mask * (1 - is_late), sizes, 2 * stride), (late, mask * is_late, late_sizes, 4 * CAPF)):
        empty = n_left * RIGHT_BITS + 4 * z.blocks * CAP1
        where = dot(below, mask)
        count = jnp.sum(mask, axis=0, keepdims=True).astype(jnp.int32)
        for n in range(pairs):
            row = compact(mask, where, value, (n,), empty)
            lists[n:n + 1, :] = jnp.where(lane == TILE - 1, count[:, n:n + 1], row)
        lists[pairs:pairs + 1, :] = jnp.full((1, TILE), empty, jnp.int32)
        lists[pairs + 1:pairs + 2, :] = parts.astype(jnp.int32)


def load_all(parts, held, sem):
    copies, at = [], 0
    for n, part in enumerate(parts):
        part, start, size = part if isinstance(part, tuple) else (part, 0, part.shape[0])
        copies.append(pltpu.make_async_copy(part.at[pl.ds(start, size)], held.at[pl.ds(at, size)], sem.at[n]))
        copies[-1].start()
        at += size
    return copies


def second_kernel(sends_ref, _, *refs):
    sources, outs, (held, sends, sem, known) = refs[:8], refs[8:12], refs[12:]
    told = pltpu.make_async_copy(sends_ref, sends, known)
    told.start()
    copies = load_all(sources, held, sem)
    told.wait()
    for copy in copies:
        copy.wait()
    for h in range(2):
        ahead, behind = outs[2 * h:2 * h + 2]
        for n, out in enumerate((ahead, behind)):
            @pl.loop(0, sends[2 * h + n, TILE - 1])
            def _(t, n=2 * h + n, out=out, base=h * SIDE * CAP1):
                out[t] = held[base + sends[n, t]]


def front_kernel(*refs):
    piece = CAPF // 2
    copies = [
        pltpu.make_async_copy(refs[n].at[pl.ds(m * piece, piece)], refs[4 + n].at[pl.ds(m * piece, piece)], refs[8].at[n, m])
        for n in range(4) for m in range(2)
    ]
    for copy in copies:
        copy.start()
    for copy in copies:
        copy.wait()


def multiply(z, lists, lefts, gathered, left, right, total, work, sem, begin):
    pairs = z.half * z.block_cols
    pieces, at = [], 0
    for part in lefts:
        pieces.append((part, 0, left, at, part.shape[0]))
        at += part.shape[0]
    for n in range(4 * z.blocks):
        pieces.append((gathered, n * CAP1, right, n * CAP1, CAP1))

    def each_copy(act):
        for n, (source, start, target, at, room) in enumerate(pieces):
            size = lists[pairs + 1, n]

            @pl.loop(0, jnp.minimum((size + CHUNK - 1) // CHUNK, room // CHUNK))
            def _(t, n=n, source=source, start=start, target=target, at=at):
                act(pltpu.make_async_copy(source.at[pl.ds(start + t * CHUNK, CHUNK)], target.at[pl.ds(at + t * CHUNK, CHUNK)], sem.at[n]))

    each_copy(lambda copy: copy.start())
    left[left.shape[0] - 1] = jnp.zeros((TILE, TILE), left.dtype)
    right[right.shape[0] - 1] = jnp.zeros((TILE, TILE), right.dtype)

    def flatten(n, at):
        def one_group(g, at):
            work[at] = n * 32 + g
            return at + 1

        return lax.fori_loop(0, (lists[n, TILE - 1] + GROUP - 1) // GROUP, one_group, at)

    found = lax.fori_loop(0, pairs, flatten, jnp.int32(0))
    for extra in range(TOGETHER):
        work[found + extra] = pairs * 32
    begin()
    each_copy(lambda copy: copy.wait())

    @pl.loop(0, (found + TOGETHER - 1) // TOGETHER)
    def _(t):
        for m in range(TOGETHER):
            item = work[t * TOGETHER + m]
            n = item // 32
            entries = [lists[n, (item % 32) * GROUP + u] for u in range(GROUP)]
            lhs = jnp.concatenate([left[e // RIGHT_BITS] for e in entries], axis=1)
            rhs = jnp.concatenate([right[e % RIGHT_BITS] for e in entries], axis=0)
            total[n] += jnp.dot(lhs, rhs, preferred_element_type=jnp.float32)


def early_kernel(z, n_left, lists, gathered, *refs):
    lefts, total = refs[:n_left], refs[n_left]
    left, right, work, sem = refs[n_left + 1:]

    def begin():
        @pl.loop(0, total.shape[0])
        def _(n):
            total[n] = jnp.zeros((TILE, TILE), jnp.float32)

    multiply(z, lists, lefts, gathered, left, right, total, work, sem, begin)


def late_kernel(z, n_left, lists, before, _, gathered, *refs):
    lefts, (mine, other, totals) = refs[:n_left], refs[n_left:n_left + 3]
    left, right, total, sums, work, sem, out_sem = refs[n_left + 3:]
    l = lax.axis_index("layer")
    width = z.block_cols * TILE // 2
    per_core = z.block_cols // 2
    load = pltpu.make_async_copy(before, total, out_sem.at[0])
    load.start()
    sums[...] = jnp.zeros_like(sums)
    multiply(z, lists, lefts, gathered, left, right, total, work, sem, load.wait)

    @pl.loop(0, z.half)
    def _(s):
        for j in range(z.block_cols):
            n = s * z.block_cols + j
            value = total[n]
            kept = value * value
            total[n] = kept
            sums[:, j * TILE:(j + 1) * TILE] += jnp.sum(kept.reshape(TILE // 8, 8, TILE), axis=0)
        n = s * z.block_cols
        near = pl.ds(n + l * per_core, per_core)
        far = pl.ds(n + (1 - l) * per_core, per_core)
        rows = pl.ds(s * per_core, per_core)
        pltpu.make_async_copy(total.at[near], mine.at[rows], out_sem.at[0]).start()
        pltpu.make_async_copy(total.at[far], other.at[rows], out_sem.at[1]).start()

    whole = jnp.sum(sums[...], axis=0, keepdims=True)
    near, far = whole[:, :width], whole[:, width:]
    totals[0:1, :] = jnp.where(l == 0, near, far)
    totals[1:2, :] = jnp.where(l == 0, far, near)
    pltpu.make_async_copy(mine, mine, out_sem.at[0]).wait()
    pltpu.make_async_copy(other, other, out_sem.at[1]).wait()


def scale_kernel(z, order, places, mine, other, totals, received, out):
    r, c, l = position()
    factor = order / (totals[0:1, :] + received[...])
    per_core = z.block_cols // 2

    @pl.loop(0, z.block_rows)
    def _(i):
        place = places[0, r * z.block_rows + i]
        core = place // z.half
        first = (place % z.half) * per_core
        target = pl.ds(pl.multiple_of(i * TILE, TILE), TILE)

        def scaled(source):
            for j in range(per_core):
                columns = slice(j * TILE, (j + 1) * TILE)
                out[target, columns] = source[first + j] * factor[:, columns]

        pl.when(core == l)(lambda: scaled(mine))
        pl.when(core != l)(lambda: scaled(other))


def turn(axis, distance, flip=True):
    pairs = []
    for place in range(SIDE * SIDE):
        for core in range(2):
            at = [place // SIDE, place % SIDE]
            at[axis] = (at[axis] + distance * (1 - 2 * core)) % SIDE
            pairs.append((place * 2 + core, (at[0] * SIDE + at[1]) * 2 + core))
    return pairs


def sparse(z, markov, pattern, keep):
    tile = lambda n: jax.ShapeDtypeStruct((n, TILE, TILE), markov.dtype)
    move = lambda x, axis, distance: lax.ppermute(x, ("col", "layer"), turn(axis, distance))
    width = z.block_cols * TILE // 2
    plan, places, first, second, both = pl.pallas_call(
        functools.partial(pack_kernel, z),
        out_shape=[
            jax.ShapeDtypeStruct((z.tiles + 8, TILE), jnp.int32),
            jax.ShapeDtypeStruct((8, TILE), jnp.int32),
            tile(CAP1),
            tile(CAP1),
            tile(2 * CAP1),
        ],
        in_specs=[VMEM, HBM],
        out_specs=[VMEM] * 5,
        scratch_shapes=[
            pltpu.VMEM(markov.shape, markov.dtype),
            pltpu.SMEM((z.tiles + 8, TILE), jnp.int32),
            pltpu.SMEM((z.block_rows,), jnp.int32),
            pltpu.SMEM((2, z.block_rows * z.block_cols), jnp.int32),
            pltpu.SemaphoreType.DMA((2,)),
        ],
        compiler_params=pltpu.CompilerParams(vmem_limit_bytes=16 * MIB),
        name="pack",
    )(pattern, markov)

    sources = []
    for h, own in enumerate((first, second)):
        behind = move(own, 1 - h, 1)
        ahead = move(own, 1 - h, -1)
        sources.append([own, behind, ahead, move(behind, 1 - h, 1)])
    swap = [(0, 1), (1, 0)]
    right = lax.all_gather(both, ("row", "layer"), axis=0, tiled=True)

    sends, early, late = pl.pallas_call(
        functools.partial(tables_kernel, z),
        out_shape=[jax.ShapeDtypeStruct((8, TILE), jnp.int32), *[jax.ShapeDtypeStruct((z.half * z.block_cols + 8, TILE), jnp.int32)] * 2],
        in_specs=[VMEM, VMEM, VMEM, HBM],
        out_specs=[VMEM] * 3,
        compiler_params=pltpu.CompilerParams(vmem_limit_bytes=8 * MIB),
        name="tables",
    )(plan, pattern, keep, first)
    flag = pl.pallas_call(
        functools.partial(check_kernel, z),
        out_shape=jax.ShapeDtypeStruct((1, 1), jnp.int32),
        in_specs=[VMEM, VMEM, HBM],
        out_specs=VMEM,
        compiler_params=pltpu.CompilerParams(vmem_limit_bytes=8 * MIB),
        name="check",
    )(pattern, keep, first)
    outs = pl.pallas_call(
        second_kernel,
        out_shape=[tile(CAPM)] * 4,
        in_specs=[HBM] * 10,
        out_specs=[VMEM] * 4,
        scratch_shapes=[
            pltpu.VMEM((2 * SIDE * CAP1, TILE, TILE), markov.dtype),
            pltpu.SMEM((8, TILE), jnp.int32),
            pltpu.SemaphoreType.DMA((8,)),
            pltpu.SemaphoreType.DMA,
        ],
        compiler_params=pltpu.CompilerParams(vmem_limit_bytes=20 * MIB),
        name="second",
    )(sends, flag, *sources[0], *sources[1])
    ahead = [move(outs[2 * h], h, 1) for h in range(2)]
    behind = [move(outs[2 * h + 1], h, -1) for h in range(2)]
    far = pl.pallas_call(
        front_kernel,
        out_shape=[tile(CAPF)] * 4,
        in_specs=[HBM] * 4,
        out_specs=[HBM] * 4,
        scratch_shapes=[pltpu.SemaphoreType.DMA((4, 2))],
        compiler_params=pltpu.CompilerParams(vmem_limit_bytes=4 * MIB),
        name="front",
    )(ahead[0], behind[0], ahead[1], behind[1])
    far = [move(part, n // 2, 1 - 2 * (n % 2)) for n, part in enumerate(far)]
    lefts = []
    for h in range(2):
        lefts += sources[h] + [ahead[h], behind[h]]

    pairs = z.half * z.block_cols
    room = lambda parts: pltpu.VMEM((sum(x.shape[0] for x in parts) + 1, TILE, TILE), markov.dtype)
    work = pltpu.SMEM((pairs * 32 + TOGETHER,), jnp.int32)
    sems = lambda parts: pltpu.SemaphoreType.DMA((len(parts) + 4 * z.blocks,))
    total = jax.ShapeDtypeStruct((pairs + 1, TILE, TILE), jnp.float32)
    before = pl.pallas_call(
        functools.partial(early_kernel, z, len(lefts)),
        out_shape=total,
        in_specs=[SMEM] + [HBM] * (len(lefts) + 1),
        out_specs=VMEM,
        scratch_shapes=[room(lefts), room([right]), work, sems(lefts)],
        compiler_params=pltpu.CompilerParams(vmem_limit_bytes=EARLY_LIMIT * MIB),
        cost_estimate=pl.CostEstimate(flops=20 * 10**9, bytes_accessed=30 * 10**6, transcendentals=0),
        name="early",
    )(early, right, *lefts)
    mine, other, totals = pl.pallas_call(
        functools.partial(late_kernel, z, len(far)),
        out_shape=[
            jax.ShapeDtypeStruct((pairs // 2, TILE, TILE), jnp.float32),
            jax.ShapeDtypeStruct((pairs // 2, TILE, TILE), jnp.float32),
            jax.ShapeDtypeStruct((2, width), jnp.float32),
        ],
        in_specs=[SMEM] + [HBM] * (3 + len(far)),
        out_specs=[HBM, HBM, VMEM],
        scratch_shapes=[
            room(far),
            room([right]),
            pltpu.VMEM(total.shape, total.dtype),
            pltpu.VMEM((8, 2 * width), jnp.float32),
            work,
            sems(far),
            pltpu.SemaphoreType.DMA((2,)),
        ],
        compiler_params=pltpu.CompilerParams(vmem_limit_bytes=LATE_LIMIT * MIB),
        name="late",
    )(late, before, flag, right, *far)
    received = lax.ppermute(other, "layer", swap)
    summed = totals
    for d in range(1, z.blocks):
        summed = summed + lax.ppermute(totals, "row", [(n, (n + d) % z.blocks) for n in range(z.blocks)])
    out = pl.pallas_call(
        functools.partial(scale_kernel, z, float(z.tiles * TILE)),
        out_shape=jax.ShapeDtypeStruct((markov.shape[0], width), jnp.float32),
        in_specs=[SMEM] + [VMEM] * 4,
        out_specs=VMEM,
        compiler_params=pltpu.CompilerParams(vmem_limit_bytes=60 * MIB),
        name="scale",
    )(places, mine, received, summed, lax.ppermute(summed[1:2], "layer", swap))
    return out, flag


def tile_scale(z, block, tiles, rows, cols):
    shaped = block.reshape(rows, TILE, cols, TILE)
    return (shaped * tiles.astype(block.dtype)[:, None, :, None]).reshape(block.shape)


def dense(z, markov, pattern, keep):
    straight = Layout(major_to_minor=(0, 1))
    markov, pattern, keep = [with_layout_constraint(x, straight) for x in (markov, pattern, keep)]
    r, c, l = position()
    rows, cols = markov.shape
    width = cols // 2
    swap = [(0, 1), (1, 0)]
    places = SIDE * SIDE
    cut = lambda x: lax.dynamic_slice(x, (r * z.block_rows, c * z.block_cols), (z.block_rows, z.block_cols))
    around = lambda x, d: lax.ppermute(x, "row", [(n, (n + d) % z.blocks) for n in range(z.blocks)])
    live = tile_scale(z, markov, cut(pattern), z.block_rows, z.block_cols)
    left = lax.dynamic_index_in_dim(live.reshape(rows, 2, width), l, 1, keepdims=False)
    right = jnp.zeros((z.blocks, rows, cols), live.dtype)
    for d in range(z.blocks):
        part = around(live, d) if d else live
        right = lax.dynamic_update_slice(right, part[None], (lax.rem(r - d + z.blocks, z.blocks), 0, 0))
    right = lax.dynamic_index_in_dim(right.reshape(places, 2, width, cols), l, 1, keepdims=False)

    def step(t, state):
        total, left = state
        block = lax.dynamic_index_in_dim(right, lax.rem(c - t + places, places), 0, keepdims=False)
        total = total + jnp.dot(left, block, preferred_element_type=jnp.float32)
        return total, lax.ppermute(left, "col", [(n, (n + 1) % places) for n in range(places)])

    square, _ = lax.fori_loop(0, places, step, (jnp.zeros((rows, cols), jnp.float32), left))
    square = square + lax.ppermute(square, "layer", swap)
    kept = tile_scale(z, square * square, cut(keep), z.block_rows, z.block_cols)
    totals = jnp.sum(kept, axis=0)
    totals = totals + sum(around(totals, d) for d in range(1, z.blocks))
    scaled = (z.tiles * TILE) * kept / totals[None, :]
    return with_layout_constraint(lax.dynamic_slice_in_dim(scaled, l * width, width, 1), straight)


def shards(markov, pattern, keep):
    z = Sizes(*markov.shape, pattern.shape[0])
    out, over = sparse(z, markov, pattern, keep)
    _, out = lax.while_loop(
        lambda state: state[0][0, 0] > 0,
        lambda state: (jnp.zeros_like(state[0]), dense(z, markov, pattern, keep)),
        (over, out),
    )
    return out


def solution(mesh):
    in_specs = (P("row", "col"), P(), P())
    out_specs = P("row", ("col", "layer"))
    return jax.shard_map(shards, mesh=mesh, in_specs=in_specs, out_specs=out_specs, check_vma=False)
```

```python
import functools

import jax
import jax.numpy as jnp
from jax import lax
from jax.experimental import pallas as pl
from jax.experimental.layout import Layout, with_layout_constraint
from jax.experimental.pallas import tpu as pltpu
from jax.sharding import PartitionSpec as P

TILE = 128
SIDE = 4
GROUP = 4
TOGETHER = 4
CAP1 = 20
CAP2 = 40
CAPM = 48
HALF2 = CAP2 // 2
CHUNK = 4
EARLY_LIMIT = 60
LATE_LIMIT = 60
RIGHT_BITS = 4096
PLACE = 16
MIB = 1024 * 1024

SMEM = pl.BlockSpec(memory_space=pltpu.SMEM)
VMEM = pl.BlockSpec(memory_space=pltpu.VMEM)
HBM = pl.BlockSpec(memory_space=pltpu.HBM)


def position():
    return lax.axis_index("row"), lax.axis_index("col"), lax.axis_index("layer")


def dot(a, b):
    return jnp.dot(a.astype(jnp.bfloat16), b.astype(jnp.bfloat16), preferred_element_type=jnp.float32)


def where_in(shape):
    return lax.broadcasted_iota(jnp.int32, shape, 0), lax.broadcasted_iota(jnp.int32, shape, 1)


def ranks(block_rows, present):
    tiles = present.shape[0]
    ones = jnp.ones((8, tiles), jnp.bfloat16)
    level_row = lax.dot_general(ones, present.astype(jnp.bfloat16), (((1,), (1,)), ((), ())), preferred_element_type=jnp.float32)[:1]
    level_col = jnp.sum(present, axis=1, keepdims=True)
    a, b = where_in((tiles, tiles))
    same = jnp.where(a // block_rows == b // block_rows, 1.0, 0.0)
    above = jnp.where(level_col > level_row, 1.0, 0.0) + jnp.where(level_col == level_row, jnp.where(a < b, 1.0, 0.0), 0.0)
    below = jnp.where(level_col < level_row, 1.0, 0.0) + jnp.where(level_col == level_row, jnp.where(a > b, 1.0, 0.0), 0.0)
    return (
        jnp.sum(above * same, axis=0, keepdims=True).astype(jnp.int32),
        jnp.sum(below * same, axis=1, keepdims=True).astype(jnp.int32),
    )


def core_slot(rank):
    return ((rank + 1) // 2) % 2, rank // 2


class Sizes:
    def __init__(self, rows_dev, cols_dev, tiles):
        self.block_rows = rows_dev // TILE
        self.block_cols = cols_dev // TILE
        self.half = self.block_rows // 2
        self.tiles = tiles
        self.blocks = tiles // self.block_rows


def check_kernel(z, pattern_ref, keep_ref, _, flag_ref):
    groups = 2 * z.blocks
    present = pattern_ref[...].astype(jnp.float32)
    keep = keep_ref[...].astype(jnp.float32)
    rank, _ = ranks(z.block_rows, present)
    core, slot = core_slot(rank)
    owner, row = where_in((2 * groups, z.tiles))
    member = jnp.where(owner % groups == (row // z.block_rows) * 2 + core, 1.0, 0.0)
    member = member * jnp.where(owner // groups == slot % 2, 1.0, 0.0)
    i, k = where_in((2 * groups, z.tiles))
    odd = (i // groups + k) % 2
    i, k = where_in((z.tiles, TILE))
    per_block = jnp.where(i // z.block_cols == k, 1.0, 0.0)
    per_outer = [
        jnp.where(i // (z.block_cols * SIDE) == k, 1.0, 0.0),
        jnp.where((i // z.block_cols) % SIDE == k, 1.0, 0.0),
    ]
    by_k = dot(member, present)
    over = jnp.zeros((1, 1), jnp.int32)
    for h in range(2):
        counts = dot(jnp.where(odd == h, by_k, 0.0), per_block)
        most = jnp.max(counts[:groups] + counts[groups:], keepdims=True)
        over = over + jnp.where(most > CAP1, 1, 0)
    present_t = present.T
    column = where_in((z.tiles, z.tiles))[1]
    lane = where_in((groups, TILE))[1]
    needs = []
    for c in range(SIDE * SIDE):
        used = dot(jnp.where(column // z.block_cols == c, keep, 0.0), present_t)
        needs.append(jnp.where(used > 0, present, 0.0))
    cores = where_in((groups, TILE))[0] % 2
    for c in range(SIDE * SIDE):
        for h in range(2):
            outer, inner = axes_of(h, c)
            up, far, down = [needs[block_at(h, (outer + d) % SIDE, inner)] for d in (1, 2, 3)]
            far_up, far_down = jnp.maximum(far, up), jnp.maximum(far, down)
            for mask, most, core in ((far, CAP2, None), (up, CAP2, 1), (down, CAP2, 0), (far_up, CAPM, 0), (far_down, CAPM, 1)):
                counts = dot(jnp.where(odd == h, dot(member, mask), 0.0), per_outer[h])
                counts = counts[:groups] + counts[groups:]
                counted = jnp.where(lane == outer, counts, 0.0)
                if core is not None:
                    counted = jnp.where(cores == core, counted, 0.0)
                over = over + jnp.where(jnp.max(counted, keepdims=True) > most, 1, 0)
    flag_ref[...] = jnp.minimum(over, 1)


def axes_of(h, c):
    return (c // SIDE, c % SIDE) if h == 0 else (c % SIDE, c // SIDE)


def block_at(h, outer, inner):
    return outer * SIDE + inner if h == 0 else inner * SIDE + outer


def pack_kernel(z, pattern_ref, markov, plan_ref, places, first, second, both, held, plan, inverse, entries, sem):
    r, c, l = position()
    load = pltpu.make_async_copy(markov, held, sem.at[0])
    load.start()
    present = pattern_ref[...].astype(jnp.float32)
    i, k = where_in((z.tiles, TILE))
    weights = jnp.where(i // z.block_cols == k, jnp.left_shift(1, i % z.block_cols), 0)
    bits = dot(present, weights).astype(jnp.int32)
    rank_row, rank_col = ranks(z.block_rows, present)
    core, slot = core_slot(rank_row)
    plan_ref[...] = jnp.zeros_like(plan_ref)
    plan_ref[z.tiles:z.tiles + 1, 0:z.tiles] = core * z.half + slot
    core, slot = core_slot(rank_col)
    plan_ref[0:z.tiles, :] = jnp.where(k == PLACE, core * z.half + slot, bits)
    places[...] = plan_ref[z.tiles:z.tiles + 8, :]
    known = pltpu.make_async_copy(plan_ref, plan, sem.at[1])
    known.start()
    known.wait()

    @pl.loop(0, z.block_rows)
    def _(i):
        inverse[plan[z.tiles, r * z.block_rows + i]] = i

    def pair(t, counts):
        counts = list(counts)
        for odd in range(2):
            i = inverse[l * z.half + 2 * t + odd]
            mask = plan[r * z.block_rows + i, c]
            for j in range(z.block_cols):
                h = (odd + j) % 2
                entries[h, counts[h]] = i * 8 + j
                counts[h] = counts[h] + ((mask >> j) & 1)
        return tuple(counts)

    counts = lax.fori_loop(0, z.half // 2, pair, (jnp.int32(0), jnp.int32(0)))
    load.wait()
    for h, out in enumerate((first, second)):
        @pl.loop(0, jnp.minimum(counts[h], CAP1))
        def _(n, h=h, out=out):
            entry = entries[h, n]
            i = pl.multiple_of((entry // 8) * TILE, TILE)
            j = pl.multiple_of((entry % 8) * TILE, TILE)
            tile = held[pl.ds(i, TILE), pl.ds(j, TILE)]
            out[n] = tile
            both[h * CAP1 + n] = tile


def turned(distance, sign):
    d = lax.rem(distance * sign + 2 * SIDE, SIDE)
    return jnp.where(d == 0, 0, jnp.where(d == 3, 1, jnp.where(d == 1, 2, 3)))


def tables_kernel(z, plan, pattern_ref, keep_ref, _, sends, early, late):
    r, c, l = position()
    cz, cy = c // SIDE, c % SIDE
    sign = 1 - 2 * l
    present = pattern_ref[...].astype(jnp.float32)
    keep = keep_ref[...].astype(jnp.float32)
    one = lambda x: jnp.where(x, 1.0, 0.0)

    place = plan[0:z.tiles, PLACE:PLACE + 1]
    place_row = plan[z.tiles:z.tiles + 1, 0:z.tiles]
    k, s = where_in((z.tiles, TILE))
    mine = one((place == l * z.half + s) & (s < z.half) & (k // z.block_rows == r))
    has = dot(present.T, mine)
    kept = dot(keep.T, mine)

    a, b = where_in((z.tiles, z.tiles))
    block_a, block_b = a // z.block_cols, b // z.block_cols
    below = one(b < a)
    u, v = where_in((TILE, TILE))
    earlier = one(u < v)

    def placed(mask, group):
        return dot(group * below, mask) + dot(dot(group, mask), earlier)

    def needed(there):
        return one(dot(jnp.where(block_b == there, present, 0.0), kept) > 0) * has

    halves = [one((k + s) % 2 == h) for h in range(2)]
    block = k // z.block_cols
    outers = [block // SIDE, block % SIDE]
    groups = [one(block_a // SIDE == block_b // SIDE), one(block_a % SIDE == block_b % SIDE)]
    me = [cz, cy]
    same_block = one(block_a == block_b)
    within = sum(halves[h] * placed(has * halves[h], same_block) for h in range(2))
    lane = where_in((1, TILE))[1]
    place_left = jnp.zeros((z.tiles, TILE), jnp.float32)
    stride = SIDE * CAP1 + CAPM + CAP2
    sizes = jnp.zeros((1, TILE), jnp.float32)
    late_sizes = jnp.zeros((1, TILE), jnp.float32)
    is_late = jnp.zeros((z.tiles, TILE), jnp.float32)
    everyone = jnp.ones((TILE, TILE), jnp.float32)

    def compact(mask, position, value, columns, empty):
        where = jnp.where(mask > 0, position, -1.0).astype(jnp.int32)
        value = value.astype(jnp.int32) - empty
        row = jnp.zeros((1, TILE), jnp.int32)
        for n in columns:
            hit = where[:, n:n + 1] == where_in((z.tiles, TILE))[1]
            row = row + jnp.sum(jnp.where(hit, value[:, n:n + 1], 0), axis=0, keepdims=True)
        return row + empty

    def total(mask):
        return jnp.sum(jnp.sum(mask, axis=0, keepdims=True), axis=1, keepdims=True).astype(jnp.int32)

    def tally_halves(mask, part):
        count = total(mask).astype(jnp.float32)
        low = jnp.minimum(count, HALF2)
        return jnp.where(lane == part, low, jnp.where(lane == part + 1, count - low, 0.0))

    def tally(mask, part):
        return jnp.sum(jnp.where(s == part, dot(mask, everyone), 0.0), axis=0, keepdims=True)

    for h in range(2):
        outer, inner = outers[h], outers[1 - h]
        away = lax.rem((outer - me[h]) * sign + 2 * SIDE, SIDE)
        held = turned(inner - me[1 - h], sign).astype(jnp.float32) * CAP1 + within
        wants = []
        for distance in range(SIDE):
            there = lax.rem(me[h] + distance * sign + SIDE, SIDE)
            wants.append(needed(there * SIDE + cy if h == 0 else cz * SIDE + there) * halves[h])
        next_one = sum(jnp.where(away == d, wants[(d + 1) % SIDE], 0.0) for d in range(SIDE))
        opposite = sum(jnp.where(away == d, wants[(d + 2) % SIDE], 0.0) for d in range(SIDE))
        only_far, shared, only_next = opposite * (1 - next_one), opposite * next_one, next_one * (1 - opposite)
        count = lambda mask: dot(dot(groups[h], mask), everyone)
        start_shared = count(only_far)
        start_next = start_shared + count(shared)
        reached = only_far * placed(only_far, groups[h]) + shared * (start_shared + placed(shared, groups[h]))
        reached = reached + only_next * (start_next + placed(only_next, groups[h]))
        ring = one(away == 0)
        for n, (mask, where) in enumerate((
            ((only_far + shared + only_next) * ring, reached),
            (wants[3] * ring, placed(wants[3], groups[h])),
        )):
            row = compact(mask, where, held, range(z.half), 0)
            most = (CAPM, CAP2)[n]
            sends[h * 2 + n:h * 2 + n + 1, :] = jnp.where(lane == TILE - 1, jnp.minimum(total(mask), most), row)
        arrived = jnp.where(away == 3, reached, CAPM + placed(wants[0], groups[h]))
        early_place = h * stride + jnp.where(away == 0, held, SIDE * CAP1 + arrived)
        place_left = place_left + halves[h] * jnp.where(away == 2, h * CAP2 + reached, early_place)
        is_late = is_late + halves[h] * one(away == 2)
        sizes = sizes + tally(has * halves[h] * ring, h * 6 + turned(inner - me[1 - h], sign))
        sizes = sizes + tally((shared + only_far + only_next) * one(away == 3), h * 6 + 4)
        sizes = sizes + tally(wants[0] * one(away == 1), h * 6 + 5)
        late_sizes = late_sizes + tally_halves(opposite * one(away == 2), h * 2)

    core = place // z.half
    slot = place % z.half
    core_row = place_row // z.half
    slot_row = place_row % z.half
    ahead = one((a // z.block_rows == b // z.block_rows) & (core == core_row) & (slot_row < slot))
    column = dot(present, one((k == c * z.block_cols + s) & (s < z.block_cols)))
    place_right = jnp.zeros((z.tiles, TILE), jnp.float32)
    for h in range(2):
        half = one((slot + s) % 2 == h)
        mask = column * half
        right_part = ((k // z.block_rows) * 2 + core) * 2 + h
        sizes = sizes + tally(mask, 12 + right_part)
        late_sizes = late_sizes + tally(mask, 4 + right_part)
        place_right = place_right + half * (h * CAP1 + dot(mask, earlier) + dot(dot(ahead, mask), everyone))
    place_right = place_right + ((right_part // 2) * (2 * CAP1)).astype(jnp.float32)

    pairs = z.half * z.block_cols
    to_slot = one((u == v // z.block_cols) & (v < pairs))
    to_column = one((u == v % z.block_cols) & (v < pairs))
    kept_here = dot(kept, to_slot) * one((k == c * z.block_cols + s % z.block_cols) & (s < pairs))
    mask = dot(has, to_slot) * dot(column, to_column) * jnp.sum(kept_here, axis=0, keepdims=True)
    is_late = dot(is_late, to_slot)

    def spread(x, to):
        x = x.astype(jnp.int32)
        return dot(x // 64, to) * 64 + dot(x % 64, to)

    value = spread(place_left, to_slot) * RIGHT_BITS + spread(place_right, to_column)
    for lists, mask, parts, n_left in ((early, mask * (1 - is_late), sizes, 2 * stride), (late, mask * is_late, late_sizes, 2 * CAP2)):
        empty = n_left * RIGHT_BITS + 4 * z.blocks * CAP1
        where = dot(below, mask)
        count = jnp.sum(mask, axis=0, keepdims=True).astype(jnp.int32)
        for n in range(pairs):
            row = compact(mask, where, value, (n,), empty)
            lists[n:n + 1, :] = jnp.where(lane == TILE - 1, count[:, n:n + 1], row)
        lists[pairs:pairs + 1, :] = jnp.full((1, TILE), empty, jnp.int32)
        lists[pairs + 1:pairs + 2, :] = parts.astype(jnp.int32)


def load_all(parts, held, sem):
    copies, at = [], 0
    for n, part in enumerate(parts):
        part, start, size = part if isinstance(part, tuple) else (part, 0, part.shape[0])
        copies.append(pltpu.make_async_copy(part.at[pl.ds(start, size)], held.at[pl.ds(at, size)], sem.at[n]))
        copies[-1].start()
        at += size
    return copies


def second_kernel(sends_ref, *refs):
    sources, outs, (held, sends, sem, known) = refs[:8], refs[8:12], refs[12:]
    told = pltpu.make_async_copy(sends_ref, sends, known)
    told.start()
    copies = load_all(sources, held, sem)
    told.wait()
    for copy in copies:
        copy.wait()
    for h in range(2):
        ahead, behind = outs[2 * h:2 * h + 2]
        for n, out in enumerate((ahead, behind)):
            @pl.loop(0, sends[2 * h + n, TILE - 1])
            def _(t, n=2 * h + n, out=out, base=h * SIDE * CAP1):
                out[t] = held[base + sends[n, t]]


def front_kernel(*refs):
    piece = HALF2 // 2
    copies = [
        pltpu.make_async_copy(refs[n // 2].at[pl.ds(n % 2 * HALF2 + m * piece, piece)], refs[2 + n].at[pl.ds(m * piece, piece)], refs[6].at[n, m])
        for n in range(4) for m in range(2)
    ]
    for copy in copies:
        copy.start()
    for copy in copies:
        copy.wait()


def multiply(z, lists, lefts, gathered, left, right, total, work, sem, begin):
    pairs = z.half * z.block_cols
    pieces, at = [], 0
    for part in lefts:
        pieces.append((part, 0, left, at, part.shape[0]))
        at += part.shape[0]
    for n in range(4 * z.blocks):
        pieces.append((gathered, n * CAP1, right, n * CAP1, CAP1))

    def each_copy(act):
        for n, (source, start, target, at, room) in enumerate(pieces):
            size = lists[pairs + 1, n]

            @pl.loop(0, jnp.minimum((size + CHUNK - 1) // CHUNK, room // CHUNK))
            def _(t, n=n, source=source, start=start, target=target, at=at):
                act(pltpu.make_async_copy(source.at[pl.ds(start + t * CHUNK, CHUNK)], target.at[pl.ds(at + t * CHUNK, CHUNK)], sem.at[n]))

    each_copy(lambda copy: copy.start())
    left[left.shape[0] - 1] = jnp.zeros((TILE, TILE), left.dtype)
    right[right.shape[0] - 1] = jnp.zeros((TILE, TILE), right.dtype)

    def flatten(n, at):
        def one_group(g, at):
            work[at] = n * 32 + g
            return at + 1

        return lax.fori_loop(0, (lists[n, TILE - 1] + GROUP - 1) // GROUP, one_group, at)

    found = lax.fori_loop(0, pairs, flatten, jnp.int32(0))
    for extra in range(TOGETHER):
        work[found + extra] = pairs * 32
    begin()
    each_copy(lambda copy: copy.wait())

    @pl.loop(0, (found + TOGETHER - 1) // TOGETHER)
    def _(t):
        for m in range(TOGETHER):
            item = work[t * TOGETHER + m]
            n = item // 32
            entries = [lists[n, (item % 32) * GROUP + u] for u in range(GROUP)]
            lhs = jnp.concatenate([left[e // RIGHT_BITS] for e in entries], axis=1)
            rhs = jnp.concatenate([right[e % RIGHT_BITS] for e in entries], axis=0)
            total[n] += jnp.dot(lhs, rhs, preferred_element_type=jnp.float32)


def early_kernel(z, n_left, lists, gathered, *refs):
    lefts, total = refs[:n_left], refs[n_left]
    left, right, work, sem = refs[n_left + 1:]

    def begin():
        @pl.loop(0, total.shape[0])
        def _(n):
            total[n] = jnp.zeros((TILE, TILE), jnp.float32)

    multiply(z, lists, lefts, gathered, left, right, total, work, sem, begin)


def late_kernel(z, n_left, lists, before, _, gathered, *refs):
    lefts, (mine, other, totals) = refs[:n_left], refs[n_left:n_left + 3]
    left, right, total, sums, work, sem, out_sem = refs[n_left + 3:]
    l = lax.axis_index("layer")
    width = z.block_cols * TILE // 2
    per_core = z.block_cols // 2
    load = pltpu.make_async_copy(before, total, out_sem.at[0])
    load.start()
    sums[...] = jnp.zeros_like(sums)
    multiply(z, lists, lefts, gathered, left, right, total, work, sem, load.wait)

    @pl.loop(0, z.half)
    def _(s):
        for j in range(z.block_cols):
            n = s * z.block_cols + j
            value = total[n]
            kept = value * value
            total[n] = kept
            sums[:, j * TILE:(j + 1) * TILE] += jnp.sum(kept.reshape(TILE // 8, 8, TILE), axis=0)
        n = s * z.block_cols
        near = pl.ds(n + l * per_core, per_core)
        far = pl.ds(n + (1 - l) * per_core, per_core)
        rows = pl.ds(s * per_core, per_core)
        pltpu.make_async_copy(total.at[near], mine.at[rows], out_sem.at[0]).start()
        pltpu.make_async_copy(total.at[far], other.at[rows], out_sem.at[1]).start()

    whole = jnp.sum(sums[...], axis=0, keepdims=True)
    near, far = whole[:, :width], whole[:, width:]
    totals[0:1, :] = jnp.where(l == 0, near, far)
    totals[1:2, :] = jnp.where(l == 0, far, near)
    pltpu.make_async_copy(mine, mine, out_sem.at[0]).wait()
    pltpu.make_async_copy(other, other, out_sem.at[1]).wait()


def scale_kernel(z, order, places, mine, other, totals, received, out):
    r, c, l = position()
    factor = order / (totals[0:1, :] + received[...])
    per_core = z.block_cols // 2

    @pl.loop(0, z.block_rows)
    def _(i):
        place = places[0, r * z.block_rows + i]
        core = place // z.half
        first = (place % z.half) * per_core
        target = pl.ds(pl.multiple_of(i * TILE, TILE), TILE)

        def scaled(source):
            for j in range(per_core):
                columns = slice(j * TILE, (j + 1) * TILE)
                out[target, columns] = source[first + j] * factor[:, columns]

        pl.when(core == l)(lambda: scaled(mine))
        pl.when(core != l)(lambda: scaled(other))


def turn(axis, distance, flip=True):
    pairs = []
    for place in range(SIDE * SIDE):
        for core in range(2):
            at = [place // SIDE, place % SIDE]
            at[axis] = (at[axis] + distance * (1 - 2 * core)) % SIDE
            pairs.append((place * 2 + core, (at[0] * SIDE + at[1]) * 2 + core))
    return pairs


def sparse(z, markov, pattern, keep):
    tile = lambda n: jax.ShapeDtypeStruct((n, TILE, TILE), markov.dtype)
    move = lambda x, axis, distance: lax.ppermute(x, ("col", "layer"), turn(axis, distance))
    width = z.block_cols * TILE // 2
    plan, places, first, second, both = pl.pallas_call(
        functools.partial(pack_kernel, z),
        out_shape=[
            jax.ShapeDtypeStruct((z.tiles + 8, TILE), jnp.int32),
            jax.ShapeDtypeStruct((8, TILE), jnp.int32),
            tile(CAP1),
            tile(CAP1),
            tile(2 * CAP1),
        ],
        in_specs=[VMEM, HBM],
        out_specs=[VMEM] * 5,
        scratch_shapes=[
            pltpu.VMEM(markov.shape, markov.dtype),
            pltpu.SMEM((z.tiles + 8, TILE), jnp.int32),
            pltpu.SMEM((z.block_rows,), jnp.int32),
            pltpu.SMEM((2, z.block_rows * z.block_cols), jnp.int32),
            pltpu.SemaphoreType.DMA((2,)),
        ],
        compiler_params=pltpu.CompilerParams(vmem_limit_bytes=16 * MIB),
        name="pack",
    )(pattern, markov)

    sources = []
    for h, own in enumerate((first, second)):
        behind = move(own, 1 - h, 1)
        ahead = move(own, 1 - h, -1)
        sources.append([own, behind, ahead, move(behind, 1 - h, 1)])
    swap = [(0, 1), (1, 0)]
    after = lambda x, *others: lax.optimization_barrier((x, *others))[0]
    right = lax.all_gather(both, ("row", "layer"), axis=0, tiled=True)

    sends, early, late = pl.pallas_call(
        functools.partial(tables_kernel, z),
        out_shape=[jax.ShapeDtypeStruct((8, TILE), jnp.int32), *[jax.ShapeDtypeStruct((z.half * z.block_cols + 8, TILE), jnp.int32)] * 2],
        in_specs=[VMEM, VMEM, VMEM, HBM],
        out_specs=[VMEM] * 3,
        compiler_params=pltpu.CompilerParams(vmem_limit_bytes=8 * MIB),
        name="tables",
    )(plan, pattern, keep, first)
    outs = pl.pallas_call(
        second_kernel,
        out_shape=[tile(CAPM), tile(CAP2)] * 2,
        in_specs=[HBM] * 9,
        out_specs=[VMEM] * 4,
        scratch_shapes=[
            pltpu.VMEM((2 * SIDE * CAP1, TILE, TILE), markov.dtype),
            pltpu.SMEM((8, TILE), jnp.int32),
            pltpu.SemaphoreType.DMA((8,)),
            pltpu.SemaphoreType.DMA,
        ],
        compiler_params=pltpu.CompilerParams(vmem_limit_bytes=20 * MIB),
        name="second",
    )(sends, *sources[0], *sources[1])
    ahead = [move(outs[2 * h], h, 1) for h in range(2)]
    flag = pl.pallas_call(
        functools.partial(check_kernel, z),
        out_shape=jax.ShapeDtypeStruct((1, 1), jnp.int32),
        in_specs=[VMEM, VMEM, HBM],
        out_specs=VMEM,
        compiler_params=pltpu.CompilerParams(vmem_limit_bytes=8 * MIB),
        name="check",
    )(pattern, keep, outs[0])
    behind = [move(after(outs[2 * h + 1], flag), h, -1) for h in range(2)]
    far = pl.pallas_call(
        front_kernel,
        out_shape=[tile(HALF2)] * 4,
        in_specs=[HBM] * 2,
        out_specs=[HBM] * 4,
        scratch_shapes=[pltpu.SemaphoreType.DMA((4, 2))],
        compiler_params=pltpu.CompilerParams(vmem_limit_bytes=4 * MIB),
        name="front",
    )(*ahead)
    far = [move(part, n // 2, 1) for n, part in enumerate(far)]
    lefts = []
    for h in range(2):
        lefts += sources[h] + [ahead[h], behind[h]]

    pairs = z.half * z.block_cols
    room = lambda parts: pltpu.VMEM((sum(x.shape[0] for x in parts) + 1, TILE, TILE), markov.dtype)
    work = pltpu.SMEM((pairs * 32 + TOGETHER,), jnp.int32)
    sems = lambda parts: pltpu.SemaphoreType.DMA((len(parts) + 4 * z.blocks,))
    total = jax.ShapeDtypeStruct((pairs + 1, TILE, TILE), jnp.float32)
    before = pl.pallas_call(
        functools.partial(early_kernel, z, len(lefts)),
        out_shape=total,
        in_specs=[SMEM] + [HBM] * (len(lefts) + 1),
        out_specs=VMEM,
        scratch_shapes=[room(lefts), room([right]), work, sems(lefts)],
        compiler_params=pltpu.CompilerParams(vmem_limit_bytes=EARLY_LIMIT * MIB),
        cost_estimate=pl.CostEstimate(flops=20 * 10**9, bytes_accessed=30 * 10**6, transcendentals=0),
        name="early",
    )(early, right, *lefts)
    mine, other, totals = pl.pallas_call(
        functools.partial(late_kernel, z, len(far)),
        out_shape=[
            jax.ShapeDtypeStruct((pairs // 2, TILE, TILE), jnp.float32),
            jax.ShapeDtypeStruct((pairs // 2, TILE, TILE), jnp.float32),
            jax.ShapeDtypeStruct((2, width), jnp.float32),
        ],
        in_specs=[SMEM] + [HBM] * (3 + len(far)),
        out_specs=[HBM, HBM, VMEM],
        scratch_shapes=[
            room(far),
            room([right]),
            pltpu.VMEM(total.shape, total.dtype),
            pltpu.VMEM((8, 2 * width), jnp.float32),
            work,
            sems(far),
            pltpu.SemaphoreType.DMA((2,)),
        ],
        compiler_params=pltpu.CompilerParams(vmem_limit_bytes=LATE_LIMIT * MIB),
        name="late",
    )(late, before, flag, right, *far)
    received = lax.ppermute(other, "layer", swap)
    summed = totals
    for d in range(1, z.blocks):
        summed = summed + lax.ppermute(totals, "row", [(n, (n + d) % z.blocks) for n in range(z.blocks)])
    out = pl.pallas_call(
        functools.partial(scale_kernel, z, float(z.tiles * TILE)),
        out_shape=jax.ShapeDtypeStruct((markov.shape[0], width), jnp.float32),
        in_specs=[SMEM] + [VMEM] * 4,
        out_specs=VMEM,
        compiler_params=pltpu.CompilerParams(vmem_limit_bytes=16 * MIB),
        name="scale",
    )(places, mine, received, summed, lax.ppermute(summed[1:2], "layer", swap))
    return out, flag


def tile_scale(z, block, tiles, rows, cols):
    shaped = block.reshape(rows, TILE, cols, TILE)
    return (shaped * tiles.astype(block.dtype)[:, None, :, None]).reshape(block.shape)


def dense(z, markov, pattern, keep):
    straight = Layout(major_to_minor=(0, 1))
    markov, pattern, keep = [with_layout_constraint(x, straight) for x in (markov, pattern, keep)]
    r, c, l = position()
    rows, cols = markov.shape
    width = cols // 2
    swap = [(0, 1), (1, 0)]
    places = SIDE * SIDE
    cut = lambda x: lax.dynamic_slice(x, (r * z.block_rows, c * z.block_cols), (z.block_rows, z.block_cols))
    around = lambda x, d: lax.ppermute(x, "row", [(n, (n + d) % z.blocks) for n in range(z.blocks)])
    live = tile_scale(z, markov, cut(pattern), z.block_rows, z.block_cols)
    left = lax.dynamic_index_in_dim(live.reshape(rows, 2, width), l, 1, keepdims=False)
    right = jnp.zeros((z.blocks, rows, cols), live.dtype)
    for d in range(z.blocks):
        part = around(live, d) if d else live
        right = lax.dynamic_update_slice(right, part[None], (lax.rem(r - d + z.blocks, z.blocks), 0, 0))
    right = lax.dynamic_index_in_dim(right.reshape(places, 2, width, cols), l, 1, keepdims=False)

    def step(t, state):
        total, left = state
        block = lax.dynamic_index_in_dim(right, lax.rem(c - t + places, places), 0, keepdims=False)
        total = total + jnp.dot(left, block, preferred_element_type=jnp.float32)
        return total, lax.ppermute(left, "col", [(n, (n + 1) % places) for n in range(places)])

    square, _ = lax.fori_loop(0, places, step, (jnp.zeros((rows, cols), jnp.float32), left))
    square = square + lax.ppermute(square, "layer", swap)
    kept = tile_scale(z, square * square, cut(keep), z.block_rows, z.block_cols)
    totals = jnp.sum(kept, axis=0)
    totals = totals + sum(around(totals, d) for d in range(1, z.blocks))
    scaled = (z.tiles * TILE) * kept / totals[None, :]
    return with_layout_constraint(lax.dynamic_slice_in_dim(scaled, l * width, width, 1), straight)


def shards(markov, pattern, keep):
    z = Sizes(*markov.shape, pattern.shape[0])
    out, over = sparse(z, markov, pattern, keep)
    _, out = lax.while_loop(
        lambda state: state[0][0, 0] > 0,
        lambda state: (jnp.zeros_like(state[0]), dense(z, markov, pattern, keep)),
        (over, out),
    )
    return out


def solution(mesh):
    in_specs = (P("row", "col"), P(), P())
    out_specs = P("row", ("col", "layer"))
    return jax.shard_map(shards, mesh=mesh, in_specs=in_specs, out_specs=out_specs, check_vma=False)
```

```python
import functools

import jax
import jax.numpy as jnp
from jax import lax
from jax.experimental import pallas as pl
from jax.experimental.layout import Layout, with_layout_constraint
from jax.experimental.pallas import tpu as pltpu
from jax.sharding import PartitionSpec as P

TILE = 128
SIDE = 4
GROUP = 4
TOGETHER = 4
CAP1 = 20
CAP2 = 40
CAPM = 48
CHUNK = 4
EARLY_LIMIT = 60
LATE_LIMIT = 60
RIGHT_BITS = 4096
PLACE = 16
MIB = 1024 * 1024

SMEM = pl.BlockSpec(memory_space=pltpu.SMEM)
VMEM = pl.BlockSpec(memory_space=pltpu.VMEM)
HBM = pl.BlockSpec(memory_space=pltpu.HBM)


def position():
    return lax.axis_index("row"), lax.axis_index("col"), lax.axis_index("layer")


def dot(a, b):
    return jnp.dot(a.astype(jnp.bfloat16), b.astype(jnp.bfloat16), preferred_element_type=jnp.float32)


def where_in(shape):
    return lax.broadcasted_iota(jnp.int32, shape, 0), lax.broadcasted_iota(jnp.int32, shape, 1)


def ranks(block_rows, present):
    tiles = present.shape[0]
    ones = jnp.ones((8, tiles), jnp.bfloat16)
    level_row = lax.dot_general(ones, present.astype(jnp.bfloat16), (((1,), (1,)), ((), ())), preferred_element_type=jnp.float32)[:1]
    level_col = jnp.sum(present, axis=1, keepdims=True)
    a, b = where_in((tiles, tiles))
    same = jnp.where(a // block_rows == b // block_rows, 1.0, 0.0)
    above = jnp.where(level_col > level_row, 1.0, 0.0) + jnp.where(level_col == level_row, jnp.where(a < b, 1.0, 0.0), 0.0)
    below = jnp.where(level_col < level_row, 1.0, 0.0) + jnp.where(level_col == level_row, jnp.where(a > b, 1.0, 0.0), 0.0)
    return (
        jnp.sum(above * same, axis=0, keepdims=True).astype(jnp.int32),
        jnp.sum(below * same, axis=1, keepdims=True).astype(jnp.int32),
    )


def core_slot(rank):
    return ((rank + 1) // 2) % 2, rank // 2


class Sizes:
    def __init__(self, rows_dev, cols_dev, tiles):
        self.block_rows = rows_dev // TILE
        self.block_cols = cols_dev // TILE
        self.half = self.block_rows // 2
        self.tiles = tiles
        self.blocks = tiles // self.block_rows


def check_kernel(z, pattern_ref, keep_ref, _, flag_ref):
    groups = 2 * z.blocks
    present = pattern_ref[...].astype(jnp.float32)
    keep = keep_ref[...].astype(jnp.float32)
    rank, _ = ranks(z.block_rows, present)
    core, slot = core_slot(rank)
    owner, row = where_in((2 * groups, z.tiles))
    member = jnp.where(owner % groups == (row // z.block_rows) * 2 + core, 1.0, 0.0)
    member = member * jnp.where(owner // groups == slot % 2, 1.0, 0.0)
    i, k = where_in((2 * groups, z.tiles))
    odd = (i // groups + k) % 2
    i, k = where_in((z.tiles, TILE))
    per_block = jnp.where(i // z.block_cols == k, 1.0, 0.0)
    per_outer = [
        jnp.where(i // (z.block_cols * SIDE) == k, 1.0, 0.0),
        jnp.where((i // z.block_cols) % SIDE == k, 1.0, 0.0),
    ]
    by_k = dot(member, present)
    over = jnp.zeros((1, 1), jnp.int32)
    for h in range(2):
        counts = dot(jnp.where(odd == h, by_k, 0.0), per_block)
        most = jnp.max(counts[:groups] + counts[groups:], keepdims=True)
        over = over + jnp.where(most > CAP1, 1, 0)
    present_t = present.T
    column = where_in((z.tiles, z.tiles))[1]
    lane = where_in((groups, TILE))[1]
    needs = []
    for c in range(SIDE * SIDE):
        used = dot(jnp.where(column // z.block_cols == c, keep, 0.0), present_t)
        needs.append(jnp.where(used > 0, present, 0.0))
    cores = where_in((groups, TILE))[0] % 2
    for c in range(SIDE * SIDE):
        for h in range(2):
            outer, inner = axes_of(h, c)
            up, far, down = [needs[block_at(h, (outer + d) % SIDE, inner)] for d in (1, 2, 3)]
            far_up, far_down = jnp.maximum(far, up), jnp.maximum(far, down)
            for mask, most, core in ((far, CAP2, None), (up, CAP2, 1), (down, CAP2, 0), (far_up, CAPM, 0), (far_down, CAPM, 1)):
                counts = dot(jnp.where(odd == h, dot(member, mask), 0.0), per_outer[h])
                counts = counts[:groups] + counts[groups:]
                counted = jnp.where(lane == outer, counts, 0.0)
                if core is not None:
                    counted = jnp.where(cores == core, counted, 0.0)
                over = over + jnp.where(jnp.max(counted, keepdims=True) > most, 1, 0)
    flag_ref[...] = jnp.minimum(over, 1)


def axes_of(h, c):
    return (c // SIDE, c % SIDE) if h == 0 else (c % SIDE, c // SIDE)


def block_at(h, outer, inner):
    return outer * SIDE + inner if h == 0 else inner * SIDE + outer


def pack_kernel(z, pattern_ref, markov, plan_ref, places, first, second, both, held, plan, inverse, entries, sem):
    r, c, l = position()
    load = pltpu.make_async_copy(markov, held, sem.at[0])
    load.start()
    present = pattern_ref[...].astype(jnp.float32)
    i, k = where_in((z.tiles, TILE))
    weights = jnp.where(i // z.block_cols == k, jnp.left_shift(1, i % z.block_cols), 0)
    bits = dot(present, weights).astype(jnp.int32)
    rank_row, rank_col = ranks(z.block_rows, present)
    core, slot = core_slot(rank_row)
    plan_ref[...] = jnp.zeros_like(plan_ref)
    plan_ref[z.tiles:z.tiles + 1, 0:z.tiles] = core * z.half + slot
    core, slot = core_slot(rank_col)
    plan_ref[0:z.tiles, :] = jnp.where(k == PLACE, core * z.half + slot, bits)
    places[...] = plan_ref[z.tiles:z.tiles + 8, :]
    known = pltpu.make_async_copy(plan_ref, plan, sem.at[1])
    known.start()
    known.wait()

    @pl.loop(0, z.block_rows)
    def _(i):
        inverse[plan[z.tiles, r * z.block_rows + i]] = i

    def pair(t, counts):
        counts = list(counts)
        for odd in range(2):
            i = inverse[l * z.half + 2 * t + odd]
            mask = plan[r * z.block_rows + i, c]
            for j in range(z.block_cols):
                h = (odd + j) % 2
                entries[h, counts[h]] = i * 8 + j
                counts[h] = counts[h] + ((mask >> j) & 1)
        return tuple(counts)

    counts = lax.fori_loop(0, z.half // 2, pair, (jnp.int32(0), jnp.int32(0)))
    load.wait()
    for h, out in enumerate((first, second)):
        @pl.loop(0, jnp.minimum(counts[h], CAP1))
        def _(n, h=h, out=out):
            entry = entries[h, n]
            i = pl.multiple_of((entry // 8) * TILE, TILE)
            j = pl.multiple_of((entry % 8) * TILE, TILE)
            tile = held[pl.ds(i, TILE), pl.ds(j, TILE)]
            out[n] = tile
            both[h * CAP1 + n] = tile


def turned(distance, sign):
    d = lax.rem(distance * sign + 2 * SIDE, SIDE)
    return jnp.where(d == 0, 0, jnp.where(d == 3, 1, jnp.where(d == 1, 2, 3)))


def tables_kernel(z, plan, pattern_ref, keep_ref, _, sends, early, late):
    r, c, l = position()
    cz, cy = c // SIDE, c % SIDE
    sign = 1 - 2 * l
    present = pattern_ref[...].astype(jnp.float32)
    keep = keep_ref[...].astype(jnp.float32)
    one = lambda x: jnp.where(x, 1.0, 0.0)

    place = plan[0:z.tiles, PLACE:PLACE + 1]
    place_row = plan[z.tiles:z.tiles + 1, 0:z.tiles]
    k, s = where_in((z.tiles, TILE))
    mine = one((place == l * z.half + s) & (s < z.half) & (k // z.block_rows == r))
    has = dot(present.T, mine)
    kept = dot(keep.T, mine)

    a, b = where_in((z.tiles, z.tiles))
    block_a, block_b = a // z.block_cols, b // z.block_cols
    below = one(b < a)
    u, v = where_in((TILE, TILE))
    earlier = one(u < v)

    def placed(mask, group):
        return dot(group * below, mask) + dot(dot(group, mask), earlier)

    def needed(there):
        return one(dot(jnp.where(block_b == there, present, 0.0), kept) > 0) * has

    halves = [one((k + s) % 2 == h) for h in range(2)]
    block = k // z.block_cols
    outers = [block // SIDE, block % SIDE]
    groups = [one(block_a // SIDE == block_b // SIDE), one(block_a % SIDE == block_b % SIDE)]
    me = [cz, cy]
    same_block = one(block_a == block_b)
    within = sum(halves[h] * placed(has * halves[h], same_block) for h in range(2))
    lane = where_in((1, TILE))[1]
    place_left = jnp.zeros((z.tiles, TILE), jnp.float32)
    stride = SIDE * CAP1 + CAPM + CAP2
    sizes = jnp.zeros((1, TILE), jnp.float32)
    late_sizes = jnp.zeros((1, TILE), jnp.float32)
    is_late = jnp.zeros((z.tiles, TILE), jnp.float32)
    everyone = jnp.ones((TILE, TILE), jnp.float32)

    def compact(mask, position, value, columns, empty):
        where = jnp.where(mask > 0, position, -1.0).astype(jnp.int32)
        value = value.astype(jnp.int32) - empty
        row = jnp.zeros((1, TILE), jnp.int32)
        for n in columns:
            hit = where[:, n:n + 1] == where_in((z.tiles, TILE))[1]
            row = row + jnp.sum(jnp.where(hit, value[:, n:n + 1], 0), axis=0, keepdims=True)
        return row + empty

    def total(mask):
        return jnp.sum(jnp.sum(mask, axis=0, keepdims=True), axis=1, keepdims=True).astype(jnp.int32)

    def tally(mask, part):
        return jnp.sum(jnp.where(s == part, dot(mask, everyone), 0.0), axis=0, keepdims=True)

    for h in range(2):
        outer, inner = outers[h], outers[1 - h]
        away = lax.rem((outer - me[h]) * sign + 2 * SIDE, SIDE)
        held = turned(inner - me[1 - h], sign).astype(jnp.float32) * CAP1 + within
        wants = []
        for distance in range(SIDE):
            there = lax.rem(me[h] + distance * sign + SIDE, SIDE)
            wants.append(needed(there * SIDE + cy if h == 0 else cz * SIDE + there) * halves[h])
        next_one = sum(jnp.where(away == d, wants[(d + 1) % SIDE], 0.0) for d in range(SIDE))
        opposite = sum(jnp.where(away == d, wants[(d + 2) % SIDE], 0.0) for d in range(SIDE))
        only_far, shared, only_next = opposite * (1 - next_one), opposite * next_one, next_one * (1 - opposite)
        count = lambda mask: dot(dot(groups[h], mask), everyone)
        start_shared = count(only_far)
        start_next = start_shared + count(shared)
        reached = only_far * placed(only_far, groups[h]) + shared * (start_shared + placed(shared, groups[h]))
        reached = reached + only_next * (start_next + placed(only_next, groups[h]))
        ring = one(away == 0)
        for n, (mask, where) in enumerate((
            ((only_far + shared + only_next) * ring, reached),
            (wants[3] * ring, placed(wants[3], groups[h])),
        )):
            row = compact(mask, where, held, range(z.half), 0)
            most = (CAPM, CAP2)[n]
            sends[h * 2 + n:h * 2 + n + 1, :] = jnp.where(lane == TILE - 1, jnp.minimum(total(mask), most), row)
        arrived = jnp.where(away == 3, reached, CAPM + placed(wants[0], groups[h]))
        early_place = h * stride + jnp.where(away == 0, held, SIDE * CAP1 + arrived)
        place_left = place_left + halves[h] * jnp.where(away == 2, h * CAP2 + reached, early_place)
        is_late = is_late + halves[h] * one(away == 2)
        sizes = sizes + tally(has * halves[h] * ring, h * 6 + turned(inner - me[1 - h], sign))
        sizes = sizes + tally((shared + only_far + only_next) * one(away == 3), h * 6 + 4)
        sizes = sizes + tally(wants[0] * one(away == 1), h * 6 + 5)
        late_sizes = late_sizes + tally(opposite * one(away == 2), h)

    core = place // z.half
    slot = place % z.half
    core_row = place_row // z.half
    slot_row = place_row % z.half
    ahead = one((a // z.block_rows == b // z.block_rows) & (core == core_row) & (slot_row < slot))
    column = dot(present, one((k == c * z.block_cols + s) & (s < z.block_cols)))
    place_right = jnp.zeros((z.tiles, TILE), jnp.float32)
    for h in range(2):
        half = one((slot + s) % 2 == h)
        mask = column * half
        right_part = ((k // z.block_rows) * 2 + core) * 2 + h
        sizes = sizes + tally(mask, 12 + right_part)
        late_sizes = late_sizes + tally(mask, 2 + right_part)
        place_right = place_right + half * (h * CAP1 + dot(mask, earlier) + dot(dot(ahead, mask), everyone))
    place_right = place_right + ((right_part // 2) * (2 * CAP1)).astype(jnp.float32)

    pairs = z.half * z.block_cols
    to_slot = one((u == v // z.block_cols) & (v < pairs))
    to_column = one((u == v % z.block_cols) & (v < pairs))
    kept_here = dot(kept, to_slot) * one((k == c * z.block_cols + s % z.block_cols) & (s < pairs))
    mask = dot(has, to_slot) * dot(column, to_column) * jnp.sum(kept_here, axis=0, keepdims=True)
    is_late = dot(is_late, to_slot)

    def spread(x, to):
        x = x.astype(jnp.int32)
        return dot(x // 64, to) * 64 + dot(x % 64, to)

    value = spread(place_left, to_slot) * RIGHT_BITS + spread(place_right, to_column)
    for lists, mask, parts, n_left in ((early, mask * (1 - is_late), sizes, 2 * stride), (late, mask * is_late, late_sizes, 2 * CAP2)):
        empty = n_left * RIGHT_BITS + 4 * z.blocks * CAP1
        where = dot(below, mask)
        count = jnp.sum(mask, axis=0, keepdims=True).astype(jnp.int32)
        for n in range(pairs):
            row = compact(mask, where, value, (n,), empty)
            lists[n:n + 1, :] = jnp.where(lane == TILE - 1, count[:, n:n + 1], row)
        lists[pairs:pairs + 1, :] = jnp.full((1, TILE), empty, jnp.int32)
        lists[pairs + 1:pairs + 2, :] = parts.astype(jnp.int32)


def load_all(parts, held, sem):
    copies, at = [], 0
    for n, part in enumerate(parts):
        part, start, size = part if isinstance(part, tuple) else (part, 0, part.shape[0])
        copies.append(pltpu.make_async_copy(part.at[pl.ds(start, size)], held.at[pl.ds(at, size)], sem.at[n]))
        copies[-1].start()
        at += size
    return copies


def second_kernel(sends_ref, *refs):
    sources, outs, (held, sends, sem, known) = refs[:8], refs[8:12], refs[12:]
    told = pltpu.make_async_copy(sends_ref, sends, known)
    told.start()
    copies = load_all(sources, held, sem)
    told.wait()
    for copy in copies:
        copy.wait()
    for h in range(2):
        ahead, behind = outs[2 * h:2 * h + 2]
        for n, out in enumerate((ahead, behind)):
            @pl.loop(0, sends[2 * h + n, TILE - 1])
            def _(t, n=2 * h + n, out=out, base=h * SIDE * CAP1):
                out[t] = held[base + sends[n, t]]


def multiply(z, listed, lefts, gathered, lists, sizes, known, left, right, total, work, sem, begin):
    pairs = z.half * z.block_cols
    tell_sizes = pltpu.make_async_copy(listed.at[pl.ds(pairs, 8)], sizes, known.at[0])
    tell_lists = pltpu.make_async_copy(listed, lists, known.at[1])
    tell_sizes.start()
    tell_lists.start()
    pieces, at = [], 0
    for part in lefts:
        pieces.append((part, 0, left, at, part.shape[0]))
        at += part.shape[0]
    for n in range(4 * z.blocks):
        pieces.append((gathered, n * CAP1, right, n * CAP1, CAP1))

    def each_copy(act):
        for n, (source, start, target, at, room) in enumerate(pieces):
            size = sizes[1, n]

            @pl.loop(0, jnp.minimum((size + CHUNK - 1) // CHUNK, room // CHUNK))
            def _(t, n=n, source=source, start=start, target=target, at=at):
                act(pltpu.make_async_copy(source.at[pl.ds(start + t * CHUNK, CHUNK)], target.at[pl.ds(at + t * CHUNK, CHUNK)], sem.at[n]))

    tell_sizes.wait()
    each_copy(lambda copy: copy.start())
    left[left.shape[0] - 1] = jnp.zeros((TILE, TILE), left.dtype)
    right[right.shape[0] - 1] = jnp.zeros((TILE, TILE), right.dtype)

    def flatten(n, at):
        def one_group(g, at):
            work[at] = n * 32 + g
            return at + 1

        return lax.fori_loop(0, (lists[n, TILE - 1] + GROUP - 1) // GROUP, one_group, at)

    tell_lists.wait()
    found = lax.fori_loop(0, pairs, flatten, jnp.int32(0))
    for extra in range(TOGETHER):
        work[found + extra] = pairs * 32
    begin()
    each_copy(lambda copy: copy.wait())

    @pl.loop(0, (found + TOGETHER - 1) // TOGETHER)
    def _(t):
        for m in range(TOGETHER):
            item = work[t * TOGETHER + m]
            n = item // 32
            entries = [lists[n, (item % 32) * GROUP + u] for u in range(GROUP)]
            lhs = jnp.concatenate([left[e // RIGHT_BITS] for e in entries], axis=1)
            rhs = jnp.concatenate([right[e % RIGHT_BITS] for e in entries], axis=0)
            total[n] += jnp.dot(lhs, rhs, preferred_element_type=jnp.float32)


def early_kernel(z, n_left, lists, gathered, *refs):
    lefts, total = refs[:n_left], refs[n_left]
    known, left, right, work, sem = refs[n_left + 1:n_left + 4], *refs[n_left + 4:]

    def begin():
        @pl.loop(0, total.shape[0])
        def _(n):
            total[n] = jnp.zeros((TILE, TILE), jnp.float32)

    multiply(z, lists, lefts, gathered, *known, left, right, total, work, sem, begin)


def late_kernel(z, n_left, lists, before, _, gathered, *refs):
    lefts, (mine, other, totals) = refs[:n_left], refs[n_left:n_left + 3]
    known, left, right, total, sums, work, sem, out_sem = refs[n_left + 3:n_left + 6], *refs[n_left + 6:]
    l = lax.axis_index("layer")
    width = z.block_cols * TILE // 2
    per_core = z.block_cols // 2
    load = pltpu.make_async_copy(before, total, out_sem.at[0])
    load.start()
    sums[...] = jnp.zeros_like(sums)
    multiply(z, lists, lefts, gathered, *known, left, right, total, work, sem, load.wait)

    @pl.loop(0, z.half)
    def _(s):
        for j in range(z.block_cols):
            n = s * z.block_cols + j
            value = total[n]
            kept = value * value
            total[n] = kept
            sums[:, j * TILE:(j + 1) * TILE] += jnp.sum(kept.reshape(TILE // 8, 8, TILE), axis=0)
        n = s * z.block_cols
        near = pl.ds(n + l * per_core, per_core)
        far = pl.ds(n + (1 - l) * per_core, per_core)
        rows = pl.ds(s * per_core, per_core)
        pltpu.make_async_copy(total.at[near], mine.at[rows], out_sem.at[0]).start()
        pltpu.make_async_copy(total.at[far], other.at[rows], out_sem.at[1]).start()

    whole = jnp.sum(sums[...], axis=0, keepdims=True)
    near, far = whole[:, :width], whole[:, width:]
    totals[0:1, :] = jnp.where(l == 0, near, far)
    totals[1:2, :] = jnp.where(l == 0, far, near)
    pltpu.make_async_copy(mine, mine, out_sem.at[0]).wait()
    pltpu.make_async_copy(other, other, out_sem.at[1]).wait()


def scale_kernel(z, order, places, mine, other, totals, received, out):
    r, c, l = position()
    factor = order / (totals[0:1, :] + received[...])
    per_core = z.block_cols // 2

    @pl.loop(0, z.block_rows)
    def _(i):
        place = places[0, r * z.block_rows + i]
        core = place // z.half
        first = (place % z.half) * per_core
        target = pl.ds(pl.multiple_of(i * TILE, TILE), TILE)

        def scaled(source):
            for j in range(per_core):
                columns = slice(j * TILE, (j + 1) * TILE)
                out[target, columns] = source[first + j] * factor[:, columns]

        pl.when(core == l)(lambda: scaled(mine))
        pl.when(core != l)(lambda: scaled(other))


def turn(axis, distance, flip=True):
    pairs = []
    for place in range(SIDE * SIDE):
        for core in range(2):
            at = [place // SIDE, place % SIDE]
            at[axis] = (at[axis] + distance * (1 - 2 * core)) % SIDE
            pairs.append((place * 2 + core, (at[0] * SIDE + at[1]) * 2 + core))
    return pairs


def sparse(z, markov, pattern, keep):
    tile = lambda n: jax.ShapeDtypeStruct((n, TILE, TILE), markov.dtype)
    move = lambda x, axis, distance: lax.ppermute(x, ("col", "layer"), turn(axis, distance))
    width = z.block_cols * TILE // 2
    plan, places, first, second, both = pl.pallas_call(
        functools.partial(pack_kernel, z),
        out_shape=[
            jax.ShapeDtypeStruct((z.tiles + 8, TILE), jnp.int32),
            jax.ShapeDtypeStruct((8, TILE), jnp.int32),
            tile(CAP1),
            tile(CAP1),
            tile(2 * CAP1),
        ],
        in_specs=[VMEM, HBM],
        out_specs=[VMEM] * 5,
        scratch_shapes=[
            pltpu.VMEM(markov.shape, markov.dtype),
            pltpu.SMEM((z.tiles + 8, TILE), jnp.int32),
            pltpu.SMEM((z.block_rows,), jnp.int32),
            pltpu.SMEM((2, z.block_rows * z.block_cols), jnp.int32),
            pltpu.SemaphoreType.DMA((2,)),
        ],
        compiler_params=pltpu.CompilerParams(vmem_limit_bytes=16 * MIB),
        name="pack",
    )(pattern, markov)

    sources = []
    for h, own in enumerate((first, second)):
        behind = move(own, 1 - h, 1)
        ahead = move(own, 1 - h, -1)
        sources.append([own, behind, ahead, move(behind, 1 - h, 1)])
    swap = [(0, 1), (1, 0)]
    after = lambda x, *others: lax.optimization_barrier((x, *others))[0]
    right = lax.all_gather(both, ("row", "layer"), axis=0, tiled=True)

    sends, early, late = pl.pallas_call(
        functools.partial(tables_kernel, z),
        out_shape=[jax.ShapeDtypeStruct((8, TILE), jnp.int32), *[jax.ShapeDtypeStruct((z.half * z.block_cols + 8, TILE), jnp.int32)] * 2],
        in_specs=[VMEM, VMEM, VMEM, HBM],
        out_specs=[VMEM] * 3,
        compiler_params=pltpu.CompilerParams(vmem_limit_bytes=8 * MIB),
        name="tables",
    )(plan, pattern, keep, first)
    outs = pl.pallas_call(
        second_kernel,
        out_shape=[tile(CAPM), tile(CAP2)] * 2,
        in_specs=[HBM] * 9,
        out_specs=[VMEM] * 4,
        scratch_shapes=[
            pltpu.VMEM((2 * SIDE * CAP1, TILE, TILE), markov.dtype),
            pltpu.SMEM((8, TILE), jnp.int32),
            pltpu.SemaphoreType.DMA((8,)),
            pltpu.SemaphoreType.DMA,
        ],
        compiler_params=pltpu.CompilerParams(vmem_limit_bytes=20 * MIB),
        name="second",
    )(sends, *sources[0], *sources[1])
    ahead = [move(outs[2 * h], h, 1) for h in range(2)]
    flag = pl.pallas_call(
        functools.partial(check_kernel, z),
        out_shape=jax.ShapeDtypeStruct((1, 1), jnp.int32),
        in_specs=[VMEM, VMEM, HBM],
        out_specs=VMEM,
        compiler_params=pltpu.CompilerParams(vmem_limit_bytes=8 * MIB),
        name="check",
    )(pattern, keep, outs[0])
    behind = [move(after(outs[2 * h + 1], flag), h, -1) for h in range(2)]
    far = [move(ahead[h][:CAP2], h, 1) for h in range(2)]
    lefts = []
    for h in range(2):
        lefts += sources[h] + [ahead[h], behind[h]]

    pairs = z.half * z.block_cols
    room = lambda parts: pltpu.VMEM((sum(x.shape[0] for x in parts) + 1, TILE, TILE), markov.dtype)
    told = [pltpu.SMEM((pairs + 8, TILE), jnp.int32), pltpu.SMEM((8, TILE), jnp.int32), pltpu.SemaphoreType.DMA((2,))]
    work = pltpu.SMEM((pairs * 32 + TOGETHER,), jnp.int32)
    sems = lambda parts: pltpu.SemaphoreType.DMA((len(parts) + 4 * z.blocks,))
    total = jax.ShapeDtypeStruct((pairs + 1, TILE, TILE), jnp.float32)
    before = pl.pallas_call(
        functools.partial(early_kernel, z, len(lefts)),
        out_shape=total,
        in_specs=[HBM] * (len(lefts) + 2),
        out_specs=VMEM,
        scratch_shapes=[*told, room(lefts), room([right]), work, sems(lefts)],
        compiler_params=pltpu.CompilerParams(vmem_limit_bytes=EARLY_LIMIT * MIB),
        cost_estimate=pl.CostEstimate(flops=20 * 10**9, bytes_accessed=30 * 10**6, transcendentals=0),
        name="early",
    )(early, right, *lefts)
    mine, other, totals = pl.pallas_call(
        functools.partial(late_kernel, z, len(far)),
        out_shape=[
            jax.ShapeDtypeStruct((pairs // 2, TILE, TILE), jnp.float32),
            jax.ShapeDtypeStruct((pairs // 2, TILE, TILE), jnp.float32),
            jax.ShapeDtypeStruct((2, width), jnp.float32),
        ],
        in_specs=[HBM] * (4 + len(far)),
        out_specs=[HBM, HBM, VMEM],
        scratch_shapes=[
            *told,
            room(far),
            room([right]),
            pltpu.VMEM(total.shape, total.dtype),
            pltpu.VMEM((8, 2 * width), jnp.float32),
            work,
            sems(far),
            pltpu.SemaphoreType.DMA((2,)),
        ],
        compiler_params=pltpu.CompilerParams(vmem_limit_bytes=LATE_LIMIT * MIB),
        name="late",
    )(late, before, flag, right, *far)
    received = lax.ppermute(other, "layer", swap)
    summed = totals
    for d in range(1, z.blocks):
        summed = summed + lax.ppermute(totals, "row", [(n, (n + d) % z.blocks) for n in range(z.blocks)])
    out = pl.pallas_call(
        functools.partial(scale_kernel, z, float(z.tiles * TILE)),
        out_shape=jax.ShapeDtypeStruct((markov.shape[0], width), jnp.float32),
        in_specs=[SMEM] + [VMEM] * 4,
        out_specs=VMEM,
        compiler_params=pltpu.CompilerParams(vmem_limit_bytes=16 * MIB),
        name="scale",
    )(places, mine, received, summed, lax.ppermute(summed[1:2], "layer", swap))
    return out, flag


def tile_scale(z, block, tiles, rows, cols):
    shaped = block.reshape(rows, TILE, cols, TILE)
    return (shaped * tiles.astype(block.dtype)[:, None, :, None]).reshape(block.shape)


def dense(z, markov, pattern, keep):
    straight = Layout(major_to_minor=(0, 1))
    markov, pattern, keep = [with_layout_constraint(x, straight) for x in (markov, pattern, keep)]
    r, c, l = position()
    rows, cols = markov.shape
    width = cols // 2
    swap = [(0, 1), (1, 0)]
    places = SIDE * SIDE
    cut = lambda x: lax.dynamic_slice(x, (r * z.block_rows, c * z.block_cols), (z.block_rows, z.block_cols))
    around = lambda x, d: lax.ppermute(x, "row", [(n, (n + d) % z.blocks) for n in range(z.blocks)])
    live = tile_scale(z, markov, cut(pattern), z.block_rows, z.block_cols)
    left = lax.dynamic_index_in_dim(live.reshape(rows, 2, width), l, 1, keepdims=False)
    right = jnp.zeros((z.blocks, rows, cols), live.dtype)
    for d in range(z.blocks):
        part = around(live, d) if d else live
        right = lax.dynamic_update_slice(right, part[None], (lax.rem(r - d + z.blocks, z.blocks), 0, 0))
    right = lax.dynamic_index_in_dim(right.reshape(places, 2, width, cols), l, 1, keepdims=False)

    def step(t, state):
        total, left = state
        block = lax.dynamic_index_in_dim(right, lax.rem(c - t + places, places), 0, keepdims=False)
        total = total + jnp.dot(left, block, preferred_element_type=jnp.float32)
        return total, lax.ppermute(left, "col", [(n, (n + 1) % places) for n in range(places)])

    square, _ = lax.fori_loop(0, places, step, (jnp.zeros((rows, cols), jnp.float32), left))
    square = square + lax.ppermute(square, "layer", swap)
    kept = tile_scale(z, square * square, cut(keep), z.block_rows, z.block_cols)
    totals = jnp.sum(kept, axis=0)
    totals = totals + sum(around(totals, d) for d in range(1, z.blocks))
    scaled = (z.tiles * TILE) * kept / totals[None, :]
    return with_layout_constraint(lax.dynamic_slice_in_dim(scaled, l * width, width, 1), straight)


def shards(markov, pattern, keep):
    z = Sizes(*markov.shape, pattern.shape[0])
    out, over = sparse(z, markov, pattern, keep)
    _, out = lax.while_loop(
        lambda state: state[0][0, 0] > 0,
        lambda state: (jnp.zeros_like(state[0]), dense(z, markov, pattern, keep)),
        (over, out),
    )
    return out


def solution(mesh):
    in_specs = (P("row", "col"), P(), P())
    out_specs = P("row", ("col", "layer"))
    return jax.shard_map(shards, mesh=mesh, in_specs=in_specs, out_specs=out_specs, check_vma=False)
```

```python
import functools

import jax
import jax.numpy as jnp
from jax import lax
from jax.experimental import pallas as pl
from jax.experimental.layout import Layout, with_layout_constraint
from jax.experimental.pallas import tpu as pltpu
from jax.sharding import PartitionSpec as P

TILE = 128
SIDE = 4
GROUP = 4
TOGETHER = 4
CAP1 = 20
CAP2 = 40
CAPM = 48
CHUNK = 4
EARLY_LIMIT = 60
LATE_LIMIT = 60
RIGHT_BITS = 4096
PLACE = 16
MIB = 1024 * 1024

SMEM = pl.BlockSpec(memory_space=pltpu.SMEM)
VMEM = pl.BlockSpec(memory_space=pltpu.VMEM)
HBM = pl.BlockSpec(memory_space=pltpu.HBM)


def position():
    return lax.axis_index("row"), lax.axis_index("col"), lax.axis_index("layer")


def dot(a, b):
    return jnp.dot(a.astype(jnp.bfloat16), b.astype(jnp.bfloat16), preferred_element_type=jnp.float32)


def where_in(shape):
    return lax.broadcasted_iota(jnp.int32, shape, 0), lax.broadcasted_iota(jnp.int32, shape, 1)


def ranks(block_rows, present):
    tiles = present.shape[0]
    ones = jnp.ones((8, tiles), jnp.bfloat16)
    level_row = lax.dot_general(ones, present.astype(jnp.bfloat16), (((1,), (1,)), ((), ())), preferred_element_type=jnp.float32)[:1]
    level_col = jnp.sum(present, axis=1, keepdims=True)
    a, b = where_in((tiles, tiles))
    same = jnp.where(a // block_rows == b // block_rows, 1.0, 0.0)
    above = jnp.where(level_col > level_row, 1.0, 0.0) + jnp.where(level_col == level_row, jnp.where(a < b, 1.0, 0.0), 0.0)
    below = jnp.where(level_col < level_row, 1.0, 0.0) + jnp.where(level_col == level_row, jnp.where(a > b, 1.0, 0.0), 0.0)
    return (
        jnp.sum(above * same, axis=0, keepdims=True).astype(jnp.int32),
        jnp.sum(below * same, axis=1, keepdims=True).astype(jnp.int32),
    )


def core_slot(rank):
    return ((rank + 1) // 2) % 2, rank // 2


class Sizes:
    def __init__(self, rows_dev, cols_dev, tiles):
        self.block_rows = rows_dev // TILE
        self.block_cols = cols_dev // TILE
        self.half = self.block_rows // 2
        self.tiles = tiles
        self.blocks = tiles // self.block_rows


def check_kernel(z, pattern_ref, keep_ref, _, flag_ref):
    groups = 2 * z.blocks
    present = pattern_ref[...].astype(jnp.float32)
    keep = keep_ref[...].astype(jnp.float32)
    rank, _ = ranks(z.block_rows, present)
    core, slot = core_slot(rank)
    owner, row = where_in((2 * groups, z.tiles))
    member = jnp.where(owner % groups == (row // z.block_rows) * 2 + core, 1.0, 0.0)
    member = member * jnp.where(owner // groups == slot % 2, 1.0, 0.0)
    i, k = where_in((2 * groups, z.tiles))
    odd = (i // groups + k) % 2
    i, k = where_in((z.tiles, TILE))
    per_block = jnp.where(i // z.block_cols == k, 1.0, 0.0)
    per_outer = [
        jnp.where(i // (z.block_cols * SIDE) == k, 1.0, 0.0),
        jnp.where((i // z.block_cols) % SIDE == k, 1.0, 0.0),
    ]
    by_k = dot(member, present)
    over = jnp.zeros((1, 1), jnp.int32)
    for h in range(2):
        counts = dot(jnp.where(odd == h, by_k, 0.0), per_block)
        most = jnp.max(counts[:groups] + counts[groups:], keepdims=True)
        over = over + jnp.where(most > CAP1, 1, 0)
    present_t = present.T
    column = where_in((z.tiles, z.tiles))[1]
    lane = where_in((groups, TILE))[1]
    needs = []
    for c in range(SIDE * SIDE):
        used = dot(jnp.where(column // z.block_cols == c, keep, 0.0), present_t)
        needs.append(jnp.where(used > 0, present, 0.0))
    cores = where_in((groups, TILE))[0] % 2
    for c in range(SIDE * SIDE):
        for h in range(2):
            outer, inner = axes_of(h, c)
            up, far, down = [needs[block_at(h, (outer + d) % SIDE, inner)] for d in (1, 2, 3)]
            far_up, far_down = jnp.maximum(far, up), jnp.maximum(far, down)
            for mask, most, core in ((far, CAP2, None), (up, CAP2, 1), (down, CAP2, 0), (far_up, CAPM, 0), (far_down, CAPM, 1)):
                counts = dot(jnp.where(odd == h, dot(member, mask), 0.0), per_outer[h])
                counts = counts[:groups] + counts[groups:]
                counted = jnp.where(lane == outer, counts, 0.0)
                if core is not None:
                    counted = jnp.where(cores == core, counted, 0.0)
                over = over + jnp.where(jnp.max(counted, keepdims=True) > most, 1, 0)
    flag_ref[...] = jnp.minimum(over, 1)


def axes_of(h, c):
    return (c // SIDE, c % SIDE) if h == 0 else (c % SIDE, c // SIDE)


def block_at(h, outer, inner):
    return outer * SIDE + inner if h == 0 else inner * SIDE + outer


def pack_kernel(z, pattern_ref, markov, plan_ref, places, first, second, both, held, plan, inverse, entries, sem):
    r, c, l = position()
    load = pltpu.make_async_copy(markov, held, sem.at[0])
    load.start()
    present = pattern_ref[...].astype(jnp.float32)
    i, k = where_in((z.tiles, TILE))
    weights = jnp.where(i // z.block_cols == k, jnp.left_shift(1, i % z.block_cols), 0)
    bits = dot(present, weights).astype(jnp.int32)
    rank_row, rank_col = ranks(z.block_rows, present)
    core, slot = core_slot(rank_row)
    plan_ref[...] = jnp.zeros_like(plan_ref)
    plan_ref[z.tiles:z.tiles + 1, 0:z.tiles] = core * z.half + slot
    core, slot = core_slot(rank_col)
    plan_ref[0:z.tiles, :] = jnp.where(k == PLACE, core * z.half + slot, bits)
    places[...] = plan_ref[z.tiles:z.tiles + 8, :]
    known = pltpu.make_async_copy(plan_ref, plan, sem.at[1])
    known.start()
    known.wait()

    @pl.loop(0, z.block_rows)
    def _(i):
        inverse[plan[z.tiles, r * z.block_rows + i]] = i

    def pair(t, counts):
        counts = list(counts)
        for odd in range(2):
            i = inverse[l * z.half + 2 * t + odd]
            mask = plan[r * z.block_rows + i, c]
            for j in range(z.block_cols):
                h = (odd + j) % 2
                entries[h, counts[h]] = i * 8 + j
                counts[h] = counts[h] + ((mask >> j) & 1)
        return tuple(counts)

    counts = lax.fori_loop(0, z.half // 2, pair, (jnp.int32(0), jnp.int32(0)))
    load.wait()
    for h, out in enumerate((first, second)):
        @pl.loop(0, jnp.minimum(counts[h], CAP1))
        def _(n, h=h, out=out):
            entry = entries[h, n]
            i = pl.multiple_of((entry // 8) * TILE, TILE)
            j = pl.multiple_of((entry % 8) * TILE, TILE)
            tile = held[pl.ds(i, TILE), pl.ds(j, TILE)]
            out[n] = tile
            both[h * CAP1 + n] = tile


def turned(distance, sign):
    d = lax.rem(distance * sign + 2 * SIDE, SIDE)
    return jnp.where(d == 0, 0, jnp.where(d == 3, 1, jnp.where(d == 1, 2, 3)))


def tables_kernel(z, plan, pattern_ref, keep_ref, _, sends, early, late):
    r, c, l = position()
    cz, cy = c // SIDE, c % SIDE
    sign = 1 - 2 * l
    present = pattern_ref[...].astype(jnp.float32)
    keep = keep_ref[...].astype(jnp.float32)
    one = lambda x: jnp.where(x, 1.0, 0.0)

    place = plan[0:z.tiles, PLACE:PLACE + 1]
    place_row = plan[z.tiles:z.tiles + 1, 0:z.tiles]
    k, s = where_in((z.tiles, TILE))
    mine = one((place == l * z.half + s) & (s < z.half) & (k // z.block_rows == r))
    has = dot(present.T, mine)
    kept = dot(keep.T, mine)

    a, b = where_in((z.tiles, z.tiles))
    block_a, block_b = a // z.block_cols, b // z.block_cols
    below = one(b < a)
    u, v = where_in((TILE, TILE))
    earlier = one(u < v)

    def placed(mask, group):
        return dot(group * below, mask) + dot(dot(group, mask), earlier)

    def needed(there):
        return one(dot(jnp.where(block_b == there, present, 0.0), kept) > 0) * has

    halves = [one((k + s) % 2 == h) for h in range(2)]
    block = k // z.block_cols
    outers = [block // SIDE, block % SIDE]
    groups = [one(block_a // SIDE == block_b // SIDE), one(block_a % SIDE == block_b % SIDE)]
    me = [cz, cy]
    same_block = one(block_a == block_b)
    within = sum(halves[h] * placed(has * halves[h], same_block) for h in range(2))
    lane = where_in((1, TILE))[1]
    place_left = jnp.zeros((z.tiles, TILE), jnp.float32)
    stride = SIDE * CAP1 + CAPM + CAP2
    sizes = jnp.zeros((1, TILE), jnp.float32)
    late_sizes = jnp.zeros((1, TILE), jnp.float32)
    is_late = jnp.zeros((z.tiles, TILE), jnp.float32)
    everyone = jnp.ones((TILE, TILE), jnp.float32)

    def compact(mask, position, value, columns, empty):
        where = jnp.where(mask > 0, position, -1.0).astype(jnp.int32)
        value = value.astype(jnp.int32) - empty
        row = jnp.zeros((1, TILE), jnp.int32)
        for n in columns:
            hit = where[:, n:n + 1] == where_in((z.tiles, TILE))[1]
            row = row + jnp.sum(jnp.where(hit, value[:, n:n + 1], 0), axis=0, keepdims=True)
        return row + empty

    def total(mask):
        return jnp.sum(jnp.sum(mask, axis=0, keepdims=True), axis=1, keepdims=True).astype(jnp.int32)

    def tally(mask, part):
        return jnp.sum(jnp.where(s == part, dot(mask, everyone), 0.0), axis=0, keepdims=True)

    for h in range(2):
        outer, inner = outers[h], outers[1 - h]
        away = lax.rem((outer - me[h]) * sign + 2 * SIDE, SIDE)
        held = turned(inner - me[1 - h], sign).astype(jnp.float32) * CAP1 + within
        held = jnp.minimum(held, SIDE * CAP1 - 1)
        wants = []
        for distance in range(SIDE):
            there = lax.rem(me[h] + distance * sign + SIDE, SIDE)
            wants.append(needed(there * SIDE + cy if h == 0 else cz * SIDE + there) * halves[h])
        next_one = sum(jnp.where(away == d, wants[(d + 1) % SIDE], 0.0) for d in range(SIDE))
        opposite = sum(jnp.where(away == d, wants[(d + 2) % SIDE], 0.0) for d in range(SIDE))
        only_far, shared, only_next = opposite * (1 - next_one), opposite * next_one, next_one * (1 - opposite)
        count = lambda mask: dot(dot(groups[h], mask), everyone)
        start_shared = count(only_far)
        start_next = start_shared + count(shared)
        reached = only_far * placed(only_far, groups[h]) + shared * (start_shared + placed(shared, groups[h]))
        reached = reached + only_next * (start_next + placed(only_next, groups[h]))
        ring = one(away == 0)
        for n, (mask, where) in enumerate((
            ((only_far + shared + only_next) * ring, reached),
            (wants[3] * ring, placed(wants[3], groups[h])),
        )):
            row = compact(mask, where, held, range(z.half), 0)
            most = (CAPM, CAP2)[n]
            sends[h * 2 + n:h * 2 + n + 1, :] = jnp.where(lane == TILE - 1, jnp.minimum(total(mask), most), row)
        arrived = jnp.where(away == 3, reached, CAPM + placed(wants[0], groups[h]))
        early_place = h * stride + jnp.where(away == 0, held, SIDE * CAP1 + arrived)
        early_place = jnp.minimum(early_place, 2 * stride - 1)
        late_place = jnp.minimum(h * CAP2 + reached, 2 * CAP2 - 1)
        place_left = place_left + halves[h] * jnp.where(away == 2, late_place, early_place)
        is_late = is_late + halves[h] * one(away == 2)
        sizes = sizes + tally(has * halves[h] * ring, h * 6 + turned(inner - me[1 - h], sign))
        sizes = sizes + tally((shared + only_far + only_next) * one(away == 3), h * 6 + 4)
        sizes = sizes + tally(wants[0] * one(away == 1), h * 6 + 5)
        late_sizes = late_sizes + tally(opposite * one(away == 2), h)

    core = place // z.half
    slot = place % z.half
    core_row = place_row // z.half
    slot_row = place_row % z.half
    ahead = one((a // z.block_rows == b // z.block_rows) & (core == core_row) & (slot_row < slot))
    column = dot(present, one((k == c * z.block_cols + s) & (s < z.block_cols)))
    place_right = jnp.zeros((z.tiles, TILE), jnp.float32)
    for h in range(2):
        half = one((slot + s) % 2 == h)
        mask = column * half
        right_part = ((k // z.block_rows) * 2 + core) * 2 + h
        sizes = sizes + tally(mask, 12 + right_part)
        late_sizes = late_sizes + tally(mask, 2 + right_part)
        place_right = place_right + half * (h * CAP1 + dot(mask, earlier) + dot(dot(ahead, mask), everyone))
    place_right = place_right + ((right_part // 2) * (2 * CAP1)).astype(jnp.float32)
    place_right = jnp.minimum(place_right, 4 * z.blocks * CAP1 - 1)

    pairs = z.half * z.block_cols
    to_slot = one((u == v // z.block_cols) & (v < pairs))
    to_column = one((u == v % z.block_cols) & (v < pairs))
    kept_here = dot(kept, to_slot) * one((k == c * z.block_cols + s % z.block_cols) & (s < pairs))
    mask = dot(has, to_slot) * dot(column, to_column) * jnp.sum(kept_here, axis=0, keepdims=True)
    is_late = dot(is_late, to_slot)

    def spread(x, to):
        x = x.astype(jnp.int32)
        return dot(x // 64, to) * 64 + dot(x % 64, to)

    value = spread(place_left, to_slot) * RIGHT_BITS + spread(place_right, to_column)
    for lists, mask, parts, n_left in ((early, mask * (1 - is_late), sizes, 2 * stride), (late, mask * is_late, late_sizes, 2 * CAP2)):
        empty = n_left * RIGHT_BITS + 4 * z.blocks * CAP1
        where = dot(below, mask)
        count = jnp.sum(mask, axis=0, keepdims=True).astype(jnp.int32)
        for n in range(pairs):
            row = compact(mask, where, value, (n,), empty)
            lists[n:n + 1, :] = jnp.where(lane == TILE - 1, count[:, n:n + 1], row)
        lists[pairs:pairs + 1, :] = jnp.full((1, TILE), empty, jnp.int32)
        lists[pairs + 1:pairs + 2, :] = parts.astype(jnp.int32)


def load_all(parts, held, sem):
    copies, at = [], 0
    for n, part in enumerate(parts):
        part, start, size = part if isinstance(part, tuple) else (part, 0, part.shape[0])
        copies.append(pltpu.make_async_copy(part.at[pl.ds(start, size)], held.at[pl.ds(at, size)], sem.at[n]))
        copies[-1].start()
        at += size
    return copies


def second_kernel(sends_ref, *refs):
    sources, outs, (held, sends, sem, known) = refs[:8], refs[8:12], refs[12:]
    told = pltpu.make_async_copy(sends_ref, sends, known)
    told.start()
    copies = load_all(sources, held, sem)
    told.wait()
    for copy in copies:
        copy.wait()
    for h in range(2):
        ahead, behind = outs[2 * h:2 * h + 2]
        for n, out in enumerate((ahead, behind)):
            @pl.loop(0, sends[2 * h + n, TILE - 1])
            def _(t, n=2 * h + n, out=out, base=h * SIDE * CAP1):
                out[t] = held[base + sends[n, t]]


def multiply(z, listed, lefts, gathered, lists, sizes, known, left, right, total, work, sem, begin):
    pairs = z.half * z.block_cols
    tell_sizes = pltpu.make_async_copy(listed.at[pl.ds(pairs, 8)], sizes, known.at[0])
    tell_lists = pltpu.make_async_copy(listed, lists, known.at[1])
    tell_sizes.start()
    tell_lists.start()
    pieces, at = [], 0
    for part in lefts:
        pieces.append((part, 0, left, at, part.shape[0]))
        at += part.shape[0]
    for n in range(4 * z.blocks):
        pieces.append((gathered, n * CAP1, right, n * CAP1, CAP1))

    def each_copy(act):
        for n, (source, start, target, at, room) in enumerate(pieces):
            size = sizes[1, n]

            @pl.loop(0, jnp.minimum((size + CHUNK - 1) // CHUNK, room // CHUNK))
            def _(t, n=n, source=source, start=start, target=target, at=at):
                act(pltpu.make_async_copy(source.at[pl.ds(start + t * CHUNK, CHUNK)], target.at[pl.ds(at + t * CHUNK, CHUNK)], sem.at[n]))

    tell_sizes.wait()
    each_copy(lambda copy: copy.start())
    left[left.shape[0] - 1] = jnp.zeros((TILE, TILE), left.dtype)
    right[right.shape[0] - 1] = jnp.zeros((TILE, TILE), right.dtype)

    def flatten(n, at):
        def one_group(g, at):
            work[at] = n * 32 + g
            return at + 1

        return lax.fori_loop(0, (lists[n, TILE - 1] + GROUP - 1) // GROUP, one_group, at)

    tell_lists.wait()
    found = lax.fori_loop(0, pairs, flatten, jnp.int32(0))
    for extra in range(TOGETHER):
        work[found + extra] = pairs * 32
    begin()
    each_copy(lambda copy: copy.wait())

    @pl.loop(0, (found + TOGETHER - 1) // TOGETHER)
    def _(t):
        for m in range(TOGETHER):
            item = work[t * TOGETHER + m]
            n = item // 32
            entries = [lists[n, (item % 32) * GROUP + u] for u in range(GROUP)]
            lhs = jnp.concatenate([left[e // RIGHT_BITS] for e in entries], axis=1)
            rhs = jnp.concatenate([right[e % RIGHT_BITS] for e in entries], axis=0)
            total[n] += jnp.dot(lhs, rhs, preferred_element_type=jnp.float32)


def early_kernel(z, n_left, lists, gathered, *refs):
    lefts, total = refs[:n_left], refs[n_left]
    known, left, right, work, sem = refs[n_left + 1:n_left + 4], *refs[n_left + 4:]

    def begin():
        @pl.loop(0, total.shape[0])
        def _(n):
            total[n] = jnp.zeros((TILE, TILE), jnp.float32)

    multiply(z, lists, lefts, gathered, *known, left, right, total, work, sem, begin)


def late_kernel(z, n_left, lists, before, _, gathered, *refs):
    lefts, (mine, other, totals) = refs[:n_left], refs[n_left:n_left + 3]
    known, left, right, total, sums, work, sem, out_sem = refs[n_left + 3:n_left + 6], *refs[n_left + 6:]
    l = lax.axis_index("layer")
    width = z.block_cols * TILE // 2
    per_core = z.block_cols // 2
    load = pltpu.make_async_copy(before, total, out_sem.at[0])
    load.start()
    sums[...] = jnp.zeros_like(sums)
    multiply(z, lists, lefts, gathered, *known, left, right, total, work, sem, load.wait)

    @pl.loop(0, z.half)
    def _(s):
        for j in range(z.block_cols):
            n = s * z.block_cols + j
            value = total[n]
            kept = value * value
            total[n] = kept
            sums[:, j * TILE:(j + 1) * TILE] += jnp.sum(kept.reshape(TILE // 8, 8, TILE), axis=0)
        n = s * z.block_cols
        near = pl.ds(n + l * per_core, per_core)
        far = pl.ds(n + (1 - l) * per_core, per_core)
        rows = pl.ds(s * per_core, per_core)
        pltpu.make_async_copy(total.at[near], mine.at[rows], out_sem.at[0]).start()
        pltpu.make_async_copy(total.at[far], other.at[rows], out_sem.at[1]).start()

    whole = jnp.sum(sums[...], axis=0, keepdims=True)
    near, far = whole[:, :width], whole[:, width:]
    totals[0:1, :] = jnp.where(l == 0, near, far)
    totals[1:2, :] = jnp.where(l == 0, far, near)
    pltpu.make_async_copy(mine, mine, out_sem.at[0]).wait()
    pltpu.make_async_copy(other, other, out_sem.at[1]).wait()


def scale_kernel(z, order, places, mine, other, totals, received, out):
    r, c, l = position()
    factor = order / (totals[0:1, :] + received[...])
    per_core = z.block_cols // 2

    @pl.loop(0, z.block_rows)
    def _(i):
        place = places[0, r * z.block_rows + i]
        core = place // z.half
        first = (place % z.half) * per_core
        target = pl.ds(pl.multiple_of(i * TILE, TILE), TILE)

        def scaled(source):
            for j in range(per_core):
                columns = slice(j * TILE, (j + 1) * TILE)
                out[target, columns] = source[first + j] * factor[:, columns]

        pl.when(core == l)(lambda: scaled(mine))
        pl.when(core != l)(lambda: scaled(other))


def turn(axis, distance, flip=True):
    pairs = []
    for place in range(SIDE * SIDE):
        for core in range(2):
            at = [place // SIDE, place % SIDE]
            at[axis] = (at[axis] + distance * (1 - 2 * core)) % SIDE
            pairs.append((place * 2 + core, (at[0] * SIDE + at[1]) * 2 + core))
    return pairs


def sparse(z, markov, pattern, keep):
    tile = lambda n: jax.ShapeDtypeStruct((n, TILE, TILE), markov.dtype)
    move = lambda x, axis, distance: lax.ppermute(x, ("col", "layer"), turn(axis, distance))
    width = z.block_cols * TILE // 2
    plan, places, first, second, both = pl.pallas_call(
        functools.partial(pack_kernel, z),
        out_shape=[
            jax.ShapeDtypeStruct((z.tiles + 8, TILE), jnp.int32),
            jax.ShapeDtypeStruct((8, TILE), jnp.int32),
            tile(CAP1),
            tile(CAP1),
            tile(2 * CAP1),
        ],
        in_specs=[VMEM, HBM],
        out_specs=[VMEM] * 5,
        scratch_shapes=[
            pltpu.VMEM(markov.shape, markov.dtype),
            pltpu.SMEM((z.tiles + 8, TILE), jnp.int32),
            pltpu.SMEM((z.block_rows,), jnp.int32),
            pltpu.SMEM((2, z.block_rows * z.block_cols), jnp.int32),
            pltpu.SemaphoreType.DMA((2,)),
        ],
        compiler_params=pltpu.CompilerParams(vmem_limit_bytes=16 * MIB),
        name="pack",
    )(pattern, markov)

    sources = []
    for h, own in enumerate((first, second)):
        behind = move(own, 1 - h, 1)
        ahead = move(own, 1 - h, -1)
        sources.append([own, behind, ahead, move(behind, 1 - h, 1)])
    swap = [(0, 1), (1, 0)]
    after = lambda x, *others: lax.optimization_barrier((x, *others))[0]
    right = lax.all_gather(both, ("row", "layer"), axis=0, tiled=True)

    sends, early, late = pl.pallas_call(
        functools.partial(tables_kernel, z),
        out_shape=[jax.ShapeDtypeStruct((8, TILE), jnp.int32), *[jax.ShapeDtypeStruct((z.half * z.block_cols + 8, TILE), jnp.int32)] * 2],
        in_specs=[VMEM, VMEM, VMEM, HBM],
        out_specs=[VMEM] * 3,
        compiler_params=pltpu.CompilerParams(vmem_limit_bytes=8 * MIB),
        name="tables",
    )(plan, pattern, keep, first)
    outs = pl.pallas_call(
        second_kernel,
        out_shape=[tile(CAPM), tile(CAP2)] * 2,
        in_specs=[HBM] * 9,
        out_specs=[VMEM] * 4,
        scratch_shapes=[
            pltpu.VMEM((2 * SIDE * CAP1, TILE, TILE), markov.dtype),
            pltpu.SMEM((8, TILE), jnp.int32),
            pltpu.SemaphoreType.DMA((8,)),
            pltpu.SemaphoreType.DMA,
        ],
        compiler_params=pltpu.CompilerParams(vmem_limit_bytes=20 * MIB),
        name="second",
    )(sends, *sources[0], *sources[1])
    ahead = [move(outs[2 * h], h, 1) for h in range(2)]
    flag = pl.pallas_call(
        functools.partial(check_kernel, z),
        out_shape=jax.ShapeDtypeStruct((1, 1), jnp.int32),
        in_specs=[VMEM, VMEM, HBM],
        out_specs=VMEM,
        compiler_params=pltpu.CompilerParams(vmem_limit_bytes=8 * MIB),
        name="check",
    )(pattern, keep, outs[0])
    behind = [move(after(outs[2 * h + 1], flag), h, -1) for h in range(2)]
    far = [move(ahead[h][:CAP2], h, 1) for h in range(2)]
    lefts = []
    for h in range(2):
        lefts += sources[h] + [ahead[h], behind[h]]

    pairs = z.half * z.block_cols
    room = lambda parts: pltpu.VMEM((sum(x.shape[0] for x in parts) + 1, TILE, TILE), markov.dtype)
    told = [pltpu.SMEM((pairs + 8, TILE), jnp.int32), pltpu.SMEM((8, TILE), jnp.int32), pltpu.SemaphoreType.DMA((2,))]
    work = pltpu.SMEM((pairs * 32 + TOGETHER,), jnp.int32)
    sems = lambda parts: pltpu.SemaphoreType.DMA((len(parts) + 4 * z.blocks,))
    total = jax.ShapeDtypeStruct((pairs + 1, TILE, TILE), jnp.float32)
    before = pl.pallas_call(
        functools.partial(early_kernel, z, len(lefts)),
        out_shape=total,
        in_specs=[HBM] * (len(lefts) + 2),
        out_specs=VMEM,
        scratch_shapes=[*told, room(lefts), room([right]), work, sems(lefts)],
        compiler_params=pltpu.CompilerParams(vmem_limit_bytes=EARLY_LIMIT * MIB),
        cost_estimate=pl.CostEstimate(flops=20 * 10**9, bytes_accessed=30 * 10**6, transcendentals=0),
        name="early",
    )(early, right, *lefts)
    mine, other, totals = pl.pallas_call(
        functools.partial(late_kernel, z, len(far)),
        out_shape=[
            jax.ShapeDtypeStruct((pairs // 2, TILE, TILE), jnp.float32),
            jax.ShapeDtypeStruct((pairs // 2, TILE, TILE), jnp.float32),
            jax.ShapeDtypeStruct((2, width), jnp.float32),
        ],
        in_specs=[HBM] * (4 + len(far)),
        out_specs=[HBM, HBM, VMEM],
        scratch_shapes=[
            *told,
            room(far),
            room([right]),
            pltpu.VMEM(total.shape, total.dtype),
            pltpu.VMEM((8, 2 * width), jnp.float32),
            work,
            sems(far),
            pltpu.SemaphoreType.DMA((2,)),
        ],
        compiler_params=pltpu.CompilerParams(vmem_limit_bytes=LATE_LIMIT * MIB),
        name="late",
    )(late, before, flag, right, *far)
    received = lax.ppermute(other, "layer", swap)
    summed = totals
    for d in range(1, z.blocks):
        summed = summed + lax.ppermute(totals, "row", [(n, (n + d) % z.blocks) for n in range(z.blocks)])
    out = pl.pallas_call(
        functools.partial(scale_kernel, z, float(z.tiles * TILE)),
        out_shape=jax.ShapeDtypeStruct((markov.shape[0], width), jnp.float32),
        in_specs=[SMEM] + [VMEM] * 4,
        out_specs=VMEM,
        compiler_params=pltpu.CompilerParams(vmem_limit_bytes=16 * MIB),
        name="scale",
    )(places, mine, received, summed, lax.ppermute(summed[1:2], "layer", swap))
    return out, flag


def tile_scale(z, block, tiles, rows, cols):
    shaped = block.reshape(rows, TILE, cols, TILE)
    return (shaped * tiles.astype(block.dtype)[:, None, :, None]).reshape(block.shape)


def dense(z, markov, pattern, keep):
    straight = Layout(major_to_minor=(0, 1))
    markov, pattern, keep = [with_layout_constraint(x, straight) for x in (markov, pattern, keep)]
    r, c, l = position()
    rows, cols = markov.shape
    width = cols // 2
    swap = [(0, 1), (1, 0)]
    places = SIDE * SIDE
    cut = lambda x: lax.dynamic_slice(x, (r * z.block_rows, c * z.block_cols), (z.block_rows, z.block_cols))
    around = lambda x, d: lax.ppermute(x, "row", [(n, (n + d) % z.blocks) for n in range(z.blocks)])
    live = tile_scale(z, markov, cut(pattern), z.block_rows, z.block_cols)
    left = lax.dynamic_index_in_dim(live.reshape(rows, 2, width), l, 1, keepdims=False)
    right = jnp.zeros((z.blocks, rows, cols), live.dtype)
    for d in range(z.blocks):
        part = around(live, d) if d else live
        right = lax.dynamic_update_slice(right, part[None], (lax.rem(r - d + z.blocks, z.blocks), 0, 0))
    right = lax.dynamic_index_in_dim(right.reshape(places, 2, width, cols), l, 1, keepdims=False)

    def step(t, state):
        total, left = state
        block = lax.dynamic_index_in_dim(right, lax.rem(c - t + places, places), 0, keepdims=False)
        total = total + jnp.dot(left, block, preferred_element_type=jnp.float32)
        return total, lax.ppermute(left, "col", [(n, (n + 1) % places) for n in range(places)])

    square, _ = lax.fori_loop(0, places, step, (jnp.zeros((rows, cols), jnp.float32), left))
    square = square + lax.ppermute(square, "layer", swap)
    kept = tile_scale(z, square * square, cut(keep), z.block_rows, z.block_cols)
    totals = jnp.sum(kept, axis=0)
    totals = totals + sum(around(totals, d) for d in range(1, z.blocks))
    scaled = (z.tiles * TILE) * kept / totals[None, :]
    return with_layout_constraint(lax.dynamic_slice_in_dim(scaled, l * width, width, 1), straight)


def shards(markov, pattern, keep):
    z = Sizes(*markov.shape, pattern.shape[0])
    out, over = sparse(z, markov, pattern, keep)
    _, out = lax.while_loop(
        lambda state: state[0][0, 0] > 0,
        lambda state: (jnp.zeros_like(state[0]), dense(z, markov, pattern, keep)),
        (over, out),
    )
    return out


def solution(mesh):
    in_specs = (P("row", "col"), P(), P())
    out_specs = P("row", ("col", "layer"))
    return jax.shard_map(shards, mesh=mesh, in_specs=in_specs, out_specs=out_specs, check_vma=False)
```

```python
import functools

import jax
import jax.numpy as jnp
from jax import lax
from jax.experimental import pallas as pl
from jax.experimental.layout import Layout, with_layout_constraint
from jax.experimental.pallas import tpu as pltpu
from jax.sharding import PartitionSpec as P

TILE = 128
SIDE = 4
GROUP = 4
TOGETHER = 6
CAP1 = 20
CAP2 = 40
CAPM = 48
CHUNK = 4
EARLY_LIMIT = 60
LATE_LIMIT = 60
RIGHT_BITS = 4096
PLACE = 16
MIB = 1024 * 1024

SMEM = pl.BlockSpec(memory_space=pltpu.SMEM)
VMEM = pl.BlockSpec(memory_space=pltpu.VMEM)
HBM = pl.BlockSpec(memory_space=pltpu.HBM)


def position():
    return lax.axis_index("row"), lax.axis_index("col"), lax.axis_index("layer")


def dot(a, b):
    return jnp.dot(a.astype(jnp.bfloat16), b.astype(jnp.bfloat16), preferred_element_type=jnp.float32)


def where_in(shape):
    return lax.broadcasted_iota(jnp.int32, shape, 0), lax.broadcasted_iota(jnp.int32, shape, 1)


def ranks(block_rows, present):
    tiles = present.shape[0]
    ones = jnp.ones((8, tiles), jnp.bfloat16)
    level_row = lax.dot_general(ones, present.astype(jnp.bfloat16), (((1,), (1,)), ((), ())), preferred_element_type=jnp.float32)[:1]
    level_col = jnp.sum(present, axis=1, keepdims=True)
    a, b = where_in((tiles, tiles))
    same = jnp.where(a // block_rows == b // block_rows, 1.0, 0.0)
    above = jnp.where(level_col > level_row, 1.0, 0.0) + jnp.where(level_col == level_row, jnp.where(a < b, 1.0, 0.0), 0.0)
    below = jnp.where(level_col < level_row, 1.0, 0.0) + jnp.where(level_col == level_row, jnp.where(a > b, 1.0, 0.0), 0.0)
    return (
        jnp.sum(above * same, axis=0, keepdims=True).astype(jnp.int32),
        jnp.sum(below * same, axis=1, keepdims=True).astype(jnp.int32),
    )


def core_slot(rank):
    return ((rank + 1) // 2) % 2, rank // 2


class Sizes:
    def __init__(self, rows_dev, cols_dev, tiles):
        self.block_rows = rows_dev // TILE
        self.block_cols = cols_dev // TILE
        self.half = self.block_rows // 2
        self.tiles = tiles
        self.blocks = tiles // self.block_rows


def check_kernel(z, pattern_ref, keep_ref, _, flag_ref):
    groups = 2 * z.blocks
    present = pattern_ref[...].astype(jnp.float32)
    keep = keep_ref[...].astype(jnp.float32)
    rank, _ = ranks(z.block_rows, present)
    core, slot = core_slot(rank)
    owner, row = where_in((2 * groups, z.tiles))
    member = jnp.where(owner % groups == (row // z.block_rows) * 2 + core, 1.0, 0.0)
    member = member * jnp.where(owner // groups == slot % 2, 1.0, 0.0)
    i, k = where_in((2 * groups, z.tiles))
    odd = (i // groups + k) % 2
    i, k = where_in((z.tiles, TILE))
    per_block = jnp.where(i // z.block_cols == k, 1.0, 0.0)
    per_outer = [
        jnp.where(i // (z.block_cols * SIDE) == k, 1.0, 0.0),
        jnp.where((i // z.block_cols) % SIDE == k, 1.0, 0.0),
    ]
    by_k = dot(member, present)
    over = jnp.zeros((1, 1), jnp.int32)
    for h in range(2):
        counts = dot(jnp.where(odd == h, by_k, 0.0), per_block)
        most = jnp.max(counts[:groups] + counts[groups:], keepdims=True)
        over = over + jnp.where(most > CAP1, 1, 0)
    present_t = present.T
    column = where_in((z.tiles, z.tiles))[1]
    lane = where_in((groups, TILE))[1]
    needs = []
    for c in range(SIDE * SIDE):
        used = dot(jnp.where(column // z.block_cols == c, keep, 0.0), present_t)
        needs.append(jnp.where(used > 0, present, 0.0))
    cores = where_in((groups, TILE))[0] % 2
    for c in range(SIDE * SIDE):
        for h in range(2):
            outer, inner = axes_of(h, c)
            up, far, down = [needs[block_at(h, (outer + d) % SIDE, inner)] for d in (1, 2, 3)]
            far_up, far_down = jnp.maximum(far, up), jnp.maximum(far, down)
            for mask, most, core in ((far, CAP2, None), (up, CAP2, 1), (down, CAP2, 0), (far_up, CAPM, 0), (far_down, CAPM, 1)):
                counts = dot(jnp.where(odd == h, dot(member, mask), 0.0), per_outer[h])
                counts = counts[:groups] + counts[groups:]
                counted = jnp.where(lane == outer, counts, 0.0)
                if core is not None:
                    counted = jnp.where(cores == core, counted, 0.0)
                over = over + jnp.where(jnp.max(counted, keepdims=True) > most, 1, 0)
    flag_ref[...] = jnp.minimum(over, 1)


def axes_of(h, c):
    return (c // SIDE, c % SIDE) if h == 0 else (c % SIDE, c // SIDE)


def block_at(h, outer, inner):
    return outer * SIDE + inner if h == 0 else inner * SIDE + outer


def pack_kernel(z, pattern_ref, markov, plan_ref, places, first, second, both, held, plan, inverse, entries, sem):
    r, c, l = position()
    load = pltpu.make_async_copy(markov, held, sem.at[0])
    load.start()
    present = pattern_ref[...].astype(jnp.float32)
    i, k = where_in((z.tiles, TILE))
    weights = jnp.where(i // z.block_cols == k, jnp.left_shift(1, i % z.block_cols), 0)
    bits = dot(present, weights).astype(jnp.int32)
    rank_row, rank_col = ranks(z.block_rows, present)
    core, slot = core_slot(rank_row)
    plan_ref[...] = jnp.zeros_like(plan_ref)
    plan_ref[z.tiles:z.tiles + 1, 0:z.tiles] = core * z.half + slot
    core, slot = core_slot(rank_col)
    plan_ref[0:z.tiles, :] = jnp.where(k == PLACE, core * z.half + slot, bits)
    places[...] = plan_ref[z.tiles:z.tiles + 8, :]
    known = pltpu.make_async_copy(plan_ref, plan, sem.at[1])
    known.start()
    known.wait()

    @pl.loop(0, z.block_rows)
    def _(i):
        inverse[plan[z.tiles, r * z.block_rows + i]] = i

    def pair(t, counts):
        counts = list(counts)
        for odd in range(2):
            i = inverse[l * z.half + 2 * t + odd]
            mask = plan[r * z.block_rows + i, c]
            for j in range(z.block_cols):
                h = (odd + j) % 2
                entries[h, counts[h]] = i * 8 + j
                counts[h] = counts[h] + ((mask >> j) & 1)
        return tuple(counts)

    counts = lax.fori_loop(0, z.half // 2, pair, (jnp.int32(0), jnp.int32(0)))
    load.wait()
    for h, out in enumerate((first, second)):
        @pl.loop(0, jnp.minimum(counts[h], CAP1))
        def _(n, h=h, out=out):
            entry = entries[h, n]
            i = pl.multiple_of((entry // 8) * TILE, TILE)
            j = pl.multiple_of((entry % 8) * TILE, TILE)
            tile = held[pl.ds(i, TILE), pl.ds(j, TILE)]
            out[n] = tile
            both[h * CAP1 + n] = tile


def turned(distance, sign):
    d = lax.rem(distance * sign + 2 * SIDE, SIDE)
    return jnp.where(d == 0, 0, jnp.where(d == 3, 1, jnp.where(d == 1, 2, 3)))


def tables_kernel(z, plan, pattern_ref, keep_ref, _, sends, early, late):
    r, c, l = position()
    cz, cy = c // SIDE, c % SIDE
    sign = 1 - 2 * l
    present = pattern_ref[...].astype(jnp.float32)
    keep = keep_ref[...].astype(jnp.float32)
    one = lambda x: jnp.where(x, 1.0, 0.0)

    place = plan[0:z.tiles, PLACE:PLACE + 1]
    place_row = plan[z.tiles:z.tiles + 1, 0:z.tiles]
    k, s = where_in((z.tiles, TILE))
    mine = one((place == l * z.half + s) & (s < z.half) & (k // z.block_rows == r))
    has = dot(present.T, mine)
    kept = dot(keep.T, mine)

    a, b = where_in((z.tiles, z.tiles))
    block_a, block_b = a // z.block_cols, b // z.block_cols
    below = one(b < a)
    u, v = where_in((TILE, TILE))
    earlier = one(u < v)

    def placed(mask, group):
        return dot(group * below, mask) + dot(dot(group, mask), earlier)

    def needed(there):
        return one(dot(jnp.where(block_b == there, present, 0.0), kept) > 0) * has

    halves = [one((k + s) % 2 == h) for h in range(2)]
    block = k // z.block_cols
    outers = [block // SIDE, block % SIDE]
    groups = [one(block_a // SIDE == block_b // SIDE), one(block_a % SIDE == block_b % SIDE)]
    me = [cz, cy]
    same_block = one(block_a == block_b)
    within = sum(halves[h] * placed(has * halves[h], same_block) for h in range(2))
    lane = where_in((1, TILE))[1]
    place_left = jnp.zeros((z.tiles, TILE), jnp.float32)
    stride = SIDE * CAP1 + CAPM + CAP2
    sizes = jnp.zeros((1, TILE), jnp.float32)
    late_sizes = jnp.zeros((1, TILE), jnp.float32)
    is_late = jnp.zeros((z.tiles, TILE), jnp.float32)
    everyone = jnp.ones((TILE, TILE), jnp.float32)

    def compact(mask, position, value, columns, empty):
        where = jnp.where(mask > 0, position, -1.0).astype(jnp.int32)
        value = value.astype(jnp.int32) - empty
        row = jnp.zeros((1, TILE), jnp.int32)
        for n in columns:
            hit = where[:, n:n + 1] == where_in((z.tiles, TILE))[1]
            row = row + jnp.sum(jnp.where(hit, value[:, n:n + 1], 0), axis=0, keepdims=True)
        return row + empty

    def total(mask):
        return jnp.sum(jnp.sum(mask, axis=0, keepdims=True), axis=1, keepdims=True).astype(jnp.int32)

    def tally(mask, part):
        return jnp.sum(jnp.where(s == part, dot(mask, everyone), 0.0), axis=0, keepdims=True)

    for h in range(2):
        outer, inner = outers[h], outers[1 - h]
        away = lax.rem((outer - me[h]) * sign + 2 * SIDE, SIDE)
        held = turned(inner - me[1 - h], sign).astype(jnp.float32) * CAP1 + within
        held = jnp.minimum(held, SIDE * CAP1 - 1)
        wants = []
        for distance in range(SIDE):
            there = lax.rem(me[h] + distance * sign + SIDE, SIDE)
            wants.append(needed(there * SIDE + cy if h == 0 else cz * SIDE + there) * halves[h])
        next_one = sum(jnp.where(away == d, wants[(d + 1) % SIDE], 0.0) for d in range(SIDE))
        opposite = sum(jnp.where(away == d, wants[(d + 2) % SIDE], 0.0) for d in range(SIDE))
        only_far, shared, only_next = opposite * (1 - next_one), opposite * next_one, next_one * (1 - opposite)
        count = lambda mask: dot(dot(groups[h], mask), everyone)
        start_shared = count(only_far)
        start_next = start_shared + count(shared)
        reached = only_far * placed(only_far, groups[h]) + shared * (start_shared + placed(shared, groups[h]))
        reached = reached + only_next * (start_next + placed(only_next, groups[h]))
        ring = one(away == 0)
        for n, (mask, where) in enumerate((
            ((only_far + shared + only_next) * ring, reached),
            (wants[3] * ring, placed(wants[3], groups[h])),
        )):
            row = compact(mask, where, held, range(z.half), 0)
            most = (CAPM, CAP2)[n]
            sends[h * 2 + n:h * 2 + n + 1, :] = jnp.where(lane == TILE - 1, jnp.minimum(total(mask), most), row)
        arrived = jnp.where(away == 3, reached, CAPM + placed(wants[0], groups[h]))
        early_place = h * stride + jnp.where(away == 0, held, SIDE * CAP1 + arrived)
        early_place = jnp.minimum(early_place, 2 * stride - 1)
        late_place = jnp.minimum(h * CAP2 + reached, 2 * CAP2 - 1)
        place_left = place_left + halves[h] * jnp.where(away == 2, late_place, early_place)
        is_late = is_late + halves[h] * one(away == 2)
        sizes = sizes + tally(has * halves[h] * ring, h * 6 + turned(inner - me[1 - h], sign))
        sizes = sizes + tally((shared + only_far + only_next) * one(away == 3), h * 6 + 4)
        sizes = sizes + tally(wants[0] * one(away == 1), h * 6 + 5)
        late_sizes = late_sizes + tally(opposite * one(away == 2), h)

    core = place // z.half
    slot = place % z.half
    core_row = place_row // z.half
    slot_row = place_row % z.half
    ahead = one((a // z.block_rows == b // z.block_rows) & (core == core_row) & (slot_row < slot))
    column = dot(present, one((k == c * z.block_cols + s) & (s < z.block_cols)))
    place_right = jnp.zeros((z.tiles, TILE), jnp.float32)
    for h in range(2):
        half = one((slot + s) % 2 == h)
        mask = column * half
        right_part = ((k // z.block_rows) * 2 + core) * 2 + h
        sizes = sizes + tally(mask, 12 + right_part)
        late_sizes = late_sizes + tally(mask, 2 + right_part)
        place_right = place_right + half * (h * CAP1 + dot(mask, earlier) + dot(dot(ahead, mask), everyone))
    place_right = place_right + ((right_part // 2) * (2 * CAP1)).astype(jnp.float32)
    place_right = jnp.minimum(place_right, 4 * z.blocks * CAP1 - 1)

    pairs = z.half * z.block_cols
    to_slot = one((u == v // z.block_cols) & (v < pairs))
    to_column = one((u == v % z.block_cols) & (v < pairs))
    kept_here = dot(kept, to_slot) * one((k == c * z.block_cols + s % z.block_cols) & (s < pairs))
    mask = dot(has, to_slot) * dot(column, to_column) * jnp.sum(kept_here, axis=0, keepdims=True)
    is_late = dot(is_late, to_slot)

    def spread(x, to):
        x = x.astype(jnp.int32)
        return dot(x // 64, to) * 64 + dot(x % 64, to)

    value = spread(place_left, to_slot) * RIGHT_BITS + spread(place_right, to_column)
    for lists, mask, parts, n_left in ((early, mask * (1 - is_late), sizes, 2 * stride), (late, mask * is_late, late_sizes, 2 * CAP2)):
        empty = n_left * RIGHT_BITS + 4 * z.blocks * CAP1
        where = dot(below, mask)
        count = jnp.sum(mask, axis=0, keepdims=True).astype(jnp.int32)
        for n in range(pairs):
            row = compact(mask, where, value, (n,), empty)
            lists[n:n + 1, :] = jnp.where(lane == TILE - 1, count[:, n:n + 1], row)
        lists[pairs:pairs + 1, :] = jnp.full((1, TILE), empty, jnp.int32)
        lists[pairs + 1:pairs + 2, :] = parts.astype(jnp.int32)


def load_all(parts, held, sem):
    copies, at = [], 0
    for n, part in enumerate(parts):
        part, start, size = part if isinstance(part, tuple) else (part, 0, part.shape[0])
        copies.append(pltpu.make_async_copy(part.at[pl.ds(start, size)], held.at[pl.ds(at, size)], sem.at[n]))
        copies[-1].start()
        at += size
    return copies


def second_kernel(sends_ref, *refs):
    sources, outs, (held, sends, sem, known) = refs[:8], refs[8:12], refs[12:]
    told = pltpu.make_async_copy(sends_ref, sends, known)
    told.start()
    copies = load_all(sources, held, sem)
    told.wait()
    for copy in copies:
        copy.wait()
    for h in range(2):
        ahead, behind = outs[2 * h:2 * h + 2]
        for n, out in enumerate((ahead, behind)):
            @pl.loop(0, sends[2 * h + n, TILE - 1])
            def _(t, n=2 * h + n, out=out, base=h * SIDE * CAP1):
                out[t] = held[base + sends[n, t]]


def multiply(z, listed, lefts, gathered, lists, sizes, known, left, right, total, work, sem, begin):
    pairs = z.half * z.block_cols
    tell_sizes = pltpu.make_async_copy(listed.at[pl.ds(pairs, 8)], sizes, known.at[0])
    tell_lists = pltpu.make_async_copy(listed, lists, known.at[1])
    tell_sizes.start()
    tell_lists.start()
    pieces, at = [], 0
    for part in lefts:
        pieces.append((part, 0, left, at, part.shape[0]))
        at += part.shape[0]
    for n in range(4 * z.blocks):
        pieces.append((gathered, n * CAP1, right, n * CAP1, CAP1))

    def each_copy(act):
        for n, (source, start, target, at, room) in enumerate(pieces):
            size = sizes[1, n]

            @pl.loop(0, jnp.minimum((size + CHUNK - 1) // CHUNK, room // CHUNK))
            def _(t, n=n, source=source, start=start, target=target, at=at):
                act(pltpu.make_async_copy(source.at[pl.ds(start + t * CHUNK, CHUNK)], target.at[pl.ds(at + t * CHUNK, CHUNK)], sem.at[n]))

    tell_sizes.wait()
    each_copy(lambda copy: copy.start())
    left[left.shape[0] - 1] = jnp.zeros((TILE, TILE), left.dtype)
    right[right.shape[0] - 1] = jnp.zeros((TILE, TILE), right.dtype)

    def flatten(n, at):
        def one_group(g, at):
            work[at] = n * 32 + g
            return at + 1

        return lax.fori_loop(0, (lists[n, TILE - 1] + GROUP - 1) // GROUP, one_group, at)

    tell_lists.wait()
    found = lax.fori_loop(0, pairs, flatten, jnp.int32(0))
    for extra in range(TOGETHER):
        work[found + extra] = pairs * 32
    begin()
    each_copy(lambda copy: copy.wait())

    @pl.loop(0, (found + TOGETHER - 1) // TOGETHER)
    def _(t):
        for m in range(TOGETHER):
            item = work[t * TOGETHER + m]
            n = item // 32
            entries = [lists[n, (item % 32) * GROUP + u] for u in range(GROUP)]
            lhs = jnp.concatenate([left[e // RIGHT_BITS] for e in entries], axis=1)
            rhs = jnp.concatenate([right[e % RIGHT_BITS] for e in entries], axis=0)
            total[n] += jnp.dot(lhs, rhs, preferred_element_type=jnp.float32)


def early_kernel(z, n_left, lists, gathered, *refs):
    lefts, total = refs[:n_left], refs[n_left]
    known, left, right, work, sem = refs[n_left + 1:n_left + 4], *refs[n_left + 4:]

    def begin():
        @pl.loop(0, total.shape[0])
        def _(n):
            total[n] = jnp.zeros((TILE, TILE), jnp.float32)

    multiply(z, lists, lefts, gathered, *known, left, right, total, work, sem, begin)


def late_kernel(z, n_left, lists, before, _, gathered, *refs):
    lefts, (mine, other, totals) = refs[:n_left], refs[n_left:n_left + 3]
    known, left, right, total, sums, work, sem, out_sem = refs[n_left + 3:n_left + 6], *refs[n_left + 6:]
    l = lax.axis_index("layer")
    width = z.block_cols * TILE // 2
    per_core = z.block_cols // 2
    load = pltpu.make_async_copy(before, total, out_sem.at[0])
    load.start()
    sums[...] = jnp.zeros_like(sums)
    multiply(z, lists, lefts, gathered, *known, left, right, total, work, sem, load.wait)

    @pl.loop(0, z.half)
    def _(s):
        for j in range(z.block_cols):
            n = s * z.block_cols + j
            value = total[n]
            kept = value * value
            total[n] = kept
            sums[:, j * TILE:(j + 1) * TILE] += jnp.sum(kept.reshape(TILE // 8, 8, TILE), axis=0)
        n = s * z.block_cols
        near = pl.ds(n + l * per_core, per_core)
        far = pl.ds(n + (1 - l) * per_core, per_core)
        rows = pl.ds(s * per_core, per_core)
        pltpu.make_async_copy(total.at[near], mine.at[rows], out_sem.at[0]).start()
        pltpu.make_async_copy(total.at[far], other.at[rows], out_sem.at[1]).start()

    whole = jnp.sum(sums[...], axis=0, keepdims=True)
    near, far = whole[:, :width], whole[:, width:]
    totals[0:1, :] = jnp.where(l == 0, near, far)
    totals[1:2, :] = jnp.where(l == 0, far, near)
    pltpu.make_async_copy(mine, mine, out_sem.at[0]).wait()
    pltpu.make_async_copy(other, other, out_sem.at[1]).wait()


def scale_kernel(z, order, places, mine, other, totals, received, out):
    r, c, l = position()
    factor = order / (totals[0:1, :] + received[...])
    per_core = z.block_cols // 2

    @pl.loop(0, z.block_rows)
    def _(i):
        place = places[0, r * z.block_rows + i]
        core = place // z.half
        first = (place % z.half) * per_core
        target = pl.ds(pl.multiple_of(i * TILE, TILE), TILE)

        def scaled(source):
            for j in range(per_core):
                columns = slice(j * TILE, (j + 1) * TILE)
                out[target, columns] = source[first + j] * factor[:, columns]

        pl.when(core == l)(lambda: scaled(mine))
        pl.when(core != l)(lambda: scaled(other))


def turn(axis, distance, flip=True):
    pairs = []
    for place in range(SIDE * SIDE):
        for core in range(2):
            at = [place // SIDE, place % SIDE]
            at[axis] = (at[axis] + distance * (1 - 2 * core)) % SIDE
            pairs.append((place * 2 + core, (at[0] * SIDE + at[1]) * 2 + core))
    return pairs


def sparse(z, markov, pattern, keep):
    tile = lambda n: jax.ShapeDtypeStruct((n, TILE, TILE), markov.dtype)
    move = lambda x, axis, distance: lax.ppermute(x, ("col", "layer"), turn(axis, distance))
    width = z.block_cols * TILE // 2
    plan, places, first, second, both = pl.pallas_call(
        functools.partial(pack_kernel, z),
        out_shape=[
            jax.ShapeDtypeStruct((z.tiles + 8, TILE), jnp.int32),
            jax.ShapeDtypeStruct((8, TILE), jnp.int32),
            tile(CAP1),
            tile(CAP1),
            tile(2 * CAP1),
        ],
        in_specs=[VMEM, HBM],
        out_specs=[VMEM] * 5,
        scratch_shapes=[
            pltpu.VMEM(markov.shape, markov.dtype),
            pltpu.SMEM((z.tiles + 8, TILE), jnp.int32),
            pltpu.SMEM((z.block_rows,), jnp.int32),
            pltpu.SMEM((2, z.block_rows * z.block_cols), jnp.int32),
            pltpu.SemaphoreType.DMA((2,)),
        ],
        compiler_params=pltpu.CompilerParams(vmem_limit_bytes=16 * MIB),
        name="pack",
    )(pattern, markov)

    sources = []
    for h, own in enumerate((first, second)):
        behind = move(own, 1 - h, 1)
        ahead = move(own, 1 - h, -1)
        sources.append([own, behind, ahead, move(behind, 1 - h, 1)])
    swap = [(0, 1), (1, 0)]
    after = lambda x, *others: lax.optimization_barrier((x, *others))[0]
    right = lax.all_gather(both, ("row", "layer"), axis=0, tiled=True)

    sends, early, late = pl.pallas_call(
        functools.partial(tables_kernel, z),
        out_shape=[jax.ShapeDtypeStruct((8, TILE), jnp.int32), *[jax.ShapeDtypeStruct((z.half * z.block_cols + 8, TILE), jnp.int32)] * 2],
        in_specs=[VMEM, VMEM, VMEM, HBM],
        out_specs=[VMEM] * 3,
        compiler_params=pltpu.CompilerParams(vmem_limit_bytes=8 * MIB),
        name="tables",
    )(plan, pattern, keep, first)
    outs = pl.pallas_call(
        second_kernel,
        out_shape=[tile(CAPM), tile(CAP2)] * 2,
        in_specs=[HBM] * 9,
        out_specs=[VMEM] * 4,
        scratch_shapes=[
            pltpu.VMEM((2 * SIDE * CAP1, TILE, TILE), markov.dtype),
            pltpu.SMEM((8, TILE), jnp.int32),
            pltpu.SemaphoreType.DMA((8,)),
            pltpu.SemaphoreType.DMA,
        ],
        compiler_params=pltpu.CompilerParams(vmem_limit_bytes=20 * MIB),
        name="second",
    )(sends, *sources[0], *sources[1])
    ahead = [move(outs[2 * h], h, 1) for h in range(2)]
    flag = pl.pallas_call(
        functools.partial(check_kernel, z),
        out_shape=jax.ShapeDtypeStruct((1, 1), jnp.int32),
        in_specs=[VMEM, VMEM, HBM],
        out_specs=VMEM,
        compiler_params=pltpu.CompilerParams(vmem_limit_bytes=8 * MIB),
        name="check",
    )(pattern, keep, outs[0])
    behind = [move(after(outs[2 * h + 1], flag), h, -1) for h in range(2)]
    far = [move(ahead[h][:CAP2], h, 1) for h in range(2)]
    lefts = []
    for h in range(2):
        lefts += sources[h] + [ahead[h], behind[h]]

    pairs = z.half * z.block_cols
    room = lambda parts: pltpu.VMEM((sum(x.shape[0] for x in parts) + 1, TILE, TILE), markov.dtype)
    told = [pltpu.SMEM((pairs + 8, TILE), jnp.int32), pltpu.SMEM((8, TILE), jnp.int32), pltpu.SemaphoreType.DMA((2,))]
    work = pltpu.SMEM((pairs * 32 + TOGETHER,), jnp.int32)
    sems = lambda parts: pltpu.SemaphoreType.DMA((len(parts) + 4 * z.blocks,))
    total = jax.ShapeDtypeStruct((pairs + 1, TILE, TILE), jnp.float32)
    before = pl.pallas_call(
        functools.partial(early_kernel, z, len(lefts)),
        out_shape=total,
        in_specs=[HBM] * (len(lefts) + 2),
        out_specs=VMEM,
        scratch_shapes=[*told, room(lefts), room([right]), work, sems(lefts)],
        compiler_params=pltpu.CompilerParams(vmem_limit_bytes=EARLY_LIMIT * MIB),
        cost_estimate=pl.CostEstimate(flops=20 * 10**9, bytes_accessed=30 * 10**6, transcendentals=0),
        name="early",
    )(early, right, *lefts)
    mine, other, totals = pl.pallas_call(
        functools.partial(late_kernel, z, len(far)),
        out_shape=[
            jax.ShapeDtypeStruct((pairs // 2, TILE, TILE), jnp.float32),
            jax.ShapeDtypeStruct((pairs // 2, TILE, TILE), jnp.float32),
            jax.ShapeDtypeStruct((2, width), jnp.float32),
        ],
        in_specs=[HBM] * (4 + len(far)),
        out_specs=[HBM, HBM, VMEM],
        scratch_shapes=[
            *told,
            room(far),
            room([right]),
            pltpu.VMEM(total.shape, total.dtype),
            pltpu.VMEM((8, 2 * width), jnp.float32),
            work,
            sems(far),
            pltpu.SemaphoreType.DMA((2,)),
        ],
        compiler_params=pltpu.CompilerParams(vmem_limit_bytes=LATE_LIMIT * MIB),
        name="late",
    )(late, before, flag, right, *far)
    received = lax.ppermute(other, "layer", swap)
    summed = totals
    for d in range(1, z.blocks):
        summed = summed + lax.ppermute(totals, "row", [(n, (n + d) % z.blocks) for n in range(z.blocks)])
    out = pl.pallas_call(
        functools.partial(scale_kernel, z, float(z.tiles * TILE)),
        out_shape=jax.ShapeDtypeStruct((markov.shape[0], width), jnp.float32),
        in_specs=[SMEM] + [VMEM] * 4,
        out_specs=VMEM,
        compiler_params=pltpu.CompilerParams(vmem_limit_bytes=16 * MIB),
        name="scale",
    )(places, mine, received, summed, lax.ppermute(summed[1:2], "layer", swap))
    return out, flag


def tile_scale(z, block, tiles, rows, cols):
    shaped = block.reshape(rows, TILE, cols, TILE)
    return (shaped * tiles.astype(block.dtype)[:, None, :, None]).reshape(block.shape)


def dense(z, markov, pattern, keep):
    straight = Layout(major_to_minor=(0, 1))
    markov, pattern, keep = [with_layout_constraint(x, straight) for x in (markov, pattern, keep)]
    r, c, l = position()
    rows, cols = markov.shape
    width = cols // 2
    swap = [(0, 1), (1, 0)]
    places = SIDE * SIDE
    cut = lambda x: lax.dynamic_slice(x, (r * z.block_rows, c * z.block_cols), (z.block_rows, z.block_cols))
    around = lambda x, d: lax.ppermute(x, "row", [(n, (n + d) % z.blocks) for n in range(z.blocks)])
    live = tile_scale(z, markov, cut(pattern), z.block_rows, z.block_cols)
    left = lax.dynamic_index_in_dim(live.reshape(rows, 2, width), l, 1, keepdims=False)
    right = jnp.zeros((z.blocks, rows, cols), live.dtype)
    for d in range(z.blocks):
        part = around(live, d) if d else live
        right = lax.dynamic_update_slice(right, part[None], (lax.rem(r - d + z.blocks, z.blocks), 0, 0))
    right = lax.dynamic_index_in_dim(right.reshape(places, 2, width, cols), l, 1, keepdims=False)

    def step(t, state):
        total, left = state
        block = lax.dynamic_index_in_dim(right, lax.rem(c - t + places, places), 0, keepdims=False)
        total = total + jnp.dot(left, block, preferred_element_type=jnp.float32)
        return total, lax.ppermute(left, "col", [(n, (n + 1) % places) for n in range(places)])

    square, _ = lax.fori_loop(0, places, step, (jnp.zeros((rows, cols), jnp.float32), left))
    square = square + lax.ppermute(square, "layer", swap)
    kept = tile_scale(z, square * square, cut(keep), z.block_rows, z.block_cols)
    totals = jnp.sum(kept, axis=0)
    totals = totals + sum(around(totals, d) for d in range(1, z.blocks))
    scaled = (z.tiles * TILE) * kept / totals[None, :]
    return with_layout_constraint(lax.dynamic_slice_in_dim(scaled, l * width, width, 1), straight)


def shards(markov, pattern, keep):
    z = Sizes(*markov.shape, pattern.shape[0])
    out, over = sparse(z, markov, pattern, keep)
    _, out = lax.while_loop(
        lambda state: state[0][0, 0] > 0,
        lambda state: (jnp.zeros_like(state[0]), dense(z, markov, pattern, keep)),
        (over, out),
    )
    return out


def solution(mesh):
    in_specs = (P("row", "col"), P(), P())
    out_specs = P("row", ("col", "layer"))
    return jax.shard_map(shards, mesh=mesh, in_specs=in_specs, out_specs=out_specs, check_vma=False)
```
